256 devices in a mesh: gx: 32 (over z, x), gy: 8 (over y, core).
Axes of the slice: x: 4, y: 4, z: 8, core: 2. Of those that a mesh axis runs over, the one named last changes fastest.
Arguments:
- pressure: float32 [10, 256, 1024], P(None, 'gx', 'gy'), may hold values from -3 to 1
- saturation_old: float32 [10, 256, 1024], P(None, 'gx', 'gy'), may hold values from 0.3 to 1
- soil_type: int32 [10, 256, 1024], P(None, 'gx', 'gy'), may hold values from 0 to 23
- recharge: float32 [256, 1024], P('gx', 'gy'), may hold values from -6 to 6
- ksat_table: float32 [24], replicated, may hold values from 0.05 to 5
- alpha_table: float32 [24], replicated, may hold values from 0.3 to 3
- porosity_table: float32 [24], replicated, may hold values from 0.1 to 0.5
- residual_table: float32 [24], replicated, may hold values from 0.02 to 0.3
Outputs:
- pressure_new: float32 [10, 256, 1024], P(None, 'gx', 'gy')
The draws below stay inside these ranges and needn't reach their ends.
All inputs are finite; a program needn't handle non-finite values.
Results may differ from the reference program's by a relative error of at most 0.0003.
Values sent between devices are 32-bit elements; how exact they have to be, the bound alone decides.
No kernel may reach another device: no remote copies, remote signals or barrier semaphores. Data moves between devices by JAX's collectives and lax.ppermute only.
A program may use at most 64 MiB of HBM per device.

```python
import math
import jax
import jax.numpy as jnp
from jax import lax

NZ = 10
CX = 8
CY = 128
NTYPES = 24
NEWTON = 2
KRYLOV = 2
SWEEPS = 2
COARSE_SWEEPS = 4
NX = 256
NY = 1024


def draw_recharge(key, part):
    key = jax.random.fold_in(key, 11)
    level_key, rough_key = jax.random.split(key, 2)
    block_rows = NX // CX
    block_cols = NY // CY
    levels = jnp.exp(jax.random.uniform(level_key, (block_rows, block_cols), jnp.float32, -1.2, 0.6))
    rough_part = jax.random.normal(rough_key, (NX, NY), jnp.float32)
    sign_row = jnp.where(jnp.arange(block_cols) % 2 == 0, 1.0, -1.0).astype(jnp.float32)
    levels = levels * sign_row[None, :]
    smooth_part = jnp.repeat(jnp.repeat(levels, CX, axis=0), CY, axis=1)
    return jnp.clip(smooth_part + rough_part, -6.0, 6.0).astype(jnp.float32)


def with_ends(drawn, rng, low, high):
    dims = drawn.shape
    place = [jax.random.randint(jax.random.fold_in(rng, axis), (), 0, dims[axis]) for axis in range(len(dims))]
    drawn = drawn.at[tuple(place)].set(low)
    longest = dims.index(max(dims))
    place[longest] = (place[longest] + 1) % dims[longest]
    return drawn.at[tuple(place)].set(high)


def steps_of(stream_key, dims, cuts, smallest, top_value):
    loudness, own = 1.0, jax.random.fold_in(stream_key, 6)
    for position, shards_of in cuts:
        steps = jnp.exp(jax.random.uniform(jax.random.fold_in(own, position), (shards_of,), jnp.float32, smallest / len(cuts), top_value / len(cuts)))
        loudness = loudness * jnp.repeat(steps, dims[position] // shards_of).reshape([-1 if axis == position else 1 for axis in range(len(dims))])
    return loudness


def setup_inputs(seed: int = 0) -> dict:
    keys = jax.random.split(jax.random.key(seed), 9)
    pressure = jnp.clip(-3.0 + 4.0 * jax.random.uniform(keys[0], (NZ, NX, NY), jnp.float32) ** steps_of(keys[0], (NZ, NX, NY), ((1, 32), (2, 8)), -0.2, 0.2), -3.0, 1.0)
    saturation_old = jnp.clip(0.3 + 0.7 * jax.random.uniform(keys[1], (NZ, NX, NY), jnp.float32) ** steps_of(keys[1], (NZ, NX, NY), ((1, 32), (2, 8)), -0.2, 0.2), 0.3, 1.0)
    soil_type = with_ends(jax.random.randint(keys[2], (NZ, NX, NY), 0, NTYPES), jax.random.fold_in(keys[2], 1), 0, NTYPES - 1).astype(jnp.int32)
    recharge = draw_recharge(jax.random.fold_in(keys[8], 71), 0)
    ksat_table = jnp.clip(jnp.exp(jax.random.uniform(keys[4], (NTYPES,), jnp.float32, math.log(0.05), math.log(5.0))), 0.05, 5.0)
    alpha_table = jnp.clip(jnp.exp(jax.random.uniform(keys[5], (NTYPES,), jnp.float32, math.log(0.3), math.log(3.0))), 0.3, 3.0)
    porosity_table = jnp.clip(jax.random.uniform(keys[6], (NTYPES,), jnp.float32, 0.1, 0.5), 0.1, 0.5)
    residual_table = jnp.clip(jax.random.uniform(keys[7], (NTYPES,), jnp.float32, 0.02, 0.3), 0.02, 0.3)
    return {"pressure": pressure, "saturation_old": saturation_old, "soil_type": soil_type, "recharge": recharge, "ksat_table": ksat_table, "alpha_table": alpha_table, "porosity_table": porosity_table, "residual_table": residual_table}


OMEGA = 0.8
STORAGE = 0.05
EPSILON = 1e-06

def harmonic(first, second):
    return 2.0 * first * second / (first + second)

def vertical(field):
    zeros_layer = jnp.zeros_like(field[:1])
    return (jnp.concatenate([zeros_layer, field[:-1]], 0), jnp.concatenate([field[1:], zeros_layer], 0))

def neighbours(padded):
    return (padded[:, :-2, 1:-1], padded[:, 2:, 1:-1], padded[:, 1:-1, :-2], padded[:, 1:-1, 2:])

def pad_rim(field):
    return jnp.pad(field, ((0, 0), (1, 1), (1, 1)))

def apply_level(field, padded, coefs):
    storage_term, west_face, east_face, south_face, north_face, lower_face, upper_face = coefs
    west, east, south, north = neighbours(padded)
    below, above = vertical(field)
    return storage_term * field + west_face * (field - west) + east_face * (field - east) + south_face * (field - south) + north_face * (field - north) + lower_face * (field - below) + upper_face * (field - above)

def diagonal_of(coefs):
    storage_term, west_face, east_face, south_face, north_face, lower_face, upper_face = coefs
    return storage_term + west_face + east_face + south_face + north_face + lower_face + upper_face

def blocks(field):
    depth, across, along = field.shape
    return field.reshape(depth, across // 2, 2, along // 2, 2)

def restrict(field):
    parts = blocks(field)
    return parts[:, :, 0, :, 0] + parts[:, :, 0, :, 1] + parts[:, :, 1, :, 0] + parts[:, :, 1, :, 1]

def prolong(field):
    return jnp.repeat(jnp.repeat(field, 2, axis=1), 2, axis=2)

def coarsen(coefs):
    storage_term, west_face, east_face, south_face, north_face, lower_face, upper_face = coefs
    west_parts = blocks(west_face)
    east_parts = blocks(east_face)
    south_parts = blocks(south_face)
    north_parts = blocks(north_face)
    return (restrict(storage_term), west_parts[:, :, 0, :, 0] + west_parts[:, :, 0, :, 1], east_parts[:, :, 1, :, 0] + east_parts[:, :, 1, :, 1], south_parts[:, :, 0, :, 0] + south_parts[:, :, 1, :, 0], north_parts[:, :, 0, :, 1] + north_parts[:, :, 1, :, 1], restrict(lower_face), restrict(upper_face))

def relax(rhs, coefs, diag, sweeps, rim):
    field = OMEGA * rhs / diag
    for sweep in range(sweeps - 1):
        field = field + OMEGA * (rhs - apply_level(field, rim(field), coefs)) / diag
    return field

def resume(field, rhs, coefs, diag, sweeps, rim):
    for sweep in range(sweeps):
        field = field + OMEGA * (rhs - apply_level(field, rim(field), coefs)) / diag
    return field

def vcycle(rhs_fine, level_fine, level_middle, coarse_solve):
    coefs_fine, diag_fine, rim_fine = level_fine
    coefs_middle, diag_middle, rim_middle = level_middle
    fine_iter = relax(rhs_fine, coefs_fine, diag_fine, SWEEPS, rim_fine)
    fine_resid = rhs_fine - apply_level(fine_iter, rim_fine(fine_iter), coefs_fine)
    rhs_middle = restrict(fine_resid)
    middle_iter = relax(rhs_middle, coefs_middle, diag_middle, SWEEPS, rim_middle)
    middle_resid = rhs_middle - apply_level(middle_iter, rim_middle(middle_iter), coefs_middle)
    correction = coarse_solve(restrict(middle_resid))
    middle_iter = resume(middle_iter + prolong(correction), rhs_middle, coefs_middle, diag_middle, SWEEPS, rim_middle)
    fine_iter = resume(fine_iter + prolong(middle_iter), rhs_fine, coefs_fine, diag_fine, SWEEPS, rim_fine)
    return fine_iter

def face_terms(relative, conduct, relative_pad, conduct_pad):
    rel_west, rel_east, rel_south, rel_north = neighbours(relative_pad)
    con_west, con_east, con_south, con_north = neighbours(conduct_pad)
    rel_below, rel_above = vertical(relative)
    con_below, con_above = vertical(conduct)
    return (harmonic(conduct, con_west) * (0.5 * (relative + rel_west)), harmonic(conduct, con_east) * (0.5 * (relative + rel_east)), harmonic(conduct, con_south) * (0.5 * (relative + rel_south)), harmonic(conduct, con_north) * (0.5 * (relative + rel_north)), harmonic(conduct, con_below) * (0.5 * (relative + rel_below)), harmonic(conduct, con_above) * (0.5 * (relative + rel_above)))

def flux_of(state, state_pad, faces):
    west_face, east_face, south_face, north_face, lower_face, upper_face = faces
    west, east, south, north = neighbours(state_pad)
    below, above = vertical(state)
    return west_face * (state - west) + east_face * (state - east) + south_face * (state - south) + north_face * (state - north) + lower_face * (state - below + 1.0) + upper_face * (state - above - 1.0)

def least_squares(hessen, beta, count):
    gram = [[sum((hessen[row][first] * hessen[row][second] for row in range(count + 1))) for second in range(count)] for first in range(count)]
    rhs = [beta * hessen[0][col] for col in range(count)]
    for pivot in range(count):
        for row in range(pivot + 1, count):
            factor = gram[row][pivot] / gram[pivot][pivot]
            for col in range(pivot, count):
                gram[row][col] = gram[row][col] - factor * gram[pivot][col]
            rhs[row] = rhs[row] - factor * rhs[pivot]
    weights = [0.0] * count
    for row in reversed(range(count)):
        total = rhs[row]
        for col in range(row + 1, count):
            total = total - gram[row][col] * weights[col]
        weights[row] = total / gram[row][row]
    return weights

def strip_solver(coefs_coarse, diag_coarse, width):

    def to_strips(field):
        depth, across, along = field.shape
        return field.reshape(depth, across // width, width, along).transpose(1, 0, 2, 3)
    strip_coefs = tuple((to_strips(item) for item in coefs_coarse))
    strip_diag = to_strips(diag_coarse)

    def solve(rhs_coarse):

        def single(rhs_strip, coefs_strip, diag_strip):
            level_mean = lax.optimization_barrier(jnp.sum(rhs_strip, axis=(1, 2))) / lax.optimization_barrier(jnp.sum(coefs_strip[0], axis=(1, 2)))
            start = jnp.zeros_like(rhs_strip) + level_mean[:, None, None]
            return resume(start, rhs_strip, coefs_strip, diag_strip, COARSE_SWEEPS, pad_rim)
        solved = jax.vmap(single)(to_strips(rhs_coarse), strip_coefs, strip_diag)
        return solved.transpose(1, 0, 2, 3).reshape(rhs_coarse.shape)
    return solve

def reference(pressure, saturation_old, soil_type, recharge, ksat_table, alpha_table, porosity_table, residual_table):
    conduct = ksat_table[soil_type]
    alpha = alpha_table[soil_type]
    porosity = porosity_table[soil_type]
    resid = residual_table[soil_type]
    top_layer = lax.broadcasted_iota(jnp.int32, pressure.shape, 0) == pressure.shape[0] - 1
    state = pressure
    for newton_step in range(NEWTON):
        effective = jax.nn.sigmoid(alpha * state)
        saturation = resid + (1.0 - resid) * effective
        slope = (1.0 - resid) * alpha * effective * (1.0 - effective)
        relative = effective * effective
        faces = face_terms(relative, conduct, pad_rim(relative), pad_rim(conduct))
        nonlinear = porosity * (saturation - saturation_old) + STORAGE * (state - pressure) + flux_of(state, pad_rim(state), faces)
        nonlinear = nonlinear - jnp.where(top_layer, recharge[None], 0.0)
        coefs_fine = (STORAGE + porosity * slope,) + faces
        coefs_middle = coarsen(coefs_fine)
        coefs_coarse = coarsen(coefs_middle)
        level_fine = (coefs_fine, diagonal_of(coefs_fine), pad_rim)
        level_middle = (coefs_middle, diagonal_of(coefs_middle), pad_rim)
        coarse_solve = strip_solver(coefs_coarse, diagonal_of(coefs_coarse), CX // 4)
        beta = jnp.sqrt(jnp.sum(nonlinear * nonlinear) + EPSILON)
        basis = [-nonlinear / beta]
        directions = []
        hessen = [[0.0] * KRYLOV for row in range(KRYLOV + 1)]
        for inner in range(KRYLOV):
            direction = vcycle(basis[inner], level_fine, level_middle, coarse_solve)
            directions.append(direction)
            image = apply_level(direction, pad_rim(direction), coefs_fine)
            products = [jnp.sum(vector * image) for vector in basis]
            for index in range(len(basis)):
                hessen[index][inner] = products[index]
                image = image - products[index] * basis[index]
            norm_next = jnp.sqrt(jnp.sum(image * image) + EPSILON)
            hessen[inner + 1][inner] = norm_next
            basis.append(image / norm_next)
        weights = least_squares(hessen, beta, KRYLOV)
        for inner in range(KRYLOV):
            state = state + weights[inner] * directions[inner]
    return state
```

```python
import functools

import jax
import jax.numpy as jnp
from jax import lax
from jax.experimental import pallas as pl
from jax.experimental.pallas import tpu as pltpu
from jax.sharding import PartitionSpec as P


NZ = 10
BX = 8
BY = 128
REACH = 4
ROWS = (2 * REACH + 1) * BX
SA = 24
SB = 16
LANES = 256
OWN_S = REACH * BX // 4
OMEGA = 0.8
STORAGE = 0.05
EPSILON = 1e-06
F32 = jnp.float32


def lane_roll(v, shift):
    return pltpu.roll(v, shift % v.shape[1], 1)


def row_roll(v, shift):
    return pltpu.roll(v, shift % v.shape[0], 0)


def lanes_of(rows, width=LANES):
    return lax.broadcasted_iota(jnp.int32, (rows, width), 1)


def rows_of(rows, width=LANES):
    return lax.broadcasted_iota(jnp.int32, (rows, width), 0)


def pair_sum(u, step):
    low = (lanes_of(u.shape[0]) & step) == 0
    return u + jnp.where(low, lane_roll(u, -step), lane_roll(u, step))


def from_south(u, step):
    low = (lanes_of(u.shape[0]) & step) == 0
    return jnp.where(low, u, lane_roll(u, step))


def each_layer(body):
    def step(k, carry):
        body(k)
        return carry

    lax.fori_loop(0, NZ, step, 0)


def below(k):
    return jnp.maximum(k - 1, 0)


def above(k):
    return jnp.minimum(k + 1, NZ - 1)


class Level:
    def __init__(self, storage, west, south, lower, gain, parts, step, rows):
        self.storage, self.west, self.south, self.lower, self.gain = storage, west, south, lower, gain
        self.parts, self.step, self.rows = parts, step, rows

    def west_of(self, get, j):
        return get(j - 1) if j else row_roll(get(self.parts - 1), 1)

    def total(self, k, j, get, get_low, get_up):
        s = slice(0, self.rows)
        v = get(j)
        south = self.south[k, j, s, :]
        out = south * lane_roll(v, self.step) + lane_roll(south * v, -self.step)
        out = out + self.west[k, j, s, :] * self.west_of(get, j)
        if j + 1 < self.parts:
            out = out + self.west[k, j + 1, s, :] * get(j + 1)
        else:
            out = out + row_roll(self.west[k, 0, s, :] * get(0), -1)
        return out + self.lower[k, j, s, :] * get_low(j) + self.lower[k + 1, j, s, :] * get_up(j)

    def diagonal(self, k, j):
        s = slice(0, self.rows)
        south = self.south[k, j, s, :]
        if j + 1 < self.parts:
            east = self.west[k, j + 1, s, :]
        else:
            east = row_roll(self.west[k, 0, s, :], -1)
        return (
            self.storage[k, j, s, :]
            + self.west[k, j, s, :]
            + east
            + south
            + lane_roll(south, -self.step)
            + self.lower[k, j, s, :]
            + self.lower[k + 1, j, s, :]
        )

    def sweep(self, src, dst, rhs, add=None):
        s = slice(0, self.rows)

        def body(k):
            def at(layer):
                if add is None:
                    return lambda j: src[layer, j, s, :]
                return lambda j: src[layer, j, s, :] + add(layer, j)

            get, get_low, get_up = at(k), at(below(k)), at(above(k))
            for j in range(self.parts):
                total = rhs[k, j, s, :] + self.total(k, j, get, get_low, get_up)
                dst[k, j, s, :] = (1.0 - OMEGA) * get(j) + self.gain[k, j, s, :] * total

        each_layer(body)

    def image(self, k, j, src, gravity=0.0, storage=True):
        s = slice(0, self.rows)
        kl, ku = below(k), above(k)

        def get(i):
            return src[k, i, s, :]

        v = get(j)
        south = self.south[k, j, s, :] * (v - lane_roll(v, self.step))
        out = south - lane_roll(south, -self.step)
        out = out + self.west[k, j, s, :] * (v - self.west_of(get, j))
        if j + 1 < self.parts:
            out = out + self.west[k, j + 1, s, :] * (v - get(j + 1))
        else:
            first = get(0)
            out = out - row_roll(self.west[k, 0, s, :] * (first - row_roll(v, 1)), -1)
        out = out + self.lower[k, j, s, :] * (v - src[kl, j, s, :] + gravity)
        out = out + self.lower[k + 1, j, s, :] * (v - src[ku, j, s, :] - gravity)
        if storage:
            out = out + self.storage[k, j, s, :] * v
        return out


def restrict_to(fine, src, rhs, coarse, rhs_coarse, first):
    def body(k):
        for j in range(coarse.parts):
            parts = [rhs[k, i, : fine.rows, :] - fine.image(k, i, src) for i in (2 * j, 2 * j + 1)]
            value = pair_sum(parts[0] + parts[1], fine.step)
            rhs_coarse[k, j, : fine.rows, :] = value
            first[k, j, : fine.rows, :] = coarse.gain[k, j, : fine.rows, :] * value

    each_layer(body)


def own_lanes(rows):
    lane = lanes_of(rows)
    return jnp.logical_and(lane >= BY // 2, lane < BY // 2 + BY)


def restrict_last(middle, src, rhs, rhs_last, extra):
    def body(k, sums):
        parts = [rhs[k, i, : middle.rows, :] - middle.image(k, i, src) for i in (0, 1)]
        value = pair_sum(parts[0] + parts[1], 2)[:SB]
        rhs_last[k] = value
        lane = lanes_of(SB, 128)
        total = jnp.sum(jnp.where(own_lanes(SB), value, 0.0), axis=1, keepdims=True)
        sums = jnp.where(lane == k, 0.25 * total, sums)
        if extra is not None:
            total = jnp.sum(jnp.where(own_lanes(SB), extra[k, :SB, :], 0.0), axis=1, keepdims=True)
            sums = jnp.where(lane == k + 16, 0.25 * total, sums)
        return sums

    return lax.fori_loop(0, NZ, body, jnp.zeros((SB, 128), F32))


def strip_pair(u):
    odd = (rows_of(u.shape[0], u.shape[1]) & 1) == 1
    return jnp.where(odd, row_roll(u, 1), row_roll(u, -1))


def coarsest(rhs, middle, south, lower, gain, sums, weight, one, two):
    num = sums + strip_pair(sums)
    den = weight + strip_pair(weight)
    mean = num / lane_roll(den, -16)

    def begin(k):
        lane = lanes_of(SB, 128)
        value = jnp.sum(jnp.where(lane == k, mean, 0.0), axis=1, keepdims=True)
        one[k] = jnp.broadcast_to(value, (SB, LANES))

    each_layer(begin)
    for src, dst in ((one, two), (two, one), (one, two), (two, one)):

        def body(k, src=src, dst=dst):
            v = src[k]
            s = south[k]
            total = rhs[k] + s * lane_roll(v, 4) + lane_roll(s * v, -4)
            total = total + middle[k] * strip_pair(v)
            total = total + lower[k] * src[below(k)] + lower[k + 1] * src[above(k)]
            dst[k] = (1.0 - OMEGA) * v + gain[k] * total

        each_layer(body)
    return one


def weights_of(sums):
    a, b, c, d, e, f = [sums[0:1, i : i + 1] for i in range(6)]
    beta2 = a + EPSILON
    beta = jnp.sqrt(beta2)
    kappa = (b + EPSILON) / beta2
    shift = EPSILON * (a - b) / beta2
    norm = kappa * shift - kappa * b + c
    h00 = (a - b) / beta2
    h10 = jnp.sqrt(jnp.maximum(norm, 0.0) / beta2 + EPSILON)
    scale = beta * h10
    scale2 = scale * scale
    h01 = (shift - kappa * b + d) / (beta * scale)
    h11 = (norm + kappa * (d + c - kappa * b) - e) / scale2
    p = kappa * (1.0 - h11) - h01 * h10
    q = h11 - 1.0 - kappa
    last = p * p * a + q * q * c + f + 2.0 * (p * q * b + p * d + q * e)
    h21_2 = jnp.maximum(last, 0.0) / scale2 + EPSILON
    g00 = h00 * h00 + h10 * h10
    g01 = h00 * h01 + h10 * h11
    g11 = h01 * h01 + h11 * h11 + h21_2
    r0 = beta * h00
    r1 = beta * h01
    factor = g01 / g00
    y1 = (r1 - factor * r0) / (g11 - factor * g01)
    y0 = (r0 - g01 * y1) / g00
    return y0 / beta + y1 * kappa / scale, -y1 / scale


def spread(field, left, right, first):
    lane = lanes_of(ROWS, 128)
    mid = lane_roll(field, 64)
    if not first:
        left, right = lane_roll(left, 64), lane_roll(right, 64)
    return jnp.where(lane < 64, left, mid), jnp.where(lane < 64, mid, right)


def put(ext, f, tiles):
    for half in (0, 1):
        ext[f, half, 0:ROWS, :] = tiles[half]
        ext[f, half, ROWS:, :] = tiles[half][0 : 4 * SA - ROWS]


def fetch(ext, f, j):
    return [ext[f, half, pl.ds(j, SA, stride=4), :] for half in (0, 1)]


def wide(tiles):
    return jnp.concatenate(tiles, axis=1)


def setup_kernel(second, *refs):
    refs = list(refs)
    tables, cells, left, right = refs[:4]
    refs = refs[4:]
    if second:
        moves, moves_left, moves_right, products = refs[:4]
        refs = refs[4:]
    (c0, w0, s0, l0, g0, b0, x0, c1, w1, s1, l1, g1, b1, x1, m2, s2, l2, g2, b2, sums) = refs[:20]
    ext, state, rel, con, x0a, x1a, c2, w2 = refs[20:28]
    gx, gy = lax.axis_index("gx"), lax.axis_index("gy")

    def unpack(f):
        put(ext, f, spread(cells[f], left[f], right[f], True))
        put(ext, f + 16, spread(cells[f + 16], left[f], right[f], False))

    lax.fori_loop(0, 16, lambda f, carry: (unpack(f), carry)[1], 0)
    if second:
        one, two = weights_of(products)

        def update(f):
            first = spread(moves[f], moves_left[f], moves_right[f], True)
            other = spread(moves[f + NZ], moves_left[f], moves_right[f], False)
            put(ext, f + 32, [one * first[half] + two * other[half] for half in (0, 1)])

        each_layer(update)

    table = [jnp.concatenate([tables[i]] * (SA // 8), axis=0) for i in range(4)]

    def cells_of(k):
        top = jnp.where(k == NZ - 1, 1.0, 0.0).astype(F32)
        for j in range(4):
            kind = [t.astype(jnp.int32) for t in fetch(ext, 20 + k, j)]
            ksat, alpha, porosity, resid = [
                wide([jnp.take_along_axis(table[i], t, axis=1) for t in kind]) for i in range(4)
            ]
            head = wide(fetch(ext, k, j))
            old = wide(fetch(ext, NZ + k, j))
            local = -top * wide(fetch(ext, 30, j))
            if second:
                moved = wide(fetch(ext, 32 + k, j))
                head = head + moved
                local = local + STORAGE * moved
            effective = 1.0 / (1.0 + jnp.exp(-(alpha * head)))
            local = local + porosity * (resid + (1.0 - resid) * effective - old)
            slope = (1.0 - resid) * alpha * effective * (1.0 - effective)
            state[k, j] = head
            con[k, j] = ksat
            rel[k, j] = effective * effective
            c0[k, j] = STORAGE + porosity * slope
            b0[k, j] = local

    each_layer(cells_of)

    row = gx * BX - REACH * BX + 4 * rows_of(SA)
    col = gy * BY - BY // 2 + lanes_of(SA)
    edge_col = jnp.logical_or(col == 0, col == BY * lax.axis_size("gy"))
    edge_row = jnp.logical_or(row == 0, row == BX * lax.axis_size("gx"))

    def faces(k):
        inside = jnp.where(k == 0, 0.0, 1.0).astype(F32)
        kl = below(k)
        for j in range(4):
            here, wet = con[k, j], rel[k, j]

            def face(there, wet_there):
                return here * there / (here + there) * (wet + wet_there)

            if j:
                w0[k, j] = face(con[k, j - 1], rel[k, j - 1])
            else:
                w0[k, j] = jnp.where(edge_row, 0.0, face(row_roll(con[k, 3], 1), row_roll(rel[k, 3], 1)))
            s0[k, j] = jnp.where(edge_col, 0.0, face(lane_roll(here, 1), lane_roll(wet, 1)))
            l0[k, j] = inside * face(con[kl, j], rel[kl, j])

    each_layer(faces)
    l0[NZ] = jnp.zeros((4, SA, LANES), F32)
    l1[NZ] = jnp.zeros((2, SA, LANES), F32)
    l2[NZ] = jnp.zeros((SB, LANES), F32)
    fine = Level(c0, w0, s0, l0, g0, 4, 1, SA)
    mid = Level(c1, w1, s1, l1, g1, 2, 2, SA)

    def residual(k):
        for j in range(4):
            gain = OMEGA / fine.diagonal(k, j)
            value = -(b0[k, j] + fine.image(k, j, state, 1.0, False))
            g0[k, j] = gain
            b0[k, j] = value
            x0a[k, j] = gain * value
        for j in range(2):
            c1[k, j] = pair_sum(c0[k, 2 * j] + c0[k, 2 * j + 1], 1)
            l1[k, j] = pair_sum(l0[k, 2 * j] + l0[k, 2 * j + 1], 1)
            w1[k, j] = pair_sum(w0[k, 2 * j], 1)
            s1[k, j] = from_south(s0[k, 2 * j] + s0[k, 2 * j + 1], 1)

    each_layer(residual)

    def coarse(k):
        for j in range(2):
            g1[k, j] = OMEGA / mid.diagonal(k, j)
        c2[k] = pair_sum(c1[k, 0, :SB] + c1[k, 1, :SB], 2)
        l2[k] = pair_sum(l1[k, 0, :SB] + l1[k, 1, :SB], 2)
        w2[k] = pair_sum(w1[k, 0], 2)
        s2[k] = from_south(s1[k, 0, :SB] + s1[k, 1, :SB], 2)

    each_layer(coarse)

    def coarse_gain(k):
        west = w2[k]
        east = row_roll(west, -1)[:SB]
        west = west[:SB]
        south = s2[k]
        diag = c2[k] + west + east + south + lane_roll(south, -4) + l2[k] + l2[k + 1]
        g2[k] = OMEGA / diag
        odd = (rows_of(SB) & 1) == 1
        m2[k] = jnp.where(odd, west, east)

    each_layer(coarse_gain)
    fine.sweep(x0a, x0, b0)
    restrict_to(fine, x0, b0, mid, b1, x1a)
    mid.sweep(x1a, x1, b1)
    sums[...] = restrict_last(mid, x1, b1, b2, c2)


def finish(fine, mid, last, b0, x0, b1, x1, b2, sums, weight, work0, work1, work2):
    m2, s2, l2, g2 = last
    e2 = coarsest(b2, m2, s2, l2, g2, sums, weight, *work2)
    mid.sweep(x1, work1[0], b1, lambda k, j: e2[k])
    mid.sweep(work1[0], work1[1], b1)
    corrected = work1[1]
    fine.sweep(x0, work0[0], b0, lambda k, j: corrected[k, j // 2, : fine.rows, :])
    fine.sweep(work0[0], work0[1], b0)
    return work0[1]


def write_own(dst, k, j, value):
    own = value[OWN_S : OWN_S + 8]
    lane = lanes_of(8, 128)
    own = jnp.where(lane < 64, lane_roll(own[:, :128], 64), lane_roll(own[:, 128:], 64))
    for half in (0, 1):
        dst[k, 4 * half + j : 4 * half + j + 1, :] = own[half : half + 1]


def cycle_kernel(
    total, weight, c0, w0, s0, l0, g0, b0, x0, c1, w1, s1, l1, g1, b1, x1, m2, s2, l2, g2, b2,
    r0, y0, r1, y1, r2, sums, move,
    f0, f1, h0, h1, e0, e1,
):
    fine = Level(c0, w0, s0, l0, g0, 4, 1, SB)
    mid = Level(c1, w1, s1, l1, g1, 2, 2, SB)
    z = finish(
        fine, mid, (m2, s2, l2, g2), b0, x0, b1, x1, b2, total[...], weight[...], (f0, f1), (h0, h1), (e0, e1)
    )

    def residual(k):
        for j in range(4):
            value = b0[k, j] - fine.image(k, j, z)
            r0[k, j] = value
            f0[k, j] = g0[k, j] * value
            write_own(move, k, j, z[k, j])

    each_layer(residual)
    fine.sweep(f0, y0, r0)
    restrict_to(fine, y0, r0, mid, r1, h0)
    mid.sweep(h0, y1, r1)
    sums[...] = restrict_last(mid, y1, r1, r2, None)


def last_kernel(
    total, weight, c0, w0, s0, l0, g0, start, c1, w1, s1, l1, g1, m2, s2, l2, g2, b0, x0, b1, x1, b2,
    products, move,
    f0, f1, h0, h1, e0, e1,
):
    fine = Level(c0, w0, s0, l0, g0, 4, 1, SB)
    mid = Level(c1, w1, s1, l1, g1, 2, 2, SB)
    z = finish(
        fine, mid, (m2, s2, l2, g2), b0, x0, b1, x1, b2, total[...], weight[...], (f0, f1), (h0, h1), (e0, e1)
    )
    row = rows_of(8)
    own = jnp.logical_and(own_lanes(8), row < 2)

    def body(k, sums):
        sums = list(sums)
        for j in range(4):
            write_own(move, k, j, z[k, j])
            image = fine.image(k, j, z)[OWN_S : OWN_S + 8]
            u = jnp.where(own, start[k, j, OWN_S : OWN_S + 8, :], 0.0)
            t = jnp.where(own, b0[k, j, OWN_S : OWN_S + 8, :], 0.0)
            r = jnp.where(own, t - image, 0.0)
            for i, item in enumerate((u * u, u * t, t * t, u * r, t * r, r * r)):
                sums[i] = sums[i] + item
        return tuple(sums)

    zero = jnp.zeros((8, LANES), F32)
    sums = lax.fori_loop(0, NZ, body, (zero,) * 6)
    lane = lanes_of(8, 128)
    out = jnp.zeros((8, 128), F32)
    for i, item in enumerate(sums):
        value = jnp.sum(jnp.sum(item, axis=0, keepdims=True), axis=1, keepdims=True)
        out = jnp.where(lane == i, value, out)
    products[...] = out


def end_kernel(head, one, two, out):
    state = head[...]
    for products, move in (one, two):
        first, second = weights_of(products)
        state = state + first[None] * move[0:NZ] + second[None] * move[NZ:]
    out[...] = state


def end_entry(head, products_a, move_a, products_b, move_b, out):
    end_kernel(head, (products_a, move_a), (products_b, move_b), out)


VMEM = pl.BlockSpec(memory_space=pltpu.VMEM)


def shape(*dims):
    return jax.ShapeDtypeStruct(dims, F32)


def buffer(*dims):
    return pltpu.VMEM(dims, F32)


def call(kernel, args, outs, scratch, limit):
    return pl.pallas_call(
        kernel,
        out_shape=outs,
        in_specs=[VMEM] * len(args),
        out_specs=jax.tree.map(lambda _: VMEM, outs),
        scratch_shapes=scratch,
        compiler_params=pltpu.CompilerParams(vmem_limit_bytes=limit),
    )(*args)


def setup(tables, cells, extra):
    outs = (
        [shape(NZ, 4, SA, LANES)] * 3 + [shape(NZ + 1, 4, SA, LANES)] + [shape(NZ, 4, SA, LANES)] * 3
        + [shape(NZ, 2, SA, LANES)] * 3 + [shape(NZ + 1, 2, SA, LANES)] + [shape(NZ, 2, SA, LANES)] * 3
        + [shape(NZ, SB, LANES)] * 2 + [shape(NZ + 1, SB, LANES)] + [shape(NZ, SB, LANES)] * 2
        + [shape(SB, 128)]
    )
    fields = 42 if extra else 32
    scratch = (
        [buffer(fields, 2, 4 * SA, 128)] + [buffer(NZ, 4, SA, LANES)] * 4
        + [buffer(NZ, 2, SA, LANES), buffer(NZ, SB, LANES), buffer(NZ, SA, LANES)]
    )
    return call(functools.partial(setup_kernel, bool(extra)), [tables, *cells, *extra], outs, scratch, 44 << 20)


def work():
    return [buffer(NZ, 4, SB, LANES)] * 2 + [buffer(NZ, 2, SB, LANES)] * 2 + [buffer(NZ, SB, LANES)] * 2


def shifted(field, axis, by):
    count = lax.axis_size(axis)
    return lax.ppermute(field, axis, [(i, (i + by) % count) for i in range(count)])


def surroundings(field):
    near = jnp.concatenate([shifted(field, "gx", 1), field, shifted(field, "gx", -1)], axis=1)
    rows = jnp.concatenate([shifted(near, "gx", 3), near, shifted(near, "gx", -3)], axis=1)
    half = rows.shape[0] // 2
    low, high = rows[:half], rows[half:]
    left = shifted(jnp.concatenate([low[..., 64:], high[..., 64:]], axis=2), "gy", 1)
    right = shifted(jnp.concatenate([high[..., :64], low[..., :64]], axis=2), "gy", -1)
    return rows, left, right


def summed(field, axis):
    count = lax.axis_size(axis)
    reach = 1
    while reach < count:
        field = field + lax.ppermute(field, axis, [(i, i ^ reach) for i in range(count)])
        reach *= 2
    return field


def on_device(
    pressure, saturation_old, soil_type, recharge, ksat_table, alpha_table, porosity_table, residual_table
):
    tables = jnp.stack([ksat_table, alpha_table, porosity_table, residual_table])
    tables = jnp.pad(tables, ((0, 0), (0, 128 - tables.shape[1])))
    tables = jnp.broadcast_to(tables[:, None, :], (4, 8, 128))
    fields = jnp.concatenate(
        [pressure, saturation_old, soil_type.astype(F32), recharge[None], jnp.zeros_like(recharge)[None]], axis=0
    )
    cells = surroundings(fields)
    ends = []
    for newton in range(2):
        extra = []
        if newton:
            products, moves = ends[0]
            extra = [*surroundings(moves), products]
        got = setup(tables, cells, extra)
        (c0, w0, s0, l0, g0, b0, x0, c1, w1, s1, l1, g1, b1, x1, m2, s2, l2, g2, b2, sums) = got
        weight = summed(sums, "gy")
        parts = [a[..., :SB, :] for a in (c0, w0, s0, l0, g0, b0, x0, c1, w1, s1, l1, g1, b1, x1)]
        c0, w0, s0, l0, g0, b0, x0, c1, w1, s1, l1, g1, b1, x1 = parts
        last = [m2, s2, l2, g2]
        r0, y0, r1, y1, r2, sums, move = call(
            cycle_kernel,
            [weight, weight, *parts, *last, b2],
            [shape(NZ, 4, SB, LANES)] * 2 + [shape(NZ, 2, SB, LANES)] * 2
            + [shape(NZ, SB, LANES), shape(SB, 128), shape(NZ, BX, BY)],
            work(),
            44 << 20,
        )
        total = summed(sums, "gy")
        products, move_b = call(
            last_kernel,
            [total, weight, c0, w0, s0, l0, g0, b0, c1, w1, s1, l1, g1, *last, r0, y0, r1, y1, r2],
            [shape(8, 128), shape(NZ, BX, BY)],
            work(),
            44 << 20,
        )
        products = summed(summed(products, "gy"), "gx")
        ends.append((products, jnp.concatenate([move, move_b], axis=0)))
    (products_a, move_a), (products_b, move_b) = ends
    return call(
        end_entry, [pressure, products_a, move_a, products_b, move_b], shape(NZ, BX, BY), [], 16 << 20
    )


def solution(mesh):
    placed = (P(None, "gx", "gy"),) * 3 + (P("gx", "gy"),) + (P(),) * 4
    return jax.shard_map(
        on_device, mesh=mesh, in_specs=placed, out_specs=P(None, "gx", "gy"), check_vma=False
    )
```

```python
import functools

import jax
import jax.numpy as jnp
from jax import lax
from jax.experimental import pallas as pl
from jax.experimental.pallas import tpu as pltpu
from jax.sharding import PartitionSpec as P


NZ = 10
BX = 8
BY = 128
REACH = 4
ROWS = (2 * REACH + 1) * BX
SA = 24
SB = 16
LANES = 256
OWN_S = REACH * BX // 4
OMEGA = 0.8
STORAGE = 0.05
EPSILON = 1e-06
F32 = jnp.float32


def lane_roll(v, shift):
    return pltpu.roll(v, shift % v.shape[1], 1)


def row_roll(v, shift):
    return pltpu.roll(v, shift % v.shape[0], 0)


def lanes_of(rows, width=LANES):
    return lax.broadcasted_iota(jnp.int32, (rows, width), 1)


def rows_of(rows, width=LANES):
    return lax.broadcasted_iota(jnp.int32, (rows, width), 0)


def pair_sum(u, step):
    low = (lanes_of(u.shape[0]) & step) == 0
    return u + jnp.where(low, lane_roll(u, -step), lane_roll(u, step))


def from_south(u, step):
    low = (lanes_of(u.shape[0]) & step) == 0
    return jnp.where(low, u, lane_roll(u, step))


def each_layer(body, together, count=NZ):
    if together == count:
        for k in range(count):
            body(k)
        return

    def step(i, carry):
        for j in range(together):
            body(together * i + j)
        return carry

    lax.fori_loop(0, count // together, step, 0)


def below(k):
    return max(k - 1, 0) if isinstance(k, int) else jnp.maximum(k - 1, 0)


def above(k):
    return min(k + 1, NZ - 1) if isinstance(k, int) else jnp.minimum(k + 1, NZ - 1)


def one_if(condition):
    return jnp.where(condition, 1.0, 0.0).astype(F32)


class Level:
    def __init__(self, storage, west, south, lower, gain, parts, step, rows):
        self.storage, self.west, self.south, self.lower, self.gain = storage, west, south, lower, gain
        self.parts, self.step, self.rows = parts, step, rows

    def west_of(self, get, j):
        return get(j - 1) if j else row_roll(get(self.parts - 1), 1)

    def total(self, k, j, get, get_low, get_up):
        s = slice(0, self.rows)
        v = get(j)
        south = self.south[k, j, s, :]
        out = south * lane_roll(v, self.step) + lane_roll(south * v, -self.step)
        out = out + self.west[k, j, s, :] * self.west_of(get, j)
        if j + 1 < self.parts:
            out = out + self.west[k, j + 1, s, :] * get(j + 1)
        else:
            out = out + row_roll(self.west[k, 0, s, :] * get(0), -1)
        return out + self.lower[k, j, s, :] * get_low(j) + self.lower[k + 1, j, s, :] * get_up(j)

    def diagonal(self, k, j):
        s = slice(0, self.rows)
        south = self.south[k, j, s, :]
        if j + 1 < self.parts:
            east = self.west[k, j + 1, s, :]
        else:
            east = row_roll(self.west[k, 0, s, :], -1)
        return (
            self.storage[k, j, s, :]
            + self.west[k, j, s, :]
            + east
            + south
            + lane_roll(south, -self.step)
            + self.lower[k, j, s, :]
            + self.lower[k + 1, j, s, :]
        )

    def sweep(self, src, dst, rhs, add, together):
        s = slice(0, self.rows)

        def body(k):
            def at(layer):
                if add is None:
                    return lambda j: src[layer, j, s, :]
                return lambda j: src[layer, j, s, :] + add(layer, j)

            get, get_low, get_up = at(k), at(below(k)), at(above(k))
            for j in range(self.parts):
                total = rhs[k, j, s, :] + self.total(k, j, get, get_low, get_up)
                dst[k, j, s, :] = (1.0 - OMEGA) * get(j) + self.gain[k, j, s, :] * total

        each_layer(body, together)

    def image(self, k, j, src, gravity=0.0, storage=True):
        s = slice(0, self.rows)
        kl, ku = below(k), above(k)

        def get(i):
            return src[k, i, s, :]

        v = get(j)
        south = self.south[k, j, s, :] * (v - lane_roll(v, self.step))
        out = south - lane_roll(south, -self.step)
        out = out + self.west[k, j, s, :] * (v - self.west_of(get, j))
        if j + 1 < self.parts:
            out = out + self.west[k, j + 1, s, :] * (v - get(j + 1))
        else:
            first = get(0)
            out = out - row_roll(self.west[k, 0, s, :] * (first - row_roll(v, 1)), -1)
        out = out + self.lower[k, j, s, :] * (v - src[kl, j, s, :] + gravity)
        out = out + self.lower[k + 1, j, s, :] * (v - src[ku, j, s, :] - gravity)
        if storage:
            out = out + self.storage[k, j, s, :] * v
        return out


def restrict_to(fine, src, rhs, coarse, rhs_coarse, first, together):
    def body(k):
        for j in range(coarse.parts):
            parts = [rhs[k, i, : fine.rows, :] - fine.image(k, i, src) for i in (2 * j, 2 * j + 1)]
            value = pair_sum(parts[0] + parts[1], fine.step)
            rhs_coarse[k, j, : fine.rows, :] = value
            first[k, j, : fine.rows, :] = coarse.gain[k, j, : fine.rows, :] * value

    each_layer(body, together)


def own_lanes(rows):
    lane = lanes_of(rows)
    return jnp.logical_and(lane >= BY // 2, lane < BY // 2 + BY)


def strip_sums(fields):
    lane = lanes_of(SB, 128)
    out = jnp.zeros((SB, 128), F32)
    for i, field in enumerate(fields):
        for k in range(NZ):
            value = field[k, :SB, :]
            value = jnp.where(lane < 64, value[:, 128:], value[:, :128])
            out = jnp.where(lane == 16 * i + k, 0.25 * jnp.sum(value, axis=1, keepdims=True), out)
    return out


def restrict_last(middle, src, rhs, rhs_last, together):
    def body(k):
        parts = [rhs[k, i, : middle.rows, :] - middle.image(k, i, src) for i in (0, 1)]
        rhs_last[k] = pair_sum(parts[0] + parts[1], 2)[:SB]

    each_layer(body, together)


def strip_pair(u):
    odd = (rows_of(u.shape[0], u.shape[1]) & 1) == 1
    return jnp.where(odd, row_roll(u, 1), row_roll(u, -1))


def coarsest(rhs, middle, south, lower, gain, sums, weight, out):
    num = sums + strip_pair(sums)
    den = weight + strip_pair(weight)
    mean = num / lane_roll(den, -16)

    lane = lanes_of(SB, 128)
    now = []
    for k in range(NZ):
        value = jnp.sum(jnp.where(lane == k, mean, 0.0), axis=1, keepdims=True)
        now.append(jnp.broadcast_to(value, (SB, LANES)))
    for _ in range(4):
        new = []
        for k in range(NZ):
            v, s = now[k], south[k]
            total = rhs[k] + s * lane_roll(v, 4) + lane_roll(s * v, -4) + middle[k] * strip_pair(v)
            total = total + lower[k] * now[below(k)] + lower[k + 1] * now[above(k)]
            new.append((1.0 - OMEGA) * v + gain[k] * total)
        now = new
    for k in range(NZ):
        out[k] = now[k]


def weights_of(sums):
    a, b, c, d, e, f = [sums[0:1, i : i + 1] for i in range(6)]
    beta2 = a + EPSILON
    beta = jnp.sqrt(beta2)
    kappa = (b + EPSILON) / beta2
    shift = EPSILON * (a - b) / beta2
    norm = kappa * shift - kappa * b + c
    h00 = (a - b) / beta2
    h10 = jnp.sqrt(jnp.maximum(norm, 0.0) / beta2 + EPSILON)
    scale = beta * h10
    scale2 = scale * scale
    h01 = (shift - kappa * b + d) / (beta * scale)
    h11 = (norm + kappa * (d + c - kappa * b) - e) / scale2
    p = kappa * (1.0 - h11) - h01 * h10
    q = h11 - 1.0 - kappa
    last = p * p * a + q * q * c + f + 2.0 * (p * q * b + p * d + q * e)
    h21_2 = jnp.maximum(last, 0.0) / scale2 + EPSILON
    g00 = h00 * h00 + h10 * h10
    g01 = h00 * h01 + h10 * h11
    g11 = h01 * h01 + h11 * h11 + h21_2
    r0 = beta * h00
    r1 = beta * h01
    factor = g01 / g00
    y1 = (r1 - factor * r0) / (g11 - factor * g01)
    y0 = (r0 - g01 * y1) / g00
    return y0 / beta + y1 * kappa / scale, -y1 / scale


def spread(field, left, right, first):
    lane = lanes_of(ROWS, 128)
    mid = lane_roll(field, 64)
    if not first:
        left, right = lane_roll(left, 64), lane_roll(right, 64)
    return jnp.where(lane < 64, left, mid), jnp.where(lane < 64, mid, right)


def put(ext, f, tiles):
    for half in (0, 1):
        ext[f, half, 0:ROWS, :] = tiles[half]
        ext[f, half, ROWS:, :] = tiles[half][0 : 4 * SA - ROWS]


def fetch(ext, f, j):
    return [ext[f, half, pl.ds(j, SA, stride=4), :] for half in (0, 1)]


def wide(tiles):
    return jnp.concatenate(tiles, axis=1)


def setup_kernel(second, *refs):
    refs = list(refs)
    if second:
        cells, left, right = refs[:3]
        stored, refs = refs[3:10], refs[10:]
    else:
        tables, cells, left, right = refs[:4]
        stored, refs = refs[24:31], refs[4:24] + refs[31:]
    statics, sem = refs[27:34], refs[34]
    if second:
        copies = [pltpu.make_async_copy(stored[i], statics[i], sem.at[i]) for i in range(7)]
        for copy in copies:
            copy.start()
    else:
        copies = [pltpu.make_async_copy(statics[i], stored[i], sem.at[i]) for i in range(7)]
    head, alpha, porous, base, hw, hs, hl = statics
    (c0, w0, s0, l0, g0, b0, x0, c1, w1, s1, l1, g1, b1, x1, m2, s2, l2, g2, b2, sums) = refs[:20]
    ext, state, rel, x0a, x1a, c2, w2 = refs[20:27]
    if second:

        def unpack(f):
            put(ext, f, spread(cells[f], left[f], right[f], True))
            put(ext, f + 5, spread(cells[f + 5], left[f], right[f], False))

        each_layer(lambda f: unpack(f), 5, 5)
        for copy in copies[:4]:
            copy.wait()
    else:
        con = refs[35]

        def unpack(f):
            put(ext, f, spread(cells[f], left[f], right[f], True))
            put(ext, f + 16, spread(cells[f + 16], left[f], right[f], False))

        lax.fori_loop(0, 8, lambda f, carry: (unpack(2 * f), unpack(2 * f + 1), carry)[2], 0)
        table = [jnp.concatenate([tables[i]] * (SA // 8), axis=0) for i in range(4)]

        def look_up(k):
            top = one_if(k == NZ - 1)
            for j in range(4):
                kind = [t.astype(jnp.int32) for t in fetch(ext, 20 + k, j)]
                con[k, j], here, porosity, resid = [
                    wide([jnp.take_along_axis(table[i], t, axis=1) for t in kind]) for i in range(4)
                ]
                alpha[k, j] = here
                porous[k, j] = porosity * (1.0 - resid)
                base[k, j] = porosity * (resid - wide(fetch(ext, NZ + k, j))) - top * wide(fetch(ext, 30, j))
                head[k, j] = wide(fetch(ext, k, j))

        each_layer(look_up, 5)
        row = lax.axis_index("gx") * BX - REACH * BX + 4 * rows_of(SA)
        col = lax.axis_index("gy") * BY - BY // 2 + lanes_of(SA)
        edge_col = jnp.logical_or(col == 0, col == BY * lax.axis_size("gy"))
        edge_row = jnp.logical_or(row == 0, row == BX * lax.axis_size("gx"))

        def harmonic(k):
            inside = one_if(k != 0)
            for j in range(4):
                here = con[k, j]

                def face(there):
                    return here * there / (here + there)

                west = face(con[k, j - 1]) if j else jnp.where(edge_row, 0.0, face(row_roll(con[k, 3], 1)))
                hw[k, j] = west
                hs[k, j] = jnp.where(edge_col, 0.0, face(lane_roll(here, 1)))
                hl[k, j] = inside * face(con[below(k), j])

        each_layer(harmonic, 5)
        for copy in copies:
            copy.start()

    def cells_of(k):
        for j in range(4):
            here = head[k, j]
            local = base[k, j]
            if second:
                moved = wide(fetch(ext, k, j))
                here = here + moved
                local = local + STORAGE * moved
            effective = 1.0 / (1.0 + jnp.exp(-(alpha[k, j] * here)))
            state[k, j] = here
            rel[k, j] = effective * effective
            part = porous[k, j] * effective
            c0[k, j] = STORAGE + part * (alpha[k, j] * (1.0 - effective))
            b0[k, j] = local + part

    each_layer(cells_of, 10)
    if second:
        for copy in copies[4:]:
            copy.wait()

    def faces(k):
        for j in range(4):
            wet = rel[k, j]
            w0[k, j] = hw[k, j] * (wet + (rel[k, j - 1] if j else row_roll(rel[k, 3], 1)))
            s0[k, j] = hs[k, j] * (wet + lane_roll(wet, 1))
            l0[k, j] = hl[k, j] * (wet + rel[below(k), j])

    each_layer(faces, 5)
    l0[NZ] = jnp.zeros((4, SA, LANES), F32)
    l1[NZ] = jnp.zeros((2, SA, LANES), F32)
    l2[NZ] = jnp.zeros((SB, LANES), F32)
    fine = Level(c0, w0, s0, l0, g0, 4, 1, SA)
    mid = Level(c1, w1, s1, l1, g1, 2, 2, SA)

    def residual(k):
        for j in range(4):
            gain = OMEGA / fine.diagonal(k, j)
            value = -(b0[k, j] + fine.image(k, j, state, 1.0, False))
            g0[k, j] = gain
            b0[k, j] = value
            x0a[k, j] = gain * value

    each_layer(residual, 2)

    def coarsen(k):
        for j in range(2):
            c1[k, j] = pair_sum(c0[k, 2 * j] + c0[k, 2 * j + 1], 1)
            l1[k, j] = pair_sum(l0[k, 2 * j] + l0[k, 2 * j + 1], 1)
            w1[k, j] = pair_sum(w0[k, 2 * j], 1)
            s1[k, j] = from_south(s0[k, 2 * j] + s0[k, 2 * j + 1], 1)

    each_layer(coarsen, 5)

    def coarse(k):
        for j in range(2):
            g1[k, j] = OMEGA / mid.diagonal(k, j)
        c2[k] = pair_sum(c1[k, 0, :SB] + c1[k, 1, :SB], 2)
        l2[k] = pair_sum(l1[k, 0, :SB] + l1[k, 1, :SB], 2)
        w2[k] = pair_sum(w1[k, 0], 2)
        s2[k] = from_south(s1[k, 0, :SB] + s1[k, 1, :SB], 2)

    each_layer(coarse, 5)

    def coarse_gain(k):
        west = w2[k]
        east = row_roll(west, -1)[:SB]
        west = west[:SB]
        south = s2[k]
        diag = c2[k] + west + east + south + lane_roll(south, -4) + l2[k] + l2[k + 1]
        g2[k] = OMEGA / diag
        odd = (rows_of(SB) & 1) == 1
        m2[k] = jnp.where(odd, west, east)

    each_layer(coarse_gain, 5)
    fine.sweep(x0a, x0, b0, None, 5)
    restrict_to(fine, x0, b0, mid, b1, x1a, 2)
    mid.sweep(x1a, x1, b1, None, 5)
    restrict_last(mid, x1, b1, b2, 10)
    sums[...] = strip_sums([b2, c2])
    if not second:
        for copy in copies:
            copy.wait()


def finish(fine, mid, last, b0, x0, b1, x1, b2, sums, weight, work0, work1, e2):
    m2, s2, l2, g2 = last
    coarsest(b2, m2, s2, l2, g2, sums, weight, e2)
    mid.sweep(x1, work1[0], b1, lambda k, j: e2[k], 10)
    mid.sweep(work1[0], work1[1], b1, None, 10)
    corrected = work1[1]
    fine.sweep(x0, work0[0], b0, lambda k, j: corrected[k, j // 2, : fine.rows, :], 5)
    fine.sweep(work0[0], work0[1], b0, None, 5)
    return work0[1]


def write_own(dst, k, j, value):
    own = value[OWN_S : OWN_S + 8]
    lane = lanes_of(8, 128)
    own = jnp.where(lane < 64, lane_roll(own[:, :128], 64), lane_roll(own[:, 128:], 64))
    for half in (0, 1):
        dst[k, 4 * half + j : 4 * half + j + 1, :] = own[half : half + 1]


def cycle_kernel(
    total, weight, c0, w0, s0, l0, g0, b0, x0, c1, w1, s1, l1, g1, b1, x1, m2, s2, l2, g2, b2,
    r0, y0, r1, y1, r2, sums, move,
    f0, f1, h0, h1, e2,
):
    fine = Level(c0, w0, s0, l0, g0, 4, 1, SB)
    mid = Level(c1, w1, s1, l1, g1, 2, 2, SB)
    z = finish(
        fine, mid, (m2, s2, l2, g2), b0, x0, b1, x1, b2, total[...], weight[...], (f0, f1), (h0, h1), e2
    )

    def residual(k):
        for j in range(4):
            value = b0[k, j, :SB, :] - fine.image(k, j, z)
            r0[k, j] = value
            f0[k, j] = g0[k, j, :SB, :] * value
            write_own(move, k, j, z[k, j])

    each_layer(residual, 5)
    fine.sweep(f0, y0, r0, None, 5)
    restrict_to(fine, y0, r0, mid, r1, h0, 5)
    mid.sweep(h0, y1, r1, None, 10)
    restrict_last(mid, y1, r1, r2, 10)
    sums[...] = strip_sums([r2])


def last_kernel(
    total, weight, c0, w0, s0, l0, g0, start, c1, w1, s1, l1, g1, m2, s2, l2, g2, b0, x0, b1, x1, b2,
    products, move,
    f0, f1, h0, h1, e2,
):
    fine = Level(c0, w0, s0, l0, g0, 4, 1, SB)
    mid = Level(c1, w1, s1, l1, g1, 2, 2, SB)
    z = finish(
        fine, mid, (m2, s2, l2, g2), b0, x0, b1, x1, b2, total[...], weight[...], (f0, f1), (h0, h1), e2
    )
    row = rows_of(8)
    own = jnp.logical_and(own_lanes(8), row < 2)

    def body(k, sums):
        sums = list(sums)
        for j in range(4):
            write_own(move, k, j, z[k, j])
            image = fine.image(k, j, z)[OWN_S : OWN_S + 8]
            u = jnp.where(own, start[k, j, OWN_S : OWN_S + 8, :], 0.0)
            t = jnp.where(own, b0[k, j, OWN_S : OWN_S + 8, :], 0.0)
            r = jnp.where(own, t - image, 0.0)
            for i, item in enumerate((u * u, u * t, t * t, u * r, t * r, r * r)):
                sums[i] = sums[i] + item
        return tuple(sums)

    sums = (jnp.zeros((8, LANES), F32),) * 6
    for k in range(NZ):
        sums = body(k, sums)
    lane = lanes_of(1, 128)
    out = jnp.zeros((1, 128), F32)
    for i, item in enumerate(sums):
        value = jnp.sum(jnp.sum(item, axis=0, keepdims=True), axis=1, keepdims=True)
        out = jnp.where(lane == i, value, out)
    products[...] = out


def move_kernel(products, first, second, out):
    one, two = weights_of(products)
    out[...] = one[None] * first[...] + two[None] * second[...]


def end_kernel(head, moved, products, first, second, out):
    one, two = weights_of(products)
    out[...] = head[...] + moved[...] + one[None] * first[...] + two[None] * second[...]


VMEM = pl.BlockSpec(memory_space=pltpu.VMEM)
HBM = pl.BlockSpec(memory_space=pltpu.HBM)


def shape(*dims):
    return jax.ShapeDtypeStruct(dims, F32)


def buffer(*dims):
    return pltpu.VMEM(dims, F32)


def call(kernel, args, outs, scratch, limit, in_hbm=(), out_hbm=()):
    many = isinstance(outs, list)
    spec = [HBM if i in out_hbm else VMEM for i in range(len(outs))] if many else VMEM
    return pl.pallas_call(
        kernel,
        out_shape=outs,
        in_specs=[HBM if i in in_hbm else VMEM for i in range(len(args))],
        out_specs=spec,
        scratch_shapes=scratch,
        compiler_params=pltpu.CompilerParams(vmem_limit_bytes=limit),
    )(*args)


def setup(inputs, second):
    fine = shape(NZ, 4, SA, LANES)
    outs = (
        [fine] * 3 + [shape(NZ + 1, 4, SA, LANES)] + [fine] * 3
        + [shape(NZ, 2, SA, LANES)] * 3 + [shape(NZ + 1, 2, SA, LANES)] + [shape(NZ, 2, SA, LANES)] * 3
        + [shape(NZ, SB, LANES)] * 2 + [shape(NZ + 1, SB, LANES)] + [shape(NZ, SB, LANES)] * 2
        + [shape(SB, 128)] + ([] if second else [fine] * 7)
    )
    work_fine = buffer(NZ, 4, SA, LANES)
    scratch = (
        [buffer(NZ if second else 32, 2, 4 * SA, 128)] + [work_fine] * 3
        + [buffer(NZ, 2, SA, LANES), buffer(NZ, SB, LANES), buffer(NZ, SA, LANES)]
        + [work_fine] * 7 + [pltpu.SemaphoreType.DMA((7,))] + ([] if second else [work_fine])
    )
    kernel = functools.partial(setup_kernel, second)
    if second:
        return call(kernel, inputs, outs, scratch, 15 << 20, range(3, 10))
    return call(kernel, inputs, outs, scratch, 18 << 20, (), range(20, 27))


def work():
    return [buffer(NZ, 4, SB, LANES)] * 2 + [buffer(NZ, 2, SB, LANES)] * 2 + [buffer(NZ, SB, LANES)]


def shifted(field, axis, by):
    count = lax.axis_size(axis)
    return lax.ppermute(field, axis, [(i, (i + by) % count) for i in range(count)])


def surroundings(field):
    near = jnp.concatenate([shifted(field, "gx", 1), field, shifted(field, "gx", -1)], axis=1)
    rows = jnp.concatenate([shifted(near, "gx", 3), near, shifted(near, "gx", -3)], axis=1)
    half = rows.shape[0] // 2
    low, high = rows[:half], rows[half:]
    left = shifted(jnp.concatenate([low[..., 64:], high[..., 64:]], axis=2), "gy", 1)
    right = shifted(jnp.concatenate([high[..., :64], low[..., :64]], axis=2), "gy", -1)
    return rows, left, right


def summed(field, axis):
    count = lax.axis_size(axis)
    reach = 1
    while reach < count:
        field = field + lax.ppermute(field, axis, [(i, i ^ reach) for i in range(count)])
        reach *= 2
    return field


def summed_over_all(row):
    axes = ("gx", "gy")
    count = lax.axis_size(axes)
    parts = lax.all_to_all(jnp.broadcast_to(row[None], (count, 1, 128)), axes, 0, 0, tiled=True)
    return jnp.sum(parts, axis=0)


def on_device(
    pressure, saturation_old, soil_type, recharge, ksat_table, alpha_table, porosity_table, residual_table
):
    tables = jnp.stack([ksat_table, alpha_table, porosity_table, residual_table])
    tables = jnp.pad(tables, ((0, 0), (0, 128 - tables.shape[1])))
    tables = jnp.broadcast_to(tables[:, None, :], (4, 8, 128))
    fields = jnp.concatenate(
        [pressure, saturation_old, soil_type.astype(F32), recharge[None], jnp.zeros_like(recharge)[None]], axis=0
    )
    cells = surroundings(fields)
    moved = None
    for newton in range(2):
        if newton:
            got = setup([*surroundings(moved), *statics], True)
        else:
            got = setup([tables, *cells], False)
            statics = got[20:]
        (c0, w0, s0, l0, g0, b0, x0, c1, w1, s1, l1, g1, b1, x1, m2, s2, l2, g2, b2, sums) = got[:20]
        weight = summed(sums, "gy")
        r0, y0, r1, y1, r2, sums, first = call(
            cycle_kernel,
            [weight, weight, *got[:19]],
            [shape(NZ, 4, SB, LANES)] * 2 + [shape(NZ, 2, SB, LANES)] * 2
            + [shape(NZ, SB, LANES), shape(SB, 128), shape(NZ, BX, BY)],
            work(),
            6 << 20,
        )
        total = summed(sums, "gy")
        products, second = call(
            last_kernel,
            [total, weight, c0, w0, s0, l0, g0, b0, c1, w1, s1, l1, g1, m2, s2, l2, g2, r0, y0, r1, y1, r2],
            [shape(1, 128), shape(NZ, BX, BY)],
            work(),
            6 << 20,
        )
        ends = [summed_over_all(products), first, second]
        if newton:
            return call(end_kernel, [pressure, moved, *ends], shape(NZ, BX, BY), [], 4 << 20)
        moved = call(move_kernel, ends, shape(NZ, BX, BY), [], 4 << 20)


def solution(mesh):
    placed = (P(None, "gx", "gy"),) * 3 + (P("gx", "gy"),) + (P(),) * 4
    return jax.shard_map(
        on_device, mesh=mesh, in_specs=placed, out_specs=P(None, "gx", "gy"), check_vma=False
    )
```

```python
import functools

import jax
import jax.numpy as jnp
from jax import lax
from jax.experimental import pallas as pl
from jax.experimental.pallas import tpu as pltpu
from jax.sharding import PartitionSpec as P


NZ = 10
BX = 8
BY = 128
REACH = 4
ROWS = (2 * REACH + 1) * BX
SA = 24
SB = 16
LANES = 256
OWN_S = REACH * BX // 4
OMEGA = 0.8
STORAGE = 0.05
EPSILON = 1e-06
F32 = jnp.float32


def lane_roll(v, shift):
    return pltpu.roll(v, shift % v.shape[1], 1)


def row_roll(v, shift):
    return pltpu.roll(v, shift % v.shape[0], 0)


def lanes_of(rows, width=LANES):
    return lax.broadcasted_iota(jnp.int32, (rows, width), 1)


def rows_of(rows, width=LANES):
    return lax.broadcasted_iota(jnp.int32, (rows, width), 0)


def pair_sum(u, step):
    low = (lanes_of(u.shape[0]) & step) == 0
    return u + jnp.where(low, lane_roll(u, -step), lane_roll(u, step))


def from_south(u, step):
    low = (lanes_of(u.shape[0]) & step) == 0
    return jnp.where(low, u, lane_roll(u, step))


def each_layer(body, together, count=NZ):
    if together == count:
        for k in range(count):
            body(k)
        return

    def step(i, carry):
        for j in range(together):
            body(together * i + j)
        return carry

    lax.fori_loop(0, count // together, step, 0)


def below(k):
    return max(k - 1, 0) if isinstance(k, int) else jnp.maximum(k - 1, 0)


def above(k):
    return min(k + 1, NZ - 1) if isinstance(k, int) else jnp.minimum(k + 1, NZ - 1)


def one_if(condition):
    return jnp.where(condition, 1.0, 0.0).astype(F32)


class Level:
    def __init__(self, storage, west, south, lower, gain, parts, step, rows):
        self.storage, self.west, self.south, self.lower, self.gain = storage, west, south, lower, gain
        self.parts, self.step, self.rows = parts, step, rows

    def west_of(self, get, j):
        return get(j - 1) if j else row_roll(get(self.parts - 1), 1)

    def total(self, k, j, get, get_low, get_up):
        s = slice(0, self.rows)
        v = get(j)
        south = self.south[k, j, s, :]
        out = south * lane_roll(v, self.step) + lane_roll(south * v, -self.step)
        out = out + self.west[k, j, s, :] * self.west_of(get, j)
        if j + 1 < self.parts:
            out = out + self.west[k, j + 1, s, :] * get(j + 1)
        else:
            out = out + row_roll(self.west[k, 0, s, :] * get(0), -1)
        return out + self.lower[k, j, s, :] * get_low(j) + self.lower[k + 1, j, s, :] * get_up(j)

    def diagonal(self, k, j):
        s = slice(0, self.rows)
        south = self.south[k, j, s, :]
        if j + 1 < self.parts:
            east = self.west[k, j + 1, s, :]
        else:
            east = row_roll(self.west[k, 0, s, :], -1)
        return (
            self.storage[k, j, s, :]
            + self.west[k, j, s, :]
            + east
            + south
            + lane_roll(south, -self.step)
            + self.lower[k, j, s, :]
            + self.lower[k + 1, j, s, :]
        )

    def sweep(self, src, dst, rhs, add, together):
        s = slice(0, self.rows)

        def body(k):
            def at(layer):
                if add is None:
                    return lambda j: src[layer, j, s, :]
                return lambda j: src[layer, j, s, :] + add(layer, j)

            get, get_low, get_up = at(k), at(below(k)), at(above(k))
            for j in range(self.parts):
                total = rhs[k, j, s, :] + self.total(k, j, get, get_low, get_up)
                dst[k, j, s, :] = (1.0 - OMEGA) * get(j) + self.gain[k, j, s, :] * total

        each_layer(body, together)

    def image(self, k, j, src, gravity=0.0, storage=True):
        s = slice(0, self.rows)
        kl, ku = below(k), above(k)

        def get(i):
            return src[k, i, s, :]

        v = get(j)
        south = self.south[k, j, s, :] * (v - lane_roll(v, self.step))
        out = south - lane_roll(south, -self.step)
        out = out + self.west[k, j, s, :] * (v - self.west_of(get, j))
        if j + 1 < self.parts:
            out = out + self.west[k, j + 1, s, :] * (v - get(j + 1))
        else:
            first = get(0)
            out = out - row_roll(self.west[k, 0, s, :] * (first - row_roll(v, 1)), -1)
        out = out + self.lower[k, j, s, :] * (v - src[kl, j, s, :] + gravity)
        out = out + self.lower[k + 1, j, s, :] * (v - src[ku, j, s, :] - gravity)
        if storage:
            out = out + self.storage[k, j, s, :] * v
        return out


def restrict_to(fine, src, rhs, coarse, rhs_coarse, first, together):
    def body(k):
        for j in range(coarse.parts):
            parts = [rhs[k, i, : fine.rows, :] - fine.image(k, i, src) for i in (2 * j, 2 * j + 1)]
            value = pair_sum(parts[0] + parts[1], fine.step)
            rhs_coarse[k, j, : fine.rows, :] = value
            first[k, j, : fine.rows, :] = coarse.gain[k, j, : fine.rows, :] * value

    each_layer(body, together)


def own_lanes(rows):
    lane = lanes_of(rows)
    return jnp.logical_and(lane >= BY // 2, lane < BY // 2 + BY)


def strip_sums(fields):
    lane = lanes_of(SB, 128)
    out = jnp.zeros((SB, 128), F32)
    for i, field in enumerate(fields):
        for k in range(NZ):
            value = field[k, :SB, :]
            value = jnp.where(lane < 64, value[:, 128:], value[:, :128])
            out = jnp.where(lane == 16 * i + k, 0.25 * jnp.sum(value, axis=1, keepdims=True), out)
    return out


def restrict_last(middle, src, rhs, rhs_last, together):
    def body(k):
        parts = [rhs[k, i, : middle.rows, :] - middle.image(k, i, src) for i in (0, 1)]
        rhs_last[k] = pair_sum(parts[0] + parts[1], 2)[:SB]

    each_layer(body, together)


def strip_pair(u):
    odd = (rows_of(u.shape[0], u.shape[1]) & 1) == 1
    return jnp.where(odd, row_roll(u, 1), row_roll(u, -1))


def coarsest(rhs, middle, south, lower, gain, sums, weight, out):
    num = sums + strip_pair(sums)
    den = weight + strip_pair(weight)
    mean = num / lane_roll(den, -16)

    lane = lanes_of(SB, 128)
    now = []
    for k in range(NZ):
        value = jnp.sum(jnp.where(lane == k, mean, 0.0), axis=1, keepdims=True)
        now.append(jnp.broadcast_to(value, (SB, LANES)))
    for _ in range(4):
        new = []
        for k in range(NZ):
            v, s = now[k], south[k]
            total = rhs[k] + s * lane_roll(v, 4) + lane_roll(s * v, -4) + middle[k] * strip_pair(v)
            total = total + lower[k] * now[below(k)] + lower[k + 1] * now[above(k)]
            new.append((1.0 - OMEGA) * v + gain[k] * total)
        now = new
    for k in range(NZ):
        out[k] = now[k]


def weights_of(sums):
    a, b, c, d, e, f = [sums[0:1, i : i + 1] for i in range(6)]
    beta2 = a + EPSILON
    beta = jnp.sqrt(beta2)
    kappa = (b + EPSILON) / beta2
    shift = EPSILON * (a - b) / beta2
    norm = kappa * shift - kappa * b + c
    h00 = (a - b) / beta2
    h10 = jnp.sqrt(jnp.maximum(norm, 0.0) / beta2 + EPSILON)
    scale = beta * h10
    scale2 = scale * scale
    h01 = (shift - kappa * b + d) / (beta * scale)
    h11 = (norm + kappa * (d + c - kappa * b) - e) / scale2
    p = kappa * (1.0 - h11) - h01 * h10
    q = h11 - 1.0 - kappa
    last = p * p * a + q * q * c + f + 2.0 * (p * q * b + p * d + q * e)
    h21_2 = jnp.maximum(last, 0.0) / scale2 + EPSILON
    g00 = h00 * h00 + h10 * h10
    g01 = h00 * h01 + h10 * h11
    g11 = h01 * h01 + h11 * h11 + h21_2
    r0 = beta * h00
    r1 = beta * h01
    factor = g01 / g00
    y1 = (r1 - factor * r0) / (g11 - factor * g01)
    y0 = (r0 - g01 * y1) / g00
    return y0 / beta + y1 * kappa / scale, -y1 / scale


def spread(field, left, right, first):
    lane = lanes_of(ROWS, 128)
    mid = lane_roll(field, 64)
    if not first:
        left, right = lane_roll(left, 64), lane_roll(right, 64)
    return jnp.where(lane < 64, left, mid), jnp.where(lane < 64, mid, right)


def put(ext, f, tiles):
    for half in (0, 1):
        ext[f, half, 0:ROWS, :] = tiles[half]
        ext[f, half, ROWS:, :] = tiles[half][0 : 4 * SA - ROWS]


def fetch(ext, f, j):
    return [ext[f, half, pl.ds(j, SA, stride=4), :] for half in (0, 1)]


def wide(tiles):
    return jnp.concatenate(tiles, axis=1)


def unpack_all(ext, cells, left, right, together):
    half = cells.shape[0] // 2

    def unpack(f):
        put(ext, f, spread(cells[f], left[f], right[f], True))
        put(ext, f + half, spread(cells[f + half], left[f], right[f], False))

    each_layer(unpack, together, half)


def start_kernel(head, old, soil, recharge, tables, out):
    for k in range(NZ):
        porosity, resid = [jnp.take_along_axis(tables[i], soil[k], axis=1) for i in (2, 3)]
        base = porosity * (resid - old[k])
        out[k] = head[k]
        out[NZ + k] = base - recharge[...] if k == NZ - 1 else base


def soil_kernel(tables, cells, left, right, unread, *refs):
    outs, stored, (ext, con, sem) = refs[:5], refs[5:10], refs[10:]
    alpha, porous, hw, hs, hl = outs
    copies = [pltpu.make_async_copy(outs[i], stored[i], sem.at[i]) for i in range(5)]
    unpack_all(ext, cells, left, right, 5)
    table = [jnp.concatenate([tables[i]] * (SA // 8), axis=0) for i in range(4)]

    def look_up(k):
        for j in range(4):
            kind = fetch(ext, k, j)
            con[k, j], here, porosity, resid = [
                wide([jnp.take_along_axis(table[i], t, axis=1) for t in kind]) for i in range(4)
            ]
            alpha[k, j] = here
            porous[k, j] = porosity * (1.0 - resid)

    each_layer(look_up, 5)
    for copy in copies[:2]:
        copy.start()
    row = lax.axis_index("gx") * BX - REACH * BX + 4 * rows_of(SA)
    col = lax.axis_index("gy") * BY - BY // 2 + lanes_of(SA)
    edge_col = jnp.logical_or(col == 0, col == BY * lax.axis_size("gy"))
    edge_row = jnp.logical_or(row == 0, row == BX * lax.axis_size("gx"))

    def harmonic(k):
        inside = one_if(k != 0)
        for j in range(4):
            here = con[k, j]

            def face(there):
                return here * there / (here + there)

            west = face(con[k, j - 1]) if j else jnp.where(edge_row, 0.0, face(row_roll(con[k, 3], 1)))
            hw[k, j] = west
            hs[k, j] = jnp.where(edge_col, 0.0, face(lane_roll(here, 1)))
            hl[k, j] = inside * face(con[below(k), j])

    each_layer(harmonic, 5)
    for copy in copies[2:]:
        copy.start()
    for copy in copies:
        copy.wait()


def setup_kernel(second, *refs):
    refs = list(refs)
    cells, left, right = refs[:3]
    if second:
        stored, refs = refs[3:10], refs[10:]
        statics, sem = refs[27:34], refs[34]
        copies = [pltpu.make_async_copy(stored[i], statics[i], sem.at[i]) for i in range(7)]
        for copy in copies:
            copy.start()
    else:
        given, stored, refs = refs[3:8], refs[28:30], refs[8:28] + refs[30:]
        statics, sem = refs[27:29] + given, refs[29]
        copies = [pltpu.make_async_copy(statics[i], stored[i], sem.at[i]) for i in range(2)]
    head, base, alpha, porous, hw, hs, hl = statics
    (c0, w0, s0, l0, g0, b0, x0, c1, w1, s1, l1, g1, b1, x1, m2, s2, l2, g2, b2, sums) = refs[:20]
    ext, state, rel, x0a, x1a, c2, w2 = refs[20:27]
    unpack_all(ext, cells, left, right, 5)
    if second:
        for copy in copies[:4]:
            copy.wait()

    def cells_of(k):
        for j in range(4):
            if second:
                moved = wide(fetch(ext, k, j))
                here = head[k, j] + moved
                local = base[k, j] + STORAGE * moved
            else:
                here, local = wide(fetch(ext, k, j)), wide(fetch(ext, NZ + k, j))
                head[k, j] = here
                base[k, j] = local
            effective = 1.0 / (1.0 + jnp.exp(-(alpha[k, j] * here)))
            state[k, j] = here
            rel[k, j] = effective * effective
            part = porous[k, j] * effective
            c0[k, j] = STORAGE + part * (alpha[k, j] * (1.0 - effective))
            b0[k, j] = local + part

    each_layer(cells_of, 10)
    for copy in copies[4:] if second else copies:
        if second:
            copy.wait()
        else:
            copy.start()

    def faces(k):
        for j in range(4):
            wet = rel[k, j]
            w0[k, j] = hw[k, j] * (wet + (rel[k, j - 1] if j else row_roll(rel[k, 3], 1)))
            s0[k, j] = hs[k, j] * (wet + lane_roll(wet, 1))
            l0[k, j] = hl[k, j] * (wet + rel[below(k), j])

    each_layer(faces, 5)
    l0[NZ] = jnp.zeros((4, SA, LANES), F32)
    l1[NZ] = jnp.zeros((2, SA, LANES), F32)
    l2[NZ] = jnp.zeros((SB, LANES), F32)
    fine = Level(c0, w0, s0, l0, g0, 4, 1, SA)
    mid = Level(c1, w1, s1, l1, g1, 2, 2, SA)

    def residual(k):
        for j in range(4):
            gain = OMEGA / fine.diagonal(k, j)
            value = -(b0[k, j] + fine.image(k, j, state, 1.0, False))
            g0[k, j] = gain
            b0[k, j] = value
            x0a[k, j] = gain * value

    each_layer(residual, 2)

    def coarsen(k):
        for j in range(2):
            c1[k, j] = pair_sum(c0[k, 2 * j] + c0[k, 2 * j + 1], 1)
            l1[k, j] = pair_sum(l0[k, 2 * j] + l0[k, 2 * j + 1], 1)
            w1[k, j] = pair_sum(w0[k, 2 * j], 1)
            s1[k, j] = from_south(s0[k, 2 * j] + s0[k, 2 * j + 1], 1)

    each_layer(coarsen, 5)

    def coarse(k):
        for j in range(2):
            g1[k, j] = OMEGA / mid.diagonal(k, j)
        c2[k] = pair_sum(c1[k, 0, :SB] + c1[k, 1, :SB], 2)
        l2[k] = pair_sum(l1[k, 0, :SB] + l1[k, 1, :SB], 2)
        w2[k] = pair_sum(w1[k, 0], 2)
        s2[k] = from_south(s1[k, 0, :SB] + s1[k, 1, :SB], 2)

    each_layer(coarse, 5)

    def coarse_gain(k):
        west = w2[k]
        east = row_roll(west, -1)[:SB]
        west = west[:SB]
        south = s2[k]
        diag = c2[k] + west + east + south + lane_roll(south, -4) + l2[k] + l2[k + 1]
        g2[k] = OMEGA / diag
        odd = (rows_of(SB) & 1) == 1
        m2[k] = jnp.where(odd, west, east)

    each_layer(coarse_gain, 5)
    fine.sweep(x0a, x0, b0, None, 5)
    restrict_to(fine, x0, b0, mid, b1, x1a, 2)
    mid.sweep(x1a, x1, b1, None, 5)
    restrict_last(mid, x1, b1, b2, 10)
    sums[...] = strip_sums([b2, c2])
    if not second:
        for copy in copies:
            copy.wait()


def finish(fine, mid, last, b0, x0, b1, x1, b2, sums, weight, work0, work1, e2):
    m2, s2, l2, g2 = last
    coarsest(b2, m2, s2, l2, g2, sums, weight, e2)
    mid.sweep(x1, work1[0], b1, lambda k, j: e2[k], 10)
    mid.sweep(work1[0], work1[1], b1, None, 10)
    corrected = work1[1]
    fine.sweep(x0, work0[0], b0, lambda k, j: corrected[k, j // 2, : fine.rows, :], 5)
    fine.sweep(work0[0], work0[1], b0, None, 5)
    return work0[1]


def write_own(dst, k, j, value):
    own = value[OWN_S : OWN_S + 8]
    lane = lanes_of(8, 128)
    own = jnp.where(lane < 64, lane_roll(own[:, :128], 64), lane_roll(own[:, 128:], 64))
    for half in (0, 1):
        dst[k, 4 * half + j : 4 * half + j + 1, :] = own[half : half + 1]


def cycle_kernel(
    total, weight, c0, w0, s0, l0, g0, b0, x0, c1, w1, s1, l1, g1, b1, x1, m2, s2, l2, g2, b2,
    r0, y0, r1, y1, r2, sums, move,
    f0, f1, h0, h1, e2,
):
    fine = Level(c0, w0, s0, l0, g0, 4, 1, SB)
    mid = Level(c1, w1, s1, l1, g1, 2, 2, SB)
    z = finish(
        fine, mid, (m2, s2, l2, g2), b0, x0, b1, x1, b2, total[...], weight[...], (f0, f1), (h0, h1), e2
    )

    def residual(k):
        for j in range(4):
            value = b0[k, j, :SB, :] - fine.image(k, j, z)
            r0[k, j] = value
            f0[k, j] = g0[k, j, :SB, :] * value
            write_own(move, k, j, z[k, j])

    each_layer(residual, 5)
    fine.sweep(f0, y0, r0, None, 5)
    restrict_to(fine, y0, r0, mid, r1, h0, 5)
    mid.sweep(h0, y1, r1, None, 10)
    restrict_last(mid, y1, r1, r2, 10)
    sums[...] = strip_sums([r2])


def last_kernel(
    total, weight, c0, w0, s0, l0, g0, start, c1, w1, s1, l1, g1, m2, s2, l2, g2, b0, x0, b1, x1, b2,
    products, move,
    f0, f1, h0, h1, e2,
):
    fine = Level(c0, w0, s0, l0, g0, 4, 1, SB)
    mid = Level(c1, w1, s1, l1, g1, 2, 2, SB)
    z = finish(
        fine, mid, (m2, s2, l2, g2), b0, x0, b1, x1, b2, total[...], weight[...], (f0, f1), (h0, h1), e2
    )
    row = rows_of(8)
    own = jnp.logical_and(own_lanes(8), row < 2)

    def body(k, sums):
        sums = list(sums)
        for j in range(4):
            write_own(move, k, j, z[k, j])
            image = fine.image(k, j, z)[OWN_S : OWN_S + 8]
            u = jnp.where(own, start[k, j, OWN_S : OWN_S + 8, :], 0.0)
            t = jnp.where(own, b0[k, j, OWN_S : OWN_S + 8, :], 0.0)
            r = jnp.where(own, t - image, 0.0)
            for i, item in enumerate((u * u, u * t, t * t, u * r, t * r, r * r)):
                sums[i] = sums[i] + item
        return tuple(sums)

    sums = (jnp.zeros((8, LANES), F32),) * 6
    for k in range(NZ):
        sums = body(k, sums)
    lane = lanes_of(1, 128)
    out = jnp.zeros((1, 128), F32)
    for i, item in enumerate(sums):
        value = jnp.sum(jnp.sum(item, axis=0, keepdims=True), axis=1, keepdims=True)
        out = jnp.where(lane == i, value, out)
    products[...] = out


def move_kernel(products, first, second, out):
    one, two = weights_of(products)
    out[...] = one[None] * first[...] + two[None] * second[...]


def end_kernel(head, moved, products, first, second, out):
    one, two = weights_of(products)
    out[...] = head[...] + moved[...] + one[None] * first[...] + two[None] * second[...]


VMEM = pl.BlockSpec(memory_space=pltpu.VMEM)
HBM = pl.BlockSpec(memory_space=pltpu.HBM)


def shape(*dims):
    return jax.ShapeDtypeStruct(dims, F32)


def buffer(*dims):
    return pltpu.VMEM(dims, F32)


ANY = pl.BlockSpec(memory_space=pl.ANY)


def call(kernel, args, outs, scratch, limit, in_hbm=(), out_hbm=(), unread=(), cost=None):
    place = [ANY if i in unread else HBM if i in in_hbm else VMEM for i in range(len(args))]
    args = [pltpu.with_memory_space_constraint(a, pltpu.HBM) if i in in_hbm else a for i, a in enumerate(args)]
    many = isinstance(outs, list)
    if many:
        outs = [pltpu.HBM(a.shape, a.dtype) if i in out_hbm else a for i, a in enumerate(outs)]
    spec = [HBM if i in out_hbm else VMEM for i in range(len(outs))] if many else VMEM
    return pl.pallas_call(
        kernel,
        out_shape=outs,
        in_specs=place,
        out_specs=spec,
        scratch_shapes=scratch,
        compiler_params=pltpu.CompilerParams(vmem_limit_bytes=limit),
        cost_estimate=cost,
    )(*args)


FINE = (NZ, 4, SA, LANES)


def soil_fields(inputs):
    scratch = [pltpu.VMEM((NZ, 2, 4 * SA, 128), jnp.int32), buffer(*FINE), pltpu.SemaphoreType.DMA((5,))]
    outs = [shape(*FINE)] * 10
    cost = pl.CostEstimate(flops=10**7, bytes_accessed=2 * 10**7, transcendentals=0)
    return call(soil_kernel, inputs, outs, scratch, 6 << 20, (), range(5, 10), (4,), cost)


def setup(inputs, second):
    fine = shape(*FINE)
    outs = (
        [fine] * 3 + [shape(NZ + 1, 4, SA, LANES)] + [fine] * 3
        + [shape(NZ, 2, SA, LANES)] * 3 + [shape(NZ + 1, 2, SA, LANES)] + [shape(NZ, 2, SA, LANES)] * 3
        + [shape(NZ, SB, LANES)] * 2 + [shape(NZ + 1, SB, LANES)] + [shape(NZ, SB, LANES)] * 2
        + [shape(SB, 128)] + ([] if second else [fine] * 2)
    )
    stored = 7 if second else 2
    scratch = (
        [buffer(NZ if second else 2 * NZ, 2, 4 * SA, 128)] + [buffer(*FINE)] * 3
        + [buffer(NZ, 2, SA, LANES), buffer(NZ, SB, LANES), buffer(NZ, SA, LANES)]
        + [buffer(*FINE)] * stored + [pltpu.SemaphoreType.DMA((stored,))]
    )
    kernel = functools.partial(setup_kernel, second)
    if second:
        return call(kernel, inputs, outs, scratch, 15 << 20, range(3, 10))
    return call(kernel, inputs, outs, scratch, 11 << 20, (), range(20, 22))


def work():
    return [buffer(NZ, 4, SB, LANES)] * 2 + [buffer(NZ, 2, SB, LANES)] * 2 + [buffer(NZ, SB, LANES)]


def shifted(field, axis, by):
    count = lax.axis_size(axis)
    return lax.ppermute(field, axis, [(i, (i + by) % count) for i in range(count)])


def across(field):
    near = jnp.concatenate([shifted(field, "gx", 1), field, shifted(field, "gx", -1)], axis=1)
    return shifted(near, "gx", 3), near, shifted(near, "gx", -3)


def pack_kernel(west, near, east, *refs):
    rows, to_north, to_south = refs[-3:]
    half = rows.shape[0] // 2
    lane = lanes_of(ROWS, 128)

    def pack(f):
        low, high = [
            jnp.concatenate([part[i] for part in (west, near, east)], axis=0) for i in (f, f + half)
        ]
        rows[f] = low
        rows[f + half] = high
        low = lane_roll(low, 64)
        to_north[f] = jnp.where(lane < 64, low, high)
        to_south[f] = jnp.where(lane < 64, high, low)

    each_layer(pack, 5, half)


def packed(parts, after=()):
    fields, dtype = parts[0].shape[0], parts[0].dtype
    full = jax.ShapeDtypeStruct((fields, ROWS, BY), dtype)
    half = jax.ShapeDtypeStruct((fields // 2, ROWS, BY), dtype)
    return call(pack_kernel, [*parts, *after], [full, half, half], [], 4 << 20, unread=range(3, 3 + len(after)))


def surroundings(field):
    rows, to_north, to_south = packed(across(field))
    return rows, shifted(to_north, "gy", 1), shifted(to_south, "gy", -1)


def summed(field):
    count = lax.axis_size("gy")
    for flip in (1, 2, 6):
        if flip < count:
            field = field + lax.ppermute(field, "gy", [(i, i ^ flip) for i in range(count)])
    return field


def summed_over_all(row):
    axes = ("gx", "gy")
    count = lax.axis_size(axes)
    parts = lax.all_to_all(jnp.broadcast_to(row[None], (count, 1, 128)), axes, 0, 0, tiled=True)
    return jnp.sum(parts, axis=0)


def on_device(
    pressure, saturation_old, soil_type, recharge, ksat_table, alpha_table, porosity_table, residual_table
):
    tables = jnp.stack([ksat_table, alpha_table, porosity_table, residual_table])
    tables = jnp.pad(tables, ((0, 0), (0, 128 - tables.shape[1])))
    tables = jnp.broadcast_to(tables[:, None, :], (4, 8, 128))
    soil_cells = surroundings(soil_type)
    start = call(
        start_kernel,
        [pressure, saturation_old, soil_type, recharge, tables],
        shape(2 * NZ, BX, BY),
        [],
        4 << 20,
    )
    rows, to_north, to_south = packed(across(start), soil_cells[1:])
    cells = (rows, shifted(to_north, "gy", 1), shifted(to_south, "gy", -1))
    got = soil_fields([tables, *soil_cells, to_north])
    given, statics = got[:5], got[5:]
    moved = None
    for newton in range(2):
        if newton:
            got = setup([*surroundings(moved), *statics], True)
        else:
            got = setup([*cells, *given], False)
            statics = [*got[20:], *statics]
        (c0, w0, s0, l0, g0, b0, x0, c1, w1, s1, l1, g1, b1, x1, m2, s2, l2, g2, b2, sums) = got[:20]
        weight = summed(sums)
        r0, y0, r1, y1, r2, sums, first = call(
            cycle_kernel,
            [weight, weight, *got[:19]],
            [shape(NZ, 4, SB, LANES)] * 2 + [shape(NZ, 2, SB, LANES)] * 2
            + [shape(NZ, SB, LANES), shape(SB, 128), shape(NZ, BX, BY)],
            work(),
            6 << 20,
        )
        total = summed(sums)
        products, second = call(
            last_kernel,
            [total, weight, c0, w0, s0, l0, g0, b0, c1, w1, s1, l1, g1, m2, s2, l2, g2, r0, y0, r1, y1, r2],
            [shape(1, 128), shape(NZ, BX, BY)],
            work(),
            6 << 20,
        )
        ends = [summed_over_all(products), first, second]
        if newton:
            return call(end_kernel, [pressure, moved, *ends], shape(NZ, BX, BY), [], 4 << 20)
        moved = call(move_kernel, ends, shape(NZ, BX, BY), [], 4 << 20)


def solution(mesh):
    placed = (P(None, "gx", "gy"),) * 3 + (P("gx", "gy"),) + (P(),) * 4
    return jax.shard_map(
        on_device, mesh=mesh, in_specs=placed, out_specs=P(None, "gx", "gy"), check_vma=False
    )
```

```python
import functools

import jax
import jax.numpy as jnp
from jax import lax
from jax.experimental import pallas as pl
from jax.experimental.pallas import tpu as pltpu
from jax.sharding import PartitionSpec as P


NZ = 10
BX = 8
BY = 128
REACH = 4
ROWS = (2 * REACH + 1) * BX
SA = 24
SB = 16
LANES = 128
OWN_S = REACH * BX // 4
OMEGA = 0.8
STORAGE = 0.05
EPSILON = 1e-06
F32 = jnp.float32


def lane_roll(v, shift):
    return pltpu.roll(v, shift % v.shape[1], 1)


def row_roll(v, shift):
    return pltpu.roll(v, shift % v.shape[0], 0)


def lanes_of(rows, width=LANES):
    return lax.broadcasted_iota(jnp.int32, (rows, width), 1)


def rows_of(rows, width=LANES):
    return lax.broadcasted_iota(jnp.int32, (rows, width), 0)


def pair_sum(u, step):
    low = (lanes_of(u.shape[0]) & step) == 0
    return u + jnp.where(low, lane_roll(u, -step), lane_roll(u, step))


def from_south(u, step):
    low = (lanes_of(u.shape[0]) & step) == 0
    return jnp.where(low, u, lane_roll(u, step))


def each_layer(body, together, count=NZ):
    if together == count:
        for k in range(count):
            body(k)
        return

    def step(i, carry):
        for j in range(together):
            body(together * i + j)
        return carry

    lax.fori_loop(0, count // together, step, 0)


def below(k):
    return max(k - 1, 0) if isinstance(k, int) else jnp.maximum(k - 1, 0)


def above(k):
    return min(k + 1, NZ - 1) if isinstance(k, int) else jnp.minimum(k + 1, NZ - 1)


def one_if(condition):
    return jnp.where(condition, 1.0, 0.0).astype(F32)


class Level:
    def __init__(self, storage, west, south, lower, gain, across, along, rows):
        self.storage, self.west, self.south, self.lower, self.gain = storage, west, south, lower, gain
        self.across, self.along, self.rows = across, along, rows
        self.parts = across * along

    def load(self, src, k):
        return [src[k, j, 0 : self.rows, :] for j in range(self.parts)]

    def from_west(self, v):
        n = self.along
        return [v[j - n] if j >= n else row_roll(v[self.parts - n + j], 1) for j in range(self.parts)]

    def from_east(self, v):
        n, m = self.along, self.parts
        return [v[j + n] if j + n < m else row_roll(v[j + n - m], -1) for j in range(m)]

    def from_south(self, v):
        n = self.along
        return [v[j - 1] if j % n else lane_roll(v[j + n - 1], 1) for j in range(self.parts)]

    def from_north(self, v):
        n = self.along
        return [v[j + 1] if (j + 1) % n else lane_roll(v[j + 1 - n], -1) for j in range(self.parts)]

    def diagonals(self, k):
        west, south = self.load(self.west, k), self.load(self.south, k)
        east, north = self.from_east(west), self.from_north(south)
        out = []
        for j in range(self.parts):
            s = slice(0, self.rows)
            total = self.storage[k, j, s, :] + west[j] + east[j] + south[j] + north[j]
            out.append(total + self.lower[k, j, s, :] + self.lower[k + 1, j, s, :])
        return out

    def sweep(self, src, dst, rhs, add, together):
        s = slice(0, self.rows)

        def body(k):
            def at(layer, j):
                return src[layer, j, s, :] if add is None else src[layer, j, s, :] + add(layer, j)

            now = [at(k, j) for j in range(self.parts)]
            west, south = self.load(self.west, k), self.load(self.south, k)
            w, b = self.from_west(now), self.from_south(now)
            e = self.from_east([p * q for p, q in zip(west, now)])
            f = self.from_north([p * q for p, q in zip(south, now)])
            for j in range(self.parts):
                total = rhs[k, j, s, :] + west[j] * w[j] + e[j] + south[j] * b[j] + f[j]
                total = total + self.lower[k, j, s, :] * at(below(k), j) + self.lower[k + 1, j, s, :] * at(above(k), j)
                dst[k, j, s, :] = (1.0 - OMEGA) * now[j] + self.gain[k, j, s, :] * total

        each_layer(body, together)

    def images(self, k, src, gravity=0.0, storage=True):
        s = slice(0, self.rows)
        now = self.load(src, k)
        west, south = self.load(self.west, k), self.load(self.south, k)
        w = [p * (v - n) for p, v, n in zip(west, now, self.from_west(now))]
        b = [p * (v - n) for p, v, n in zip(south, now, self.from_south(now))]
        e, f = self.from_east(w), self.from_north(b)
        out = []
        for j in range(self.parts):
            total = (w[j] - e[j]) + (b[j] - f[j])
            total = total + self.lower[k, j, s, :] * (now[j] - src[below(k), j, s, :] + gravity)
            total = total + self.lower[k + 1, j, s, :] * (now[j] - src[above(k), j, s, :] - gravity)
            if storage:
                total = total + self.storage[k, j, s, :] * now[j]
            out.append(total)
        return out


def restrict_to(fine, src, rhs, coarse, rhs_coarse, first, together):
    def body(k):
        images = fine.images(k, src)
        for j in range(coarse.parts):
            parts = [rhs[k, i, : fine.rows, :] - images[i] for i in range(4 * j, 4 * j + 4)]
            value = (parts[0] + parts[1]) + (parts[2] + parts[3])
            rhs_coarse[k, j, : fine.rows, :] = value
            first[k, j, : fine.rows, :] = coarse.gain[k, j, : fine.rows, :] * value

    each_layer(body, together)


def own_lanes(rows):
    lane = lanes_of(rows)
    return jnp.logical_and(lane >= BY // 4, lane < BY // 4 + BY // 2)


def strip_sums(fields):
    lane = lanes_of(SB, 128)
    out = jnp.zeros((SB, 128), F32)
    for i, field in enumerate(fields):
        for k in range(NZ):
            value = jnp.where(own_lanes(SB), field[k, :SB, :], 0.0)
            out = jnp.where(lane == 16 * i + k, 0.5 * jnp.sum(value, axis=1, keepdims=True), out)
    return out


def restrict_last(middle, src, rhs, rhs_last, together):
    def body(k):
        parts = [rhs[k, i, : middle.rows, :] - image for i, image in enumerate(middle.images(k, src))]
        rhs_last[k] = pair_sum(parts[0] + parts[1], 1)[:SB]

    each_layer(body, together)


def strip_pair(u):
    odd = (rows_of(u.shape[0], u.shape[1]) & 1) == 1
    return jnp.where(odd, row_roll(u, 1), row_roll(u, -1))


def coarsest(rhs, middle, south, lower, gain, sums, weight, out):
    num = sums + strip_pair(sums)
    den = weight + strip_pair(weight)
    mean = num / lane_roll(den, -16)

    lane = lanes_of(SB, 128)
    now = []
    for k in range(NZ):
        value = jnp.sum(jnp.where(lane == k, mean, 0.0), axis=1, keepdims=True)
        now.append(jnp.broadcast_to(value, (SB, LANES)))
    for _ in range(4):
        new = []
        for k in range(NZ):
            v, s = now[k], south[k]
            total = rhs[k] + s * lane_roll(v, 2) + lane_roll(s * v, -2) + middle[k] * strip_pair(v)
            total = total + lower[k] * now[below(k)] + lower[k + 1] * now[above(k)]
            new.append((1.0 - OMEGA) * v + gain[k] * total)
        now = new
    for k in range(NZ):
        out[k] = now[k]


def weights_of(sums):
    a, b, c, d, e, f = [sums[0:1, i : i + 1] for i in range(6)]
    beta2 = a + EPSILON
    beta = jnp.sqrt(beta2)
    kappa = (b + EPSILON) / beta2
    shift = EPSILON * (a - b) / beta2
    norm = kappa * shift - kappa * b + c
    h00 = (a - b) / beta2
    h10 = jnp.sqrt(jnp.maximum(norm, 0.0) / beta2 + EPSILON)
    scale = beta * h10
    scale2 = scale * scale
    h01 = (shift - kappa * b + d) / (beta * scale)
    h11 = (norm + kappa * (d + c - kappa * b) - e) / scale2
    p = kappa * (1.0 - h11) - h01 * h10
    q = h11 - 1.0 - kappa
    last = p * p * a + q * q * c + f + 2.0 * (p * q * b + p * d + q * e)
    h21_2 = jnp.maximum(last, 0.0) / scale2 + EPSILON
    g00 = h00 * h00 + h10 * h10
    g01 = h00 * h01 + h10 * h11
    g11 = h01 * h01 + h11 * h11 + h21_2
    r0 = beta * h00
    r1 = beta * h01
    factor = g01 / g00
    y1 = (r1 - factor * r0) / (g11 - factor * g01)
    y0 = (r0 - g01 * y1) / g00
    return y0 / beta + y1 * kappa / scale, -y1 / scale


def spread(field, left, right, first):
    lane = lanes_of(ROWS, 128)
    begin, end = lane < 32, lane >= 96
    tiles = []
    for odd in (0, 1):
        turn = 32 * odd + (0 if first else 64)
        low, high = (lane_roll(left, -turn), lane_roll(right, turn)) if turn else (left, right)
        tiles.append(jnp.where(begin, low, jnp.where(end, high, lane_roll(field, -32 if odd else 32))))
    return tiles


def put(ext, f, tiles):
    for half in (0, 1):
        ext[f, half, 0:ROWS, :] = tiles[half]
        ext[f, half, ROWS:, :] = tiles[half][0 : 4 * SA - ROWS]


def fetch(ext, f, j):
    return [ext[f, half, pl.ds(j, SA, stride=4), :] for half in (0, 1)]


def unpack_all(ext, cells, left, right, together):
    half = cells.shape[0] // 2

    def unpack(f):
        put(ext, f, spread(cells[f], left[f], right[f], True))
        put(ext, f + half, spread(cells[f + half], left[f], right[f], False))

    each_layer(unpack, together, half)


def sorted_lanes(inverse=False):
    a, b = lanes_of(128), rows_of(128)
    if inverse:
        a, b = b, a
    return jnp.where(a == (b & 1) * 64 + (b >> 1), 1.0, 0.0).astype(F32)


def moved_lanes(field, matrix):
    rows = field.reshape(-1, 128)
    out = jnp.dot(rows, matrix, precision=lax.Precision.HIGHEST, preferred_element_type=F32)
    return out.reshape(field.shape)


def start_kernel(head_in, old_in, soil_in, recharge_in, tables, kinds, out, head, old, soil, recharge, sem):
    pairs = [(soil_in, soil), (old_in, old), (recharge_in, recharge), (head_in, head)]
    copies = [pltpu.make_async_copy(a, b, sem.at[i]) for i, (a, b) in enumerate(pairs)]
    for copy in copies:
        copy.start()
    matrix = sorted_lanes()
    copies[0].wait()
    kinds[...] = moved_lanes(soil[...].astype(F32), matrix)
    for copy in copies[1:]:
        copy.wait()
    base = []
    for k in range(NZ):
        porosity, resid = [jnp.take_along_axis(tables[i], soil[k], axis=1) for i in (2, 3)]
        value = porosity * (resid - old[k])
        base.append(value - recharge[...] if k == NZ - 1 else value)
    out[0:NZ] = moved_lanes(head[...], matrix)
    out[NZ:] = moved_lanes(jnp.stack(base), matrix)


def soil_kernel(tables, cells, left, right, unread, *refs):
    outs, stored, (ext, con, sem) = refs[:5], refs[5:10], refs[10:]
    alpha, porous, hw, hs, hl = outs
    copies = [pltpu.make_async_copy(outs[i], stored[i], sem.at[i]) for i in range(5)]
    unpack_all(ext, cells, left, right, 5)
    table = [jnp.concatenate([tables[i]] * (SA // 8), axis=0) for i in range(4)]

    def look_up(k):
        for j in range(4):
            for odd, tile in enumerate(fetch(ext, k, j)):
                kind = tile.astype(jnp.int32)
                con[k, 2 * j + odd], here, porosity, resid = [
                    jnp.take_along_axis(table[i], kind, axis=1) for i in range(4)
                ]
                alpha[k, 2 * j + odd] = here
                porous[k, 2 * j + odd] = porosity * (1.0 - resid)

    each_layer(look_up, 5)
    for copy in copies[:2]:
        copy.start()
    row = lax.axis_index("gx") * BX - REACH * BX + 4 * rows_of(SA)
    col = lax.axis_index("gy") * BY - BY // 2 + 2 * lanes_of(SA)
    edge_col = jnp.logical_or(col == 0, col == BY * lax.axis_size("gy"))
    edge_row = jnp.logical_or(row == 0, row == BX * lax.axis_size("gx"))

    def harmonic(k):
        inside = one_if(k != 0)
        for j in range(8):
            here = con[k, j]

            def face(there):
                return here * there / (here + there)

            west = face(con[k, j - 2]) if j > 1 else jnp.where(edge_row, 0.0, face(row_roll(con[k, 6 + j], 1)))
            south = face(con[k, j - 1]) if j % 2 else jnp.where(edge_col, 0.0, face(lane_roll(con[k, j + 1], 1)))
            hw[k, j] = west
            hs[k, j] = south
            hl[k, j] = inside * face(con[below(k), j])

    each_layer(harmonic, 5)
    for copy in copies[2:]:
        copy.start()
    for copy in copies:
        copy.wait()


def setup_kernel(second, *refs):
    refs = list(refs)
    cells, left, right = refs[:3]
    if second:
        stored, refs = refs[3:10], refs[10:]
        statics, sem = refs[27:34], refs[34]
        copies = [pltpu.make_async_copy(stored[i], statics[i], sem.at[i]) for i in range(7)]
        for copy in copies:
            copy.start()
    else:
        given, stored, refs = refs[3:8], refs[28:30], refs[8:28] + refs[30:]
        statics, sem = refs[27:29] + given, refs[29]
        copies = [pltpu.make_async_copy(statics[i], stored[i], sem.at[i]) for i in range(2)]
    head, base, alpha, porous, hw, hs, hl = statics
    (c0, w0, s0, l0, g0, b0, x0, c1, w1, s1, l1, g1, b1, x1, m2, s2, l2, g2, b2, sums) = refs[:20]
    ext, state, rel, x0a, x1a, c2, w2 = refs[20:27]
    unpack_all(ext, cells, left, right, 5)
    if second:
        for copy in copies[:4]:
            copy.wait()

    def cells_of(k):
        for j in range(8):
            if j % 2 == 0:
                tiles = fetch(ext, k, j // 2)
                others = None if second else fetch(ext, NZ + k, j // 2)
            if second:
                moved = tiles[j % 2]
                here = head[k, j] + moved
                local = base[k, j] + STORAGE * moved
            else:
                here, local = tiles[j % 2], others[j % 2]
                head[k, j] = here
                base[k, j] = local
            effective = 1.0 / (1.0 + jnp.exp(-(alpha[k, j] * here)))
            state[k, j] = here
            rel[k, j] = effective * effective
            part = porous[k, j] * effective
            c0[k, j] = STORAGE + part * (alpha[k, j] * (1.0 - effective))
            b0[k, j] = local + part

    each_layer(cells_of, 10)
    for copy in copies[4:] if second else copies:
        if second:
            copy.wait()
        else:
            copy.start()

    fine = Level(c0, w0, s0, l0, g0, 4, 2, SA)
    mid = Level(c1, w1, s1, l1, g1, 2, 1, SA)

    def faces(k):
        wet = fine.load(rel, k)
        w, b = fine.from_west(wet), fine.from_south(wet)
        for j in range(8):
            w0[k, j] = hw[k, j] * (wet[j] + w[j])
            s0[k, j] = hs[k, j] * (wet[j] + b[j])
            l0[k, j] = hl[k, j] * (wet[j] + rel[below(k), j])

    each_layer(faces, 5)
    l0[NZ] = jnp.zeros((8, SA, LANES), F32)
    l1[NZ] = jnp.zeros((2, SA, LANES), F32)
    l2[NZ] = jnp.zeros((SB, LANES), F32)

    def residual(k):
        diagonals, images = fine.diagonals(k), fine.images(k, state, 1.0, False)
        for j in range(8):
            gain = OMEGA / diagonals[j]
            value = -(b0[k, j] + images[j])
            g0[k, j] = gain
            b0[k, j] = value
            x0a[k, j] = gain * value

    each_layer(residual, 2)

    def coarsen(k):
        for j in range(2):
            i = 4 * j
            c1[k, j] = (c0[k, i] + c0[k, i + 1]) + (c0[k, i + 2] + c0[k, i + 3])
            l1[k, j] = (l0[k, i] + l0[k, i + 1]) + (l0[k, i + 2] + l0[k, i + 3])
            w1[k, j] = w0[k, i] + w0[k, i + 1]
            s1[k, j] = s0[k, i] + s0[k, i + 2]

    each_layer(coarsen, 5)

    def coarse(k):
        for j, diagonal in enumerate(mid.diagonals(k)):
            g1[k, j] = OMEGA / diagonal
        c2[k] = pair_sum(c1[k, 0, :SB] + c1[k, 1, :SB], 1)
        l2[k] = pair_sum(l1[k, 0, :SB] + l1[k, 1, :SB], 1)
        w2[k] = pair_sum(w1[k, 0], 1)
        s2[k] = from_south(s1[k, 0, :SB] + s1[k, 1, :SB], 1)

    each_layer(coarse, 5)

    def coarse_gain(k):
        west = w2[k]
        east = row_roll(west, -1)[:SB]
        west = west[:SB]
        south = s2[k]
        diag = c2[k] + west + east + south + lane_roll(south, -2) + l2[k] + l2[k + 1]
        g2[k] = OMEGA / diag
        odd = (rows_of(SB) & 1) == 1
        m2[k] = jnp.where(odd, west, east)

    each_layer(coarse_gain, 5)
    fine.sweep(x0a, x0, b0, None, 5)
    restrict_to(fine, x0, b0, mid, b1, x1a, 2)
    mid.sweep(x1a, x1, b1, None, 5)
    restrict_last(mid, x1, b1, b2, 10)
    sums[...] = strip_sums([b2, c2])
    if not second:
        for copy in copies:
            copy.wait()


def finish(fine, mid, last, b0, x0, b1, x1, b2, sums, weight, work0, work1, e2):
    m2, s2, l2, g2 = last
    coarsest(b2, m2, s2, l2, g2, sums, weight, e2)
    mid.sweep(x1, work1[0], b1, lambda k, j: e2[k], 10)
    mid.sweep(work1[0], work1[1], b1, None, 10)
    corrected = work1[1]
    fine.sweep(x0, work0[0], b0, lambda k, j: corrected[k, j // 4, : fine.rows, :], 5)
    fine.sweep(work0[0], work0[1], b0, None, 5)
    return work0[1]


def write_own(dst, k, j, even, odd):
    lane = lanes_of(8, 128)
    s = slice(OWN_S, OWN_S + 8)
    own = jnp.where(lane < 64, lane_roll(even[s], -32), lane_roll(odd[s], 32))
    for half in (0, 1):
        dst[k, 4 * half + j : 4 * half + j + 1, :] = own[half : half + 1]


def cycle_kernel(
    total, weight, c0, w0, s0, l0, g0, b0, x0, c1, w1, s1, l1, g1, b1, x1, m2, s2, l2, g2, b2,
    r0, y0, r1, y1, r2, sums, move,
    f0, f1, h0, h1, e2,
):
    fine = Level(c0, w0, s0, l0, g0, 4, 2, SB)
    mid = Level(c1, w1, s1, l1, g1, 2, 1, SB)
    z = finish(
        fine, mid, (m2, s2, l2, g2), b0, x0, b1, x1, b2, total[...], weight[...], (f0, f1), (h0, h1), e2
    )

    def residual(k):
        images = fine.images(k, z)
        for j in range(8):
            value = b0[k, j, :SB, :] - images[j]
            r0[k, j] = value
            f0[k, j] = g0[k, j, :SB, :] * value
        for j in range(4):
            write_own(move, k, j, z[k, 2 * j], z[k, 2 * j + 1])

    each_layer(residual, 5)
    fine.sweep(f0, y0, r0, None, 5)
    restrict_to(fine, y0, r0, mid, r1, h0, 5)
    mid.sweep(h0, y1, r1, None, 10)
    restrict_last(mid, y1, r1, r2, 10)
    sums[...] = strip_sums([r2])


def last_kernel(
    total, weight, c0, w0, s0, l0, g0, start, c1, w1, s1, l1, g1, m2, s2, l2, g2, b0, x0, b1, x1, b2,
    products, move,
    f0, f1, h0, h1, e2,
):
    fine = Level(c0, w0, s0, l0, g0, 4, 2, SB)
    mid = Level(c1, w1, s1, l1, g1, 2, 1, SB)
    z = finish(
        fine, mid, (m2, s2, l2, g2), b0, x0, b1, x1, b2, total[...], weight[...], (f0, f1), (h0, h1), e2
    )
    row = rows_of(8)
    own = jnp.logical_and(own_lanes(8), row < 2)

    def body(k, sums):
        sums = list(sums)
        images = fine.images(k, z)
        for j in range(4):
            write_own(move, k, j, z[k, 2 * j], z[k, 2 * j + 1])
        for j in range(8):
            image = images[j][OWN_S : OWN_S + 8]
            u = jnp.where(own, start[k, j, OWN_S : OWN_S + 8, :], 0.0)
            t = jnp.where(own, b0[k, j, OWN_S : OWN_S + 8, :], 0.0)
            r = jnp.where(own, t - image, 0.0)
            for i, item in enumerate((u * u, u * t, t * t, u * r, t * r, r * r)):
                sums[i] = sums[i] + item
        return tuple(sums)

    sums = (jnp.zeros((8, LANES), F32),) * 6
    for k in range(NZ):
        sums = body(k, sums)
    lane = lanes_of(1, 128)
    out = jnp.zeros((1, 128), F32)
    for i, item in enumerate(sums):
        value = jnp.sum(jnp.sum(item, axis=0, keepdims=True), axis=1, keepdims=True)
        out = jnp.where(lane == i, value, out)
    products[...] = out


def move_kernel(products, first, second, out):
    one, two = weights_of(products)
    out[...] = one[None] * first[...] + two[None] * second[...]


def end_kernel(head, moved, products, first, second, out):
    one, two = weights_of(products)
    change = moved[...] + one[None] * first[...] + two[None] * second[...]
    out[...] = head[...] + moved_lanes(change, sorted_lanes(True))


VMEM = pl.BlockSpec(memory_space=pltpu.VMEM)
HBM = pl.BlockSpec(memory_space=pltpu.HBM)


def shape(*dims):
    return jax.ShapeDtypeStruct(dims, F32)


def buffer(*dims):
    return pltpu.VMEM(dims, F32)


ANY = pl.BlockSpec(memory_space=pl.ANY)


def call(kernel, args, outs, scratch, limit, in_hbm=(), out_hbm=(), unread=(), cost=None):
    place = [ANY if i in unread else HBM if i in in_hbm else VMEM for i in range(len(args))]
    args = [pltpu.with_memory_space_constraint(a, pltpu.HBM) if i in in_hbm else a for i, a in enumerate(args)]
    many = isinstance(outs, list)
    if many:
        outs = [pltpu.HBM(a.shape, a.dtype) if i in out_hbm else a for i, a in enumerate(outs)]
    spec = [HBM if i in out_hbm else VMEM for i in range(len(outs))] if many else VMEM
    return pl.pallas_call(
        kernel,
        out_shape=outs,
        in_specs=place,
        out_specs=spec,
        scratch_shapes=scratch,
        compiler_params=pltpu.CompilerParams(vmem_limit_bytes=limit),
        cost_estimate=cost,
    )(*args)


FINE = (NZ, 8, SA, LANES)


def soil_fields(inputs):
    scratch = [buffer(NZ, 2, 4 * SA, 128), buffer(*FINE), pltpu.SemaphoreType.DMA((5,))]
    outs = [shape(*FINE)] * 10
    cost = pl.CostEstimate(flops=10**7, bytes_accessed=2 * 10**7, transcendentals=0)
    return call(soil_kernel, inputs, outs, scratch, 6 << 20, (), range(5, 10), (4,), cost)


def setup(inputs, second):
    fine = shape(*FINE)
    outs = (
        [fine] * 3 + [shape(NZ + 1, 8, SA, LANES)] + [fine] * 3
        + [shape(NZ, 2, SA, LANES)] * 3 + [shape(NZ + 1, 2, SA, LANES)] + [shape(NZ, 2, SA, LANES)] * 3
        + [shape(NZ, SB, LANES)] * 2 + [shape(NZ + 1, SB, LANES)] + [shape(NZ, SB, LANES)] * 2
        + [shape(SB, 128)] + ([] if second else [fine] * 2)
    )
    stored = 7 if second else 2
    scratch = (
        [buffer(NZ if second else 2 * NZ, 2, 4 * SA, 128)] + [buffer(*FINE)] * 3
        + [buffer(NZ, 2, SA, LANES), buffer(NZ, SB, LANES), buffer(NZ, SA, LANES)]
        + [buffer(*FINE)] * stored + [pltpu.SemaphoreType.DMA((stored,))]
    )
    kernel = functools.partial(setup_kernel, second)
    if second:
        return call(kernel, inputs, outs, scratch, 15 << 20, range(3, 10))
    return call(kernel, inputs, outs, scratch, 11 << 20, (), range(20, 22))


def work():
    return [buffer(NZ, 8, SB, LANES)] * 2 + [buffer(NZ, 2, SB, LANES)] * 2 + [buffer(NZ, SB, LANES)]


def shifted(field, axis, by):
    count = lax.axis_size(axis)
    return lax.ppermute(field, axis, [(i, (i + by) % count) for i in range(count)])


def across(field):
    near = jnp.concatenate([shifted(field, "gx", 1), field, shifted(field, "gx", -1)], axis=1)
    return shifted(near, "gx", 3), near, shifted(near, "gx", -3)


def pack_kernel(west, near, east, *refs):
    rows, to_north, to_south = refs[-3:]
    half = rows.shape[0] // 2
    lane = lanes_of(ROWS, 128)

    def quarters(*parts):
        return jnp.where(lane < 64, jnp.where(lane < 32, *parts[:2]), jnp.where(lane < 96, *parts[2:]))

    def pack(f):
        low, high = [
            jnp.concatenate([part[i] for part in (west, near, east)], axis=0) for i in (f, f + half)
        ]
        rows[f] = low
        rows[f + half] = high
        to_north[f] = quarters(lane_roll(low, -32), lane_roll(low, -64), lane_roll(high, 32), high)
        to_south[f] = quarters(lane_roll(high, -64), lane_roll(high, 32), low, lane_roll(low, 96))

    each_layer(pack, 5, half)


def packed(parts, after=()):
    fields, dtype = parts[0].shape[0], parts[0].dtype
    full = jax.ShapeDtypeStruct((fields, ROWS, BY), dtype)
    half = jax.ShapeDtypeStruct((fields // 2, ROWS, BY), dtype)
    return call(pack_kernel, [*parts, *after], [full, half, half], [], 4 << 20, unread=range(3, 3 + len(after)))


def surroundings(field):
    rows, to_north, to_south = packed(across(field))
    return rows, shifted(to_north, "gy", 1), shifted(to_south, "gy", -1)


def summed(field):
    count = lax.axis_size("gy")
    for flip in (1, 2, 6):
        if flip < count:
            field = field + lax.ppermute(field, "gy", [(i, i ^ flip) for i in range(count)])
    return field


def summed_over_all(row):
    axes = ("gx", "gy")
    count = lax.axis_size(axes)
    parts = lax.all_to_all(jnp.broadcast_to(row[None], (count, 1, 128)), axes, 0, 0, tiled=True)
    return jnp.sum(parts, axis=0)


def on_device(
    pressure, saturation_old, soil_type, recharge, ksat_table, alpha_table, porosity_table, residual_table
):
    tables = jnp.stack([ksat_table, alpha_table, porosity_table, residual_table])
    tables = jnp.pad(tables, ((0, 0), (0, 128 - tables.shape[1])))
    tables = jnp.broadcast_to(tables[:, None, :], (4, 8, 128))
    block = (NZ, BX, BY)
    kinds, start = call(
        start_kernel,
        [pressure, saturation_old, soil_type, recharge, tables],
        [shape(*block), shape(2 * NZ, BX, BY)],
        [buffer(*block), buffer(*block), pltpu.VMEM(block, jnp.int32), buffer(BX, BY), pltpu.SemaphoreType.DMA((4,))],
        4 << 20,
        range(4),
    )
    soil_cells = surroundings(kinds)
    rows, to_north, to_south = packed(across(start), soil_cells[1:])
    cells = (rows, shifted(to_north, "gy", 1), shifted(to_south, "gy", -1))
    got = soil_fields([tables, *soil_cells, to_north])
    given, statics = got[:5], got[5:]
    moved = None
    for newton in range(2):
        if newton:
            got = setup([*surroundings(moved), *statics], True)
        else:
            got = setup([*cells, *given], False)
            statics = [*got[20:], *statics]
        (c0, w0, s0, l0, g0, b0, x0, c1, w1, s1, l1, g1, b1, x1, m2, s2, l2, g2, b2, sums) = got[:20]
        weight = summed(sums)
        r0, y0, r1, y1, r2, sums, first = call(
            cycle_kernel,
            [weight, weight, *got[:19]],
            [shape(NZ, 8, SB, LANES)] * 2 + [shape(NZ, 2, SB, LANES)] * 2
            + [shape(NZ, SB, LANES), shape(SB, 128), shape(NZ, BX, BY)],
            work(),
            6 << 20,
        )
        total = summed(sums)
        products, second = call(
            last_kernel,
            [total, weight, c0, w0, s0, l0, g0, b0, c1, w1, s1, l1, g1, m2, s2, l2, g2, r0, y0, r1, y1, r2],
            [shape(1, 128), shape(NZ, BX, BY)],
            work(),
            6 << 20,
        )
        ends = [summed_over_all(products), first, second]
        if newton:
            return call(end_kernel, [pressure, moved, *ends], shape(NZ, BX, BY), [], 4 << 20)
        moved = call(move_kernel, ends, shape(NZ, BX, BY), [], 4 << 20)


def solution(mesh):
    placed = (P(None, "gx", "gy"),) * 3 + (P("gx", "gy"),) + (P(),) * 4
    return jax.shard_map(
        on_device, mesh=mesh, in_specs=placed, out_specs=P(None, "gx", "gy"), check_vma=False
    )
```

```python
import functools

import jax
import jax.numpy as jnp
from jax import lax
from jax.experimental import pallas as pl
from jax.experimental.pallas import tpu as pltpu
from jax.sharding import PartitionSpec as P


NZ = 10
BX = 8
BY = 128
REACH = 4
ROWS = (2 * REACH + 1) * BX
SA = 24
SB = 16
LANES = 128
OWN_S = REACH * BX // 4
OMEGA = 0.8
STORAGE = 0.05
EPSILON = 1e-06
F32 = jnp.float32


def lane_roll(v, shift):
    return pltpu.roll(v, shift % v.shape[1], 1)


def row_roll(v, shift):
    return pltpu.roll(v, shift % v.shape[0], 0)


def lanes_of(rows, width=LANES):
    return lax.broadcasted_iota(jnp.int32, (rows, width), 1)


def rows_of(rows, width=LANES):
    return lax.broadcasted_iota(jnp.int32, (rows, width), 0)


def pair_sum(u, step):
    low = (lanes_of(u.shape[0]) & step) == 0
    return u + jnp.where(low, lane_roll(u, -step), lane_roll(u, step))


def from_south(u, step):
    low = (lanes_of(u.shape[0]) & step) == 0
    return jnp.where(low, u, lane_roll(u, step))


def each_layer(body, together, count=NZ):
    if together == count:
        for k in range(count):
            body(k)
        return

    def step(i, carry):
        for j in range(together):
            body(together * i + j)
        return carry

    lax.fori_loop(0, count // together, step, 0)


def below(k):
    return max(k - 1, 0) if isinstance(k, int) else jnp.maximum(k - 1, 0)


def above(k):
    return min(k + 1, NZ - 1) if isinstance(k, int) else jnp.minimum(k + 1, NZ - 1)


def one_if(condition):
    return jnp.where(condition, 1.0, 0.0).astype(F32)


class Level:
    def __init__(self, storage, west, south, lower, gain, across, along, rows):
        self.storage, self.west, self.south, self.lower, self.gain = storage, west, south, lower, gain
        self.across, self.along, self.rows = across, along, rows
        self.parts = across * along

    def load(self, src, k):
        return [src[k, j, 0 : self.rows, :] for j in range(self.parts)]

    def from_west(self, v):
        n = self.along
        return [v[j - n] if j >= n else row_roll(v[self.parts - n + j], 1) for j in range(self.parts)]

    def from_east(self, v):
        n, m = self.along, self.parts
        return [v[j + n] if j + n < m else row_roll(v[j + n - m], -1) for j in range(m)]

    def from_south(self, v):
        n = self.along
        return [v[j - 1] if j % n else lane_roll(v[j + n - 1], 1) for j in range(self.parts)]

    def from_north(self, v):
        n = self.along
        return [v[j + 1] if (j + 1) % n else lane_roll(v[j + 1 - n], -1) for j in range(self.parts)]

    def diagonals(self, k):
        west, south = self.load(self.west, k), self.load(self.south, k)
        east, north = self.from_east(west), self.from_north(south)
        out = []
        for j in range(self.parts):
            s = slice(0, self.rows)
            total = self.storage[k, j, s, :] + west[j] + east[j] + south[j] + north[j]
            out.append(total + self.lower[k, j, s, :] + self.lower[k + 1, j, s, :])
        return out

    def sweep(self, src, dst, rhs, add, together):
        s = slice(0, self.rows)

        def body(k):
            def at(layer, j):
                return src[layer, j, s, :] if add is None else src[layer, j, s, :] + add(layer, j)

            now = [at(k, j) for j in range(self.parts)]
            west, south = self.load(self.west, k), self.load(self.south, k)
            w, b = self.from_west(now), self.from_south(now)
            e = self.from_east([p * q for p, q in zip(west, now)])
            f = self.from_north([p * q for p, q in zip(south, now)])
            for j in range(self.parts):
                total = rhs[k, j, s, :] + west[j] * w[j] + e[j] + south[j] * b[j] + f[j]
                total = total + self.lower[k, j, s, :] * at(below(k), j) + self.lower[k + 1, j, s, :] * at(above(k), j)
                dst[k, j, s, :] = (1.0 - OMEGA) * now[j] + self.gain[k, j, s, :] * total

        each_layer(body, together)

    def images(self, k, src, gravity=0.0, storage=True):
        s = slice(0, self.rows)
        now = self.load(src, k)
        west, south = self.load(self.west, k), self.load(self.south, k)
        w = [p * (v - n) for p, v, n in zip(west, now, self.from_west(now))]
        b = [p * (v - n) for p, v, n in zip(south, now, self.from_south(now))]
        e, f = self.from_east(w), self.from_north(b)
        out = []
        for j in range(self.parts):
            total = (w[j] - e[j]) + (b[j] - f[j])
            total = total + self.lower[k, j, s, :] * (now[j] - src[below(k), j, s, :] + gravity)
            total = total + self.lower[k + 1, j, s, :] * (now[j] - src[above(k), j, s, :] - gravity)
            if storage:
                total = total + self.storage[k, j, s, :] * now[j]
            out.append(total)
        return out


def restrict_to(fine, src, rhs, coarse, rhs_coarse, first, together):
    def body(k):
        images = fine.images(k, src)
        for j in range(coarse.parts):
            parts = [rhs[k, i, : fine.rows, :] - images[i] for i in range(4 * j, 4 * j + 4)]
            value = (parts[0] + parts[1]) + (parts[2] + parts[3])
            rhs_coarse[k, j, : fine.rows, :] = value
            first[k, j, : fine.rows, :] = coarse.gain[k, j, : fine.rows, :] * value

    each_layer(body, together)


def own_lanes(rows):
    lane = lanes_of(rows)
    return jnp.logical_and(lane >= BY // 4, lane < BY // 4 + BY // 2)


def strip_sums(fields):
    lane = lanes_of(SB, 128)
    out = jnp.zeros((SB, 128), F32)
    for i, field in enumerate(fields):
        for k in range(NZ):
            value = jnp.where(own_lanes(SB), field[k, :SB, :], 0.0)
            out = jnp.where(lane == 16 * i + k, 0.5 * jnp.sum(value, axis=1, keepdims=True), out)
    return out


def restrict_last(middle, src, rhs, rhs_last, together):
    def body(k):
        parts = [rhs[k, i, : middle.rows, :] - image for i, image in enumerate(middle.images(k, src))]
        rhs_last[k] = pair_sum(parts[0] + parts[1], 1)[:SB]

    each_layer(body, together)


def strip_pair(u):
    odd = (rows_of(u.shape[0], u.shape[1]) & 1) == 1
    return jnp.where(odd, row_roll(u, 1), row_roll(u, -1))


def coarsest(rhs, middle, south, lower, gain, sums, weight, out):
    num = sums + strip_pair(sums)
    den = weight + strip_pair(weight)
    mean = num / lane_roll(den, -16)

    lane = lanes_of(SB, 128)
    now = []
    for k in range(NZ):
        value = jnp.sum(jnp.where(lane == k, mean, 0.0), axis=1, keepdims=True)
        now.append(jnp.broadcast_to(value, (SB, LANES)))
    for _ in range(4):
        new = []
        for k in range(NZ):
            v, s = now[k], south[k]
            total = rhs[k] + s * lane_roll(v, 2) + lane_roll(s * v, -2) + middle[k] * strip_pair(v)
            total = total + lower[k] * now[below(k)] + lower[k + 1] * now[above(k)]
            new.append((1.0 - OMEGA) * v + gain[k] * total)
        now = new
    for k in range(NZ):
        out[k] = now[k]


def weights_of(sums):
    a, b, c, d, e, f = [sums[0:1, i : i + 1] for i in range(6)]
    beta2 = a + EPSILON
    beta = jnp.sqrt(beta2)
    kappa = (b + EPSILON) / beta2
    shift = EPSILON * (a - b) / beta2
    norm = kappa * shift - kappa * b + c
    h00 = (a - b) / beta2
    h10 = jnp.sqrt(jnp.maximum(norm, 0.0) / beta2 + EPSILON)
    scale = beta * h10
    scale2 = scale * scale
    h01 = (shift - kappa * b + d) / (beta * scale)
    h11 = (norm + kappa * (d + c - kappa * b) - e) / scale2
    p = kappa * (1.0 - h11) - h01 * h10
    q = h11 - 1.0 - kappa
    last = p * p * a + q * q * c + f + 2.0 * (p * q * b + p * d + q * e)
    h21_2 = jnp.maximum(last, 0.0) / scale2 + EPSILON
    g00 = h00 * h00 + h10 * h10
    g01 = h00 * h01 + h10 * h11
    g11 = h01 * h01 + h11 * h11 + h21_2
    r0 = beta * h00
    r1 = beta * h01
    factor = g01 / g00
    y1 = (r1 - factor * r0) / (g11 - factor * g01)
    y0 = (r0 - g01 * y1) / g00
    return y0 / beta + y1 * kappa / scale, -y1 / scale


def spread(field, left, right, first):
    lane = lanes_of(ROWS, 128)
    begin, end = lane < 32, lane >= 96
    tiles = []
    for odd in (0, 1):
        turn = 32 * odd + (0 if first else 64)
        low, high = (lane_roll(left, -turn), lane_roll(right, turn)) if turn else (left, right)
        tiles.append(jnp.where(begin, low, jnp.where(end, high, lane_roll(field, -32 if odd else 32))))
    return tiles


def put(ext, f, tiles):
    for half in (0, 1):
        ext[f, half, 0:ROWS, :] = tiles[half]
        ext[f, half, ROWS:, :] = tiles[half][0 : 4 * SA - ROWS]


def fetch(ext, f, j):
    return [ext[f, half, pl.ds(j, SA, stride=4), :] for half in (0, 1)]


def unpack_all(ext, cells, left, right, half, together):
    def unpack(f):
        put(ext, f, spread(cells(f), left(f), right(f), True))
        put(ext, f + half, spread(cells(f + half), left(f), right(f), False))

    each_layer(unpack, together, half)


def sorted_lanes(inverse=False):
    a, b = lanes_of(128), rows_of(128)
    if inverse:
        a, b = b, a
    return jnp.where(a == (b & 1) * 64 + (b >> 1), 1.0, 0.0).astype(F32)


def moved_lanes(field, matrix):
    rows = field.reshape(-1, 128)
    out = jnp.dot(rows, matrix, precision=lax.Precision.HIGHEST, preferred_element_type=F32)
    return out.reshape(field.shape)


def start_kernel(head_in, old_in, soil_in, recharge_in, tables, kinds, out, head, old, soil, recharge, sem):
    pairs = [(soil_in, soil), (old_in, old), (recharge_in, recharge), (head_in, head)]
    copies = [pltpu.make_async_copy(a, b, sem.at[i]) for i, (a, b) in enumerate(pairs)]
    for copy in copies:
        copy.start()
    matrix = sorted_lanes()
    copies[0].wait()
    kinds[...] = moved_lanes(soil[...].astype(F32), matrix)
    for copy in copies[1:]:
        copy.wait()
    base = []
    for k in range(NZ):
        porosity, resid = [jnp.take_along_axis(tables[i], soil[k], axis=1) for i in (2, 3)]
        value = porosity * (resid - old[k])
        base.append(value - recharge[...] if k == NZ - 1 else value)
    out[0:NZ] = moved_lanes(head[...], matrix)
    out[NZ:] = moved_lanes(jnp.stack(base), matrix)


def soil_kernel(tables, cells, left, right, unread, *refs):
    (alpha, porous, hw, hs, hl), (ext, con) = refs[:5], refs[5:]
    unpack_all(ext, lambda f: cells[f], lambda f: left[f], lambda f: right[f], NZ // 2, 5)
    table = [jnp.concatenate([tables[i]] * (SA // 8), axis=0) for i in range(4)]

    def look_up(k):
        for j in range(4):
            for odd, tile in enumerate(fetch(ext, k, j)):
                kind = tile.astype(jnp.int32)
                con[k, 2 * j + odd], here, porosity, resid = [
                    jnp.take_along_axis(table[i], kind, axis=1) for i in range(4)
                ]
                alpha[k, 2 * j + odd] = here
                porous[k, 2 * j + odd] = porosity * (1.0 - resid)

    each_layer(look_up, 5)
    row = lax.axis_index("gx") * BX - REACH * BX + 4 * rows_of(SA)
    col = lax.axis_index("gy") * BY - BY // 2 + 2 * lanes_of(SA)
    edge_col = jnp.logical_or(col == 0, col == BY * lax.axis_size("gy"))
    edge_row = jnp.logical_or(row == 0, row == BX * lax.axis_size("gx"))

    def harmonic(k):
        inside = one_if(k != 0)
        for j in range(8):
            here = con[k, j]

            def face(there):
                return here * there / (here + there)

            west = face(con[k, j - 2]) if j > 1 else jnp.where(edge_row, 0.0, face(row_roll(con[k, 6 + j], 1)))
            south = face(con[k, j - 1]) if j % 2 else jnp.where(edge_col, 0.0, face(lane_roll(con[k, j + 1], 1)))
            hw[k, j] = west
            hs[k, j] = south
            hl[k, j] = inside * face(con[below(k), j])

    each_layer(harmonic, 5)


def fetch_kernel(*refs):
    stored, outs, sem = refs[:7], refs[8:15], refs[15]
    copies = [pltpu.make_async_copy(stored[i], outs[i], sem.at[i]) for i in range(7)]
    for copy in copies:
        copy.start()
    for copy in copies:
        copy.wait()


def setup_kernel(second, *refs):
    refs = list(refs)
    one, two, three = refs[:3]
    if second:
        statics, refs = refs[3:10], refs[10:]
    else:
        given, stored, refs = refs[3:8], refs[28:35], refs[8:28] + refs[35:]
        statics, sem = refs[27:29] + given, refs[29]
        copies = [pltpu.make_async_copy(statics[i], stored[i], sem.at[i]) for i in range(7)]
        for copy in copies[2:]:
            copy.start()
    head, base, alpha, porous, hw, hs, hl = statics
    (c0, w0, s0, l0, g0, b0, x0, c1, w1, s1, l1, g1, b1, x1, m2, s2, l2, g2, b2, sums) = refs[:20]
    ext, state, rel, x0a, x1a, c2, w2 = refs[20:27]
    if second:

        def rows(f):
            return jnp.concatenate([part[f] for part in (one, two, three)], axis=0)

        unpack_all(ext, rows, lambda f: rows(NZ + f), lambda f: rows(NZ + NZ // 2 + f), NZ // 2, 5)
    else:
        unpack_all(ext, lambda f: one[f], lambda f: two[f], lambda f: three[f], NZ, 5)

    def cells_of(k):
        for j in range(8):
            if j % 2 == 0:
                tiles = fetch(ext, k, j // 2)
                others = None if second else fetch(ext, NZ + k, j // 2)
            if second:
                moved = tiles[j % 2]
                here = head[k, j] + moved
                local = base[k, j] + STORAGE * moved
            else:
                here, local = tiles[j % 2], others[j % 2]
                head[k, j] = here
                base[k, j] = local
            effective = 1.0 / (1.0 + jnp.exp(-(alpha[k, j] * here)))
            state[k, j] = here
            rel[k, j] = effective * effective
            part = porous[k, j] * effective
            c0[k, j] = STORAGE + part * (alpha[k, j] * (1.0 - effective))
            b0[k, j] = local + part

    each_layer(cells_of, 10)
    if not second:
        for copy in copies[:2]:
            copy.start()

    fine = Level(c0, w0, s0, l0, g0, 4, 2, SA)
    mid = Level(c1, w1, s1, l1, g1, 2, 1, SA)

    def faces(k):
        wet = fine.load(rel, k)
        w, b = fine.from_west(wet), fine.from_south(wet)
        for j in range(8):
            w0[k, j] = hw[k, j] * (wet[j] + w[j])
            s0[k, j] = hs[k, j] * (wet[j] + b[j])
            l0[k, j] = hl[k, j] * (wet[j] + rel[below(k), j])

    each_layer(faces, 10)
    l0[NZ] = jnp.zeros((8, SA, LANES), F32)
    l1[NZ] = jnp.zeros((2, SA, LANES), F32)
    l2[NZ] = jnp.zeros((SB, LANES), F32)

    def residual(k):
        diagonals, images = fine.diagonals(k), fine.images(k, state, 1.0, False)
        for j in range(8):
            gain = OMEGA / diagonals[j]
            value = -(b0[k, j] + images[j])
            g0[k, j] = gain
            b0[k, j] = value
            x0a[k, j] = gain * value

    each_layer(residual, 5)

    def coarsen(k):
        for j in range(2):
            i = 4 * j
            c1[k, j] = (c0[k, i] + c0[k, i + 1]) + (c0[k, i + 2] + c0[k, i + 3])
            l1[k, j] = (l0[k, i] + l0[k, i + 1]) + (l0[k, i + 2] + l0[k, i + 3])
            w1[k, j] = w0[k, i] + w0[k, i + 1]
            s1[k, j] = s0[k, i] + s0[k, i + 2]

    each_layer(coarsen, 10)

    def coarse(k):
        for j, diagonal in enumerate(mid.diagonals(k)):
            g1[k, j] = OMEGA / diagonal
        c2[k] = pair_sum(c1[k, 0, :SB] + c1[k, 1, :SB], 1)
        l2[k] = pair_sum(l1[k, 0, :SB] + l1[k, 1, :SB], 1)
        w2[k] = pair_sum(w1[k, 0], 1)
        s2[k] = from_south(s1[k, 0, :SB] + s1[k, 1, :SB], 1)

    each_layer(coarse, 10)

    def coarse_gain(k):
        west = w2[k]
        east = row_roll(west, -1)[:SB]
        west = west[:SB]
        south = s2[k]
        diag = c2[k] + west + east + south + lane_roll(south, -2) + l2[k] + l2[k + 1]
        g2[k] = OMEGA / diag
        odd = (rows_of(SB) & 1) == 1
        m2[k] = jnp.where(odd, west, east)

    each_layer(coarse_gain, 10)
    fine.sweep(x0a, x0, b0, None, 10)
    restrict_to(fine, x0, b0, mid, b1, x1a, 5)
    mid.sweep(x1a, x1, b1, None, 10)
    restrict_last(mid, x1, b1, b2, 10)
    sums[...] = strip_sums([b2, c2])
    if not second:
        for copy in copies:
            copy.wait()


def finish(fine, mid, last, b0, x0, b1, x1, b2, sums, weight, work0, work1, e2):
    m2, s2, l2, g2 = last
    coarsest(b2, m2, s2, l2, g2, sums, weight, e2)
    mid.sweep(x1, work1[0], b1, lambda k, j: e2[k], 10)
    mid.sweep(work1[0], work1[1], b1, None, 10)
    corrected = work1[1]
    fine.sweep(x0, work0[0], b0, lambda k, j: corrected[k, j // 4, : fine.rows, :], 10)
    fine.sweep(work0[0], work0[1], b0, None, 10)
    return work0[1]


def write_own(dst, k, j, even, odd):
    lane = lanes_of(8, 128)
    s = slice(OWN_S, OWN_S + 8)
    own = jnp.where(lane < 64, lane_roll(even[s], -32), lane_roll(odd[s], 32))
    for half in (0, 1):
        dst[k, 4 * half + j : 4 * half + j + 1, :] = own[half : half + 1]


def cycle_kernel(
    total, weight, c0, w0, s0, l0, g0, b0, x0, c1, w1, s1, l1, g1, b1, x1, m2, s2, l2, g2, b2,
    r0, y0, r1, y1, r2, sums, move,
    f0, f1, h0, h1, e2,
):
    fine = Level(c0, w0, s0, l0, g0, 4, 2, SB)
    mid = Level(c1, w1, s1, l1, g1, 2, 1, SB)
    z = finish(
        fine, mid, (m2, s2, l2, g2), b0, x0, b1, x1, b2, total[...], weight[...], (f0, f1), (h0, h1), e2
    )

    def residual(k):
        images = fine.images(k, z)
        for j in range(8):
            value = b0[k, j, :SB, :] - images[j]
            r0[k, j] = value
            f0[k, j] = g0[k, j, :SB, :] * value
        for j in range(4):
            write_own(move, k, j, z[k, 2 * j], z[k, 2 * j + 1])

    each_layer(residual, 5)
    fine.sweep(f0, y0, r0, None, 10)
    restrict_to(fine, y0, r0, mid, r1, h0, 5)
    mid.sweep(h0, y1, r1, None, 10)
    restrict_last(mid, y1, r1, r2, 10)
    sums[...] = strip_sums([r2])


def last_kernel(
    total, weight, c0, w0, s0, l0, g0, start, c1, w1, s1, l1, g1, m2, s2, l2, g2, b0, x0, b1, x1, b2,
    products, move,
    f0, f1, h0, h1, e2,
):
    fine = Level(c0, w0, s0, l0, g0, 4, 2, SB)
    mid = Level(c1, w1, s1, l1, g1, 2, 1, SB)
    z = finish(
        fine, mid, (m2, s2, l2, g2), b0, x0, b1, x1, b2, total[...], weight[...], (f0, f1), (h0, h1), e2
    )
    row = rows_of(8)
    own = jnp.logical_and(own_lanes(8), row < 2)

    def body(k, sums):
        sums = list(sums)
        images = fine.images(k, z)
        for j in range(4):
            write_own(move, k, j, z[k, 2 * j], z[k, 2 * j + 1])
        for j in range(8):
            image = images[j][OWN_S : OWN_S + 8]
            u = jnp.where(own, start[k, j, OWN_S : OWN_S + 8, :], 0.0)
            t = jnp.where(own, b0[k, j, OWN_S : OWN_S + 8, :], 0.0)
            r = jnp.where(own, t - image, 0.0)
            for i, item in enumerate((u * u, u * t, t * t, u * r, t * r, r * r)):
                sums[i] = sums[i] + item
        return tuple(sums)

    sums = (jnp.zeros((8, LANES), F32),) * 6
    for k in range(NZ):
        sums = body(k, sums)
    lane = lanes_of(1, 128)
    out = jnp.zeros((1, 128), F32)
    for i, item in enumerate(sums):
        value = jnp.sum(jnp.sum(item, axis=0, keepdims=True), axis=1, keepdims=True)
        out = jnp.where(lane == i, value, out)
    products[...] = out


def move_kernel(products, first, second, out):
    one, two = weights_of(products)
    out[...] = one[None] * first[...] + two[None] * second[...]


def end_kernel(head, moved, products, first, second, out):
    one, two = weights_of(products)
    change = moved[...] + one[None] * first[...] + two[None] * second[...]
    out[...] = head[...] + moved_lanes(change, sorted_lanes(True))


VMEM = pl.BlockSpec(memory_space=pltpu.VMEM)
HBM = pl.BlockSpec(memory_space=pltpu.HBM)


def shape(*dims):
    return jax.ShapeDtypeStruct(dims, F32)


def buffer(*dims):
    return pltpu.VMEM(dims, F32)


ANY = pl.BlockSpec(memory_space=pl.ANY)


def call(kernel, args, outs, scratch, limit, in_hbm=(), out_hbm=(), unread=(), cost=None):
    place = [ANY if i in unread else HBM if i in in_hbm else VMEM for i in range(len(args))]
    args = [pltpu.with_memory_space_constraint(a, pltpu.HBM) if i in in_hbm else a for i, a in enumerate(args)]
    many = isinstance(outs, list)
    if many:
        outs = [pltpu.HBM(a.shape, a.dtype) if i in out_hbm else a for i, a in enumerate(outs)]
    spec = [HBM if i in out_hbm else VMEM for i in range(len(outs))] if many else VMEM
    return pl.pallas_call(
        kernel,
        out_shape=outs,
        in_specs=place,
        out_specs=spec,
        scratch_shapes=scratch,
        compiler_params=pltpu.CompilerParams(vmem_limit_bytes=limit),
        cost_estimate=cost,
    )(*args)


FINE = (NZ, 8, SA, LANES)


def soil_fields(inputs):
    cost = pl.CostEstimate(flops=10**7, bytes_accessed=2 * 10**7, transcendentals=0)
    scratch = [buffer(NZ, 2, 4 * SA, 128), buffer(*FINE)]
    return call(soil_kernel, inputs, [shape(*FINE)] * 5, scratch, 6 << 20, unread=(4,), cost=cost)


def fetched(stored, after):
    cost = pl.CostEstimate(flops=10**6, bytes_accessed=15 * 10**6, transcendentals=0)
    sem = [pltpu.SemaphoreType.DMA((7,))]
    return call(fetch_kernel, [*stored, after], [shape(*FINE)] * 7, sem, 1 << 20, range(7), unread=(7,), cost=cost)


def setup(inputs, second):
    fine = shape(*FINE)
    outs = (
        [fine] * 3 + [shape(NZ + 1, 8, SA, LANES)] + [fine] * 3
        + [shape(NZ, 2, SA, LANES)] * 3 + [shape(NZ + 1, 2, SA, LANES)] + [shape(NZ, 2, SA, LANES)] * 3
        + [shape(NZ, SB, LANES)] * 2 + [shape(NZ + 1, SB, LANES)] + [shape(NZ, SB, LANES)] * 2
        + [shape(SB, 128)] + ([] if second else [fine] * 7)
    )
    scratch = (
        [buffer(NZ if second else 2 * NZ, 2, 4 * SA, 128)] + [buffer(*FINE)] * 3
        + [buffer(NZ, 2, SA, LANES), buffer(NZ, SB, LANES), buffer(NZ, SA, LANES)]
        + ([] if second else [buffer(*FINE)] * 2 + [pltpu.SemaphoreType.DMA((7,))])
    )
    kernel = functools.partial(setup_kernel, second)
    return call(kernel, inputs, outs, scratch, (8 if second else 11) << 20, (), () if second else range(20, 27))


def work():
    return [buffer(NZ, 8, SB, LANES)] * 2 + [buffer(NZ, 2, SB, LANES)] * 2 + [buffer(NZ, SB, LANES)]


def shifted(field, axis, by):
    count = lax.axis_size(axis)
    return lax.ppermute(field, axis, [(i, (i + by) % count) for i in range(count)])


def across(field):
    near = jnp.concatenate([shifted(field, "gx", 1), field, shifted(field, "gx", -1)], axis=1)
    return shifted(near, "gx", 3), near, shifted(near, "gx", -3)


def pack_kernel(west, near, east, *refs):
    rows, to_north, to_south = refs[-3:]
    half = rows.shape[0] // 2
    lane = lanes_of(rows.shape[1], 128)

    def quarters(*parts):
        return jnp.where(lane < 64, jnp.where(lane < 32, *parts[:2]), jnp.where(lane < 96, *parts[2:]))

    def pack(f):
        low, high = [
            jnp.concatenate([part[i] for part in (west, near, east)], axis=0) for i in (f, f + half)
        ]
        rows[f] = low
        rows[f + half] = high
        to_north[f] = quarters(lane_roll(low, -32), lane_roll(low, -64), lane_roll(high, 32), high)
        to_south[f] = quarters(lane_roll(high, -64), lane_roll(high, 32), low, lane_roll(low, 96))

    each_layer(pack, 5, half)


def packed(parts, after=()):
    fields, rows = parts[0].shape[0], 3 * parts[0].shape[1]
    outs = [shape(fields, rows, BY)] + [shape(fields // 2, rows, BY)] * 2
    return call(pack_kernel, [*parts, *after], outs, [], 4 << 20, unread=range(3, 3 + len(after)))


def sideways(packs):
    rows, to_north, to_south = packs
    return rows, shifted(to_north, "gy", 1), shifted(to_south, "gy", -1)


def around(field):
    full = jnp.concatenate(sideways(packed((shifted(field, "gx", 1), field, shifted(field, "gx", -1)))), axis=0)
    return shifted(full, "gx", 3), full, shifted(full, "gx", -3)


def summed(field):
    count = lax.axis_size("gy")
    for flip in (1, 2, 6):
        if flip < count:
            field = field + lax.ppermute(field, "gy", [(i, i ^ flip) for i in range(count)])
    return field


def summed_over_all(row):
    axes = ("gx", "gy")
    count = lax.axis_size(axes)
    parts = lax.all_to_all(jnp.broadcast_to(row[None], (count, 1, 128)), axes, 0, 0, tiled=True)
    return jnp.sum(parts, axis=0)


def on_device(
    pressure, saturation_old, soil_type, recharge, ksat_table, alpha_table, porosity_table, residual_table
):
    tables = jnp.stack([ksat_table, alpha_table, porosity_table, residual_table])
    tables = jnp.pad(tables, ((0, 0), (0, 128 - tables.shape[1])))
    tables = jnp.broadcast_to(tables[:, None, :], (4, 8, 128))
    block = (NZ, BX, BY)
    kinds, start = call(
        start_kernel,
        [pressure, saturation_old, soil_type, recharge, tables],
        [shape(*block), shape(2 * NZ, BX, BY)],
        [buffer(*block), buffer(*block), pltpu.VMEM(block, jnp.int32), buffer(BX, BY), pltpu.SemaphoreType.DMA((4,))],
        4 << 20,
        range(4),
    )
    soil_cells = sideways(packed(across(kinds)))
    packs = packed(across(start), soil_cells[1:])
    cells = sideways(packs)
    given = soil_fields([tables, *soil_cells, packs[1]])
    moved = None
    for newton in range(2):
        if newton:
            parts = around(moved)
            got = setup([*parts, *fetched(stored, parts[1])], True)
        else:
            got = setup([*cells, *given], False)
            stored = got[20:]
        (c0, w0, s0, l0, g0, b0, x0, c1, w1, s1, l1, g1, b1, x1, m2, s2, l2, g2, b2, sums) = got[:20]
        weight = summed(sums)
        r0, y0, r1, y1, r2, sums, first = call(
            cycle_kernel,
            [weight, weight, *got[:19]],
            [shape(NZ, 8, SB, LANES)] * 2 + [shape(NZ, 2, SB, LANES)] * 2
            + [shape(NZ, SB, LANES), shape(SB, 128), shape(NZ, BX, BY)],
            work(),
            6 << 20,
        )
        total = summed(sums)
        products, second = call(
            last_kernel,
            [total, weight, c0, w0, s0, l0, g0, b0, c1, w1, s1, l1, g1, m2, s2, l2, g2, r0, y0, r1, y1, r2],
            [shape(1, 128), shape(NZ, BX, BY)],
            work(),
            6 << 20,
        )
        ends = [summed_over_all(products), first, second]
        if newton:
            return call(end_kernel, [pressure, moved, *ends], shape(NZ, BX, BY), [], 4 << 20)
        moved = call(move_kernel, ends, shape(NZ, BX, BY), [], 4 << 20)


def solution(mesh):
    placed = (P(None, "gx", "gy"),) * 3 + (P("gx", "gy"),) + (P(),) * 4
    return jax.shard_map(
        on_device, mesh=mesh, in_specs=placed, out_specs=P(None, "gx", "gy"), check_vma=False
    )
```

```python
import functools

import jax
import jax.numpy as jnp
from jax import lax
from jax.experimental import pallas as pl
from jax.experimental.pallas import tpu as pltpu
from jax.sharding import PartitionSpec as P


NZ = 10
BX = 8
BY = 128
REACH = 4
ROWS = (2 * REACH + 1) * BX
SA = 24
SB = 16
LANES = 128
OWN_S = REACH * BX // 4
OMEGA = 0.8
STORAGE = 0.05
EPSILON = 1e-06
F32 = jnp.float32


def lane_roll(v, shift):
    return pltpu.roll(v, shift % v.shape[1], 1)


def row_roll(v, shift):
    return pltpu.roll(v, shift % v.shape[0], 0)


def lanes_of(rows, width=LANES):
    return lax.broadcasted_iota(jnp.int32, (rows, width), 1)


def rows_of(rows, width=LANES):
    return lax.broadcasted_iota(jnp.int32, (rows, width), 0)


def pair_sum(u, step):
    low = (lanes_of(u.shape[0]) & step) == 0
    return u + jnp.where(low, lane_roll(u, -step), lane_roll(u, step))


def from_south(u, step):
    low = (lanes_of(u.shape[0]) & step) == 0
    return jnp.where(low, u, lane_roll(u, step))


def each_layer(body, together, count=NZ):
    if together == count:
        for k in range(count):
            body(k)
        return

    def step(i, carry):
        for j in range(together):
            body(together * i + j)
        return carry

    lax.fori_loop(0, count // together, step, 0)


def below(k):
    return max(k - 1, 0) if isinstance(k, int) else jnp.maximum(k - 1, 0)


def above(k):
    return min(k + 1, NZ - 1) if isinstance(k, int) else jnp.minimum(k + 1, NZ - 1)


def one_if(condition):
    return jnp.where(condition, 1.0, 0.0).astype(F32)


class Level:
    def __init__(self, storage, west, south, lower, gain, across, along, rows):
        self.storage, self.west, self.south, self.lower, self.gain = storage, west, south, lower, gain
        self.across, self.along, self.rows = across, along, rows
        self.parts = across * along

    def load(self, src, k):
        return [src[k, j, 0 : self.rows, :] for j in range(self.parts)]

    def from_west(self, v):
        n = self.along
        return [v[j - n] if j >= n else row_roll(v[self.parts - n + j], 1) for j in range(self.parts)]

    def from_east(self, v):
        n, m = self.along, self.parts
        return [v[j + n] if j + n < m else row_roll(v[j + n - m], -1) for j in range(m)]

    def from_south(self, v):
        n = self.along
        return [v[j - 1] if j % n else lane_roll(v[j + n - 1], 1) for j in range(self.parts)]

    def from_north(self, v):
        n = self.along
        return [v[j + 1] if (j + 1) % n else lane_roll(v[j + 1 - n], -1) for j in range(self.parts)]

    def diagonals(self, k):
        west, south = self.load(self.west, k), self.load(self.south, k)
        east, north = self.from_east(west), self.from_north(south)
        out = []
        for j in range(self.parts):
            s = slice(0, self.rows)
            total = self.storage[k, j, s, :] + west[j] + east[j] + south[j] + north[j]
            out.append(total + self.lower[k, j, s, :] + self.lower[k + 1, j, s, :])
        return out

    def sweep(self, src, dst, rhs, add, together):
        s = slice(0, self.rows)

        def body(k):
            def at(layer, j):
                return src[layer, j, s, :] if add is None else src[layer, j, s, :] + add(layer, j)

            now = [at(k, j) for j in range(self.parts)]
            west, south = self.load(self.west, k), self.load(self.south, k)
            w, b = self.from_west(now), self.from_south(now)
            e = self.from_east([p * q for p, q in zip(west, now)])
            f = self.from_north([p * q for p, q in zip(south, now)])
            for j in range(self.parts):
                total = rhs[k, j, s, :] + west[j] * w[j] + e[j] + south[j] * b[j] + f[j]
                total = total + self.lower[k, j, s, :] * at(below(k), j) + self.lower[k + 1, j, s, :] * at(above(k), j)
                dst[k, j, s, :] = (1.0 - OMEGA) * now[j] + self.gain[k, j, s, :] * total

        each_layer(body, together)

    def images(self, k, src, gravity=0.0, storage=True):
        s = slice(0, self.rows)
        now = self.load(src, k)
        west, south = self.load(self.west, k), self.load(self.south, k)
        w = [p * (v - n) for p, v, n in zip(west, now, self.from_west(now))]
        b = [p * (v - n) for p, v, n in zip(south, now, self.from_south(now))]
        e, f = self.from_east(w), self.from_north(b)
        out = []
        for j in range(self.parts):
            total = (w[j] - e[j]) + (b[j] - f[j])
            total = total + self.lower[k, j, s, :] * (now[j] - src[below(k), j, s, :] + gravity)
            total = total + self.lower[k + 1, j, s, :] * (now[j] - src[above(k), j, s, :] - gravity)
            if storage:
                total = total + self.storage[k, j, s, :] * now[j]
            out.append(total)
        return out


def restrict_to(fine, src, rhs, coarse, rhs_coarse, first, together):
    def body(k):
        images = fine.images(k, src)
        for j in range(coarse.parts):
            parts = [rhs[k, i, : fine.rows, :] - images[i] for i in range(4 * j, 4 * j + 4)]
            value = (parts[0] + parts[1]) + (parts[2] + parts[3])
            rhs_coarse[k, j, : fine.rows, :] = value
            first[k, j, : fine.rows, :] = coarse.gain[k, j, : fine.rows, :] * value

    each_layer(body, together)


def own_lanes(rows):
    lane = lanes_of(rows)
    return jnp.logical_and(lane >= BY // 4, lane < BY // 4 + BY // 2)


def strip_sums(fields):
    lane = lanes_of(SB, 128)
    out = jnp.zeros((SB, 128), F32)
    for i, field in enumerate(fields):
        for k in range(NZ):
            value = jnp.where(own_lanes(SB), field[k, :SB, :], 0.0)
            out = jnp.where(lane == 16 * i + k, 0.5 * jnp.sum(value, axis=1, keepdims=True), out)
    return out


def restrict_last(middle, src, rhs, rhs_last, together):
    def body(k):
        parts = [rhs[k, i, : middle.rows, :] - image for i, image in enumerate(middle.images(k, src))]
        rhs_last[k] = pair_sum(parts[0] + parts[1], 1)[:SB]

    each_layer(body, together)


def strip_pair(u):
    odd = (rows_of(u.shape[0], u.shape[1]) & 1) == 1
    return jnp.where(odd, row_roll(u, 1), row_roll(u, -1))


def coarsest(rhs, middle, south, lower, gain, sums, weight, out):
    num = sums + strip_pair(sums)
    den = weight + strip_pair(weight)
    mean = num / lane_roll(den, -16)

    lane = lanes_of(SB, 128)
    now = []
    for k in range(NZ):
        value = jnp.sum(jnp.where(lane == k, mean, 0.0), axis=1, keepdims=True)
        now.append(jnp.broadcast_to(value, (SB, LANES)))
    for _ in range(4):
        new = []
        for k in range(NZ):
            v, s = now[k], south[k]
            total = rhs[k] + s * lane_roll(v, 2) + lane_roll(s * v, -2) + middle[k] * strip_pair(v)
            total = total + lower[k] * now[below(k)] + lower[k + 1] * now[above(k)]
            new.append((1.0 - OMEGA) * v + gain[k] * total)
        now = new
    for k in range(NZ):
        out[k] = now[k]


def weights_of(sums):
    a, b, c, d, e, f = [sums[0:1, i : i + 1] for i in range(6)]
    beta2 = a + EPSILON
    beta = jnp.sqrt(beta2)
    kappa = (b + EPSILON) / beta2
    shift = EPSILON * (a - b) / beta2
    norm = kappa * shift - kappa * b + c
    h00 = (a - b) / beta2
    h10 = jnp.sqrt(jnp.maximum(norm, 0.0) / beta2 + EPSILON)
    scale = beta * h10
    scale2 = scale * scale
    h01 = (shift - kappa * b + d) / (beta * scale)
    h11 = (norm + kappa * (d + c - kappa * b) - e) / scale2
    p = kappa * (1.0 - h11) - h01 * h10
    q = h11 - 1.0 - kappa
    last = p * p * a + q * q * c + f + 2.0 * (p * q * b + p * d + q * e)
    h21_2 = jnp.maximum(last, 0.0) / scale2 + EPSILON
    g00 = h00 * h00 + h10 * h10
    g01 = h00 * h01 + h10 * h11
    g11 = h01 * h01 + h11 * h11 + h21_2
    r0 = beta * h00
    r1 = beta * h01
    factor = g01 / g00
    y1 = (r1 - factor * r0) / (g11 - factor * g01)
    y0 = (r0 - g01 * y1) / g00
    return y0 / beta + y1 * kappa / scale, -y1 / scale


def spread(field, left, right, first):
    lane = lanes_of(ROWS, 128)
    begin, end = lane < 32, lane >= 96
    tiles = []
    for odd in (0, 1):
        turn = 32 * odd + (0 if first else 64)
        low, high = (lane_roll(left, -turn), lane_roll(right, turn)) if turn else (left, right)
        tiles.append(jnp.where(begin, low, jnp.where(end, high, lane_roll(field, -32 if odd else 32))))
    return tiles


def put(ext, f, tiles):
    for half in (0, 1):
        ext[f, half, 0:ROWS, :] = tiles[half]
        ext[f, half, ROWS:, :] = tiles[half][0 : 4 * SA - ROWS]


def fetch(ext, f, j):
    return [ext[f, half, pl.ds(j, SA, stride=4), :] for half in (0, 1)]


def unpack_all(ext, cells, left, right, half, together):
    def unpack(f):
        put(ext, f, spread(cells(f), left(f), right(f), True))
        put(ext, f + half, spread(cells(f + half), left(f), right(f), False))

    each_layer(unpack, together, half)


def sorted_lanes(inverse=False):
    a, b = lanes_of(128), rows_of(128)
    if inverse:
        a, b = b, a
    return jnp.where(a == (b & 1) * 64 + (b >> 1), 1.0, 0.0).astype(F32)


def moved_lanes(field, matrix):
    rows = field.reshape(-1, 128)
    out = jnp.dot(rows, matrix, precision=lax.Precision.HIGHEST, preferred_element_type=F32)
    return out.reshape(field.shape)


def start_kernel(head_in, old_in, soil_in, recharge_in, tables, out, head, old, soil, recharge, sem):
    pairs = [(soil_in, soil), (old_in, old), (recharge_in, recharge), (head_in, head)]
    copies = [pltpu.make_async_copy(a, b, sem.at[i]) for i, (a, b) in enumerate(pairs)]
    for copy in copies:
        copy.start()
    matrix = sorted_lanes()
    copies[0].wait()
    out[0:NZ] = moved_lanes(soil[...].astype(F32), matrix)
    for copy in copies[1:]:
        copy.wait()
    base = []
    for k in range(NZ):
        porosity, resid = [jnp.take_along_axis(tables[i], soil[k], axis=1) for i in (2, 3)]
        value = porosity * (resid - old[k])
        base.append(value - recharge[...] if k == NZ - 1 else value)
    out[NZ : 2 * NZ] = moved_lanes(head[...], matrix)
    out[2 * NZ :] = moved_lanes(jnp.stack(base), matrix)


def soil_kernel(tables, cells, left, right, unread, *refs):
    (alpha, porous, hw, hs, hl), (ext, con) = refs[:5], refs[5:]
    unpack_all(ext, lambda f: cells[f], lambda f: left[f], lambda f: right[f], NZ // 2, 5)
    table = [jnp.concatenate([tables[i]] * (SA // 8), axis=0) for i in range(4)]

    def look_up(k):
        for j in range(4):
            for odd, tile in enumerate(fetch(ext, k, j)):
                kind = tile.astype(jnp.int32)
                con[k, 2 * j + odd], here, porosity, resid = [
                    jnp.take_along_axis(table[i], kind, axis=1) for i in range(4)
                ]
                alpha[k, 2 * j + odd] = here
                porous[k, 2 * j + odd] = porosity * (1.0 - resid)

    each_layer(look_up, 5)
    row = lax.axis_index("gx") * BX - REACH * BX + 4 * rows_of(SA)
    col = lax.axis_index("gy") * BY - BY // 2 + 2 * lanes_of(SA)
    edge_col = jnp.logical_or(col == 0, col == BY * lax.axis_size("gy"))
    edge_row = jnp.logical_or(row == 0, row == BX * lax.axis_size("gx"))

    def harmonic(k):
        inside = one_if(k != 0)
        for j in range(8):
            here = con[k, j]

            def face(there):
                return here * there / (here + there)

            west = face(con[k, j - 2]) if j > 1 else jnp.where(edge_row, 0.0, face(row_roll(con[k, 6 + j], 1)))
            south = face(con[k, j - 1]) if j % 2 else jnp.where(edge_col, 0.0, face(lane_roll(con[k, j + 1], 1)))
            hw[k, j] = west
            hs[k, j] = south
            hl[k, j] = inside * face(con[below(k), j])

    each_layer(harmonic, 5)


def fetch_kernel(*refs):
    stored, outs, sem = refs[:7], refs[8:15], refs[15]
    copies = [pltpu.make_async_copy(stored[i], outs[i], sem.at[i]) for i in range(7)]
    for copy in copies:
        copy.start()
    for copy in copies:
        copy.wait()


def setup_kernel(second, *refs):
    refs = list(refs)
    one, two, three = refs[:3]
    if second:
        statics, refs = refs[3:10], refs[10:]
    else:
        given, stored, refs = refs[3:8], refs[28:35], refs[8:28] + refs[35:]
        statics, sem = refs[27:29] + given, refs[29]
        copies = [pltpu.make_async_copy(statics[i], stored[i], sem.at[i]) for i in range(7)]
        for copy in copies[2:]:
            copy.start()
    head, base, alpha, porous, hw, hs, hl = statics
    (c0, w0, s0, l0, g0, b0, x0, c1, w1, s1, l1, g1, b1, x1, m2, s2, l2, g2, b2, sums) = refs[:20]
    ext, state, rel, x0a, x1a, c2, w2 = refs[20:27]
    if second:

        def rows(f):
            return jnp.concatenate([part[f] for part in (one, two, three)], axis=0)

        unpack_all(ext, rows, lambda f: rows(NZ + f), lambda f: rows(NZ + NZ // 2 + f), NZ // 2, 5)
    else:
        unpack_all(ext, lambda f: one[f], lambda f: two[f], lambda f: three[f], NZ, 5)

    def cells_of(k):
        for j in range(8):
            if j % 2 == 0:
                tiles = fetch(ext, k, j // 2)
                others = None if second else fetch(ext, NZ + k, j // 2)
            if second:
                moved = tiles[j % 2]
                here = head[k, j] + moved
                local = base[k, j] + STORAGE * moved
            else:
                here, local = tiles[j % 2], others[j % 2]
                head[k, j] = here
                base[k, j] = local
            effective = 1.0 / (1.0 + jnp.exp(-(alpha[k, j] * here)))
            state[k, j] = here
            rel[k, j] = effective * effective
            part = porous[k, j] * effective
            c0[k, j] = STORAGE + part * (alpha[k, j] * (1.0 - effective))
            b0[k, j] = local + part

    each_layer(cells_of, 10)
    if not second:
        for copy in copies[:2]:
            copy.start()

    fine = Level(c0, w0, s0, l0, g0, 4, 2, SA)
    mid = Level(c1, w1, s1, l1, g1, 2, 1, SA)

    def faces(k):
        wet = fine.load(rel, k)
        w, b = fine.from_west(wet), fine.from_south(wet)
        for j in range(8):
            w0[k, j] = hw[k, j] * (wet[j] + w[j])
            s0[k, j] = hs[k, j] * (wet[j] + b[j])
            l0[k, j] = hl[k, j] * (wet[j] + rel[below(k), j])

    each_layer(faces, 10)
    l0[NZ] = jnp.zeros((8, SA, LANES), F32)
    l1[NZ] = jnp.zeros((2, SA, LANES), F32)
    l2[NZ] = jnp.zeros((SB, LANES), F32)

    def residual(k):
        diagonals, images = fine.diagonals(k), fine.images(k, state, 1.0, False)
        for j in range(8):
            gain = OMEGA / diagonals[j]
            value = -(b0[k, j] + images[j])
            g0[k, j] = gain
            b0[k, j] = value
            x0a[k, j] = gain * value

    each_layer(residual, 5)

    def coarsen(k):
        for j in range(2):
            i = 4 * j
            c1[k, j] = (c0[k, i] + c0[k, i + 1]) + (c0[k, i + 2] + c0[k, i + 3])
            l1[k, j] = (l0[k, i] + l0[k, i + 1]) + (l0[k, i + 2] + l0[k, i + 3])
            w1[k, j] = w0[k, i] + w0[k, i + 1]
            s1[k, j] = s0[k, i] + s0[k, i + 2]

    each_layer(coarsen, 10)

    def coarse(k):
        for j, diagonal in enumerate(mid.diagonals(k)):
            g1[k, j] = OMEGA / diagonal
        c2[k] = pair_sum(c1[k, 0, :SB] + c1[k, 1, :SB], 1)
        l2[k] = pair_sum(l1[k, 0, :SB] + l1[k, 1, :SB], 1)
        w2[k] = pair_sum(w1[k, 0], 1)
        s2[k] = from_south(s1[k, 0, :SB] + s1[k, 1, :SB], 1)

    each_layer(coarse, 10)

    def coarse_gain(k):
        west = w2[k]
        east = row_roll(west, -1)[:SB]
        west = west[:SB]
        south = s2[k]
        diag = c2[k] + west + east + south + lane_roll(south, -2) + l2[k] + l2[k + 1]
        g2[k] = OMEGA / diag
        odd = (rows_of(SB) & 1) == 1
        m2[k] = jnp.where(odd, west, east)

    each_layer(coarse_gain, 10)
    fine.sweep(x0a, x0, b0, None, 10)
    restrict_to(fine, x0, b0, mid, b1, x1a, 5)
    mid.sweep(x1a, x1, b1, None, 10)
    restrict_last(mid, x1, b1, b2, 10)
    sums[...] = strip_sums([b2, c2])
    if not second:
        for copy in copies:
            copy.wait()


def finish(fine, mid, last, b0, x0, b1, x1, b2, sums, weight, work0, work1, e2):
    m2, s2, l2, g2 = last
    coarsest(b2, m2, s2, l2, g2, sums, weight, e2)
    mid.sweep(x1, work1[0], b1, lambda k, j: e2[k], 10)
    mid.sweep(work1[0], work1[1], b1, None, 10)
    corrected = work1[1]
    fine.sweep(x0, work0[0], b0, lambda k, j: corrected[k, j // 4, : fine.rows, :], 10)
    fine.sweep(work0[0], work0[1], b0, None, 10)
    return work0[1]


def write_own(dst, k, j, even, odd):
    lane = lanes_of(8, 128)
    s = slice(OWN_S, OWN_S + 8)
    own = jnp.where(lane < 64, lane_roll(even[s], -32), lane_roll(odd[s], 32))
    for half in (0, 1):
        dst[k, 4 * half + j : 4 * half + j + 1, :] = own[half : half + 1]


def cycle_kernel(
    total, weight, c0, w0, s0, l0, g0, b0, x0, c1, w1, s1, l1, g1, b1, x1, m2, s2, l2, g2, b2,
    r0, y0, r1, y1, r2, sums, move,
    f0, f1, h0, h1, e2,
):
    fine = Level(c0, w0, s0, l0, g0, 4, 2, SB)
    mid = Level(c1, w1, s1, l1, g1, 2, 1, SB)
    z = finish(
        fine, mid, (m2, s2, l2, g2), b0, x0, b1, x1, b2, total[...], weight[...], (f0, f1), (h0, h1), e2
    )

    def residual(k):
        images = fine.images(k, z)
        for j in range(8):
            value = b0[k, j, :SB, :] - images[j]
            r0[k, j] = value
            f0[k, j] = g0[k, j, :SB, :] * value
        for j in range(4):
            write_own(move, k, j, z[k, 2 * j], z[k, 2 * j + 1])

    each_layer(residual, 5)
    fine.sweep(f0, y0, r0, None, 10)
    restrict_to(fine, y0, r0, mid, r1, h0, 5)
    mid.sweep(h0, y1, r1, None, 10)
    restrict_last(mid, y1, r1, r2, 10)
    sums[...] = strip_sums([r2])


def last_kernel(
    total, weight, c0, w0, s0, l0, g0, start, c1, w1, s1, l1, g1, m2, s2, l2, g2, b0, x0, b1, x1, b2,
    products, move,
    f0, f1, h0, h1, e2,
):
    fine = Level(c0, w0, s0, l0, g0, 4, 2, SB)
    mid = Level(c1, w1, s1, l1, g1, 2, 1, SB)
    z = finish(
        fine, mid, (m2, s2, l2, g2), b0, x0, b1, x1, b2, total[...], weight[...], (f0, f1), (h0, h1), e2
    )
    row = rows_of(8)
    own = jnp.logical_and(own_lanes(8), row < 2)

    def body(k, sums):
        sums = list(sums)
        images = fine.images(k, z)
        for j in range(4):
            write_own(move, k, j, z[k, 2 * j], z[k, 2 * j + 1])
        for j in range(8):
            image = images[j][OWN_S : OWN_S + 8]
            u = jnp.where(own, start[k, j, OWN_S : OWN_S + 8, :], 0.0)
            t = jnp.where(own, b0[k, j, OWN_S : OWN_S + 8, :], 0.0)
            r = jnp.where(own, t - image, 0.0)
            for i, item in enumerate((u * u, u * t, t * t, u * r, t * r, r * r)):
                sums[i] = sums[i] + item
        return tuple(sums)

    sums = (jnp.zeros((8, LANES), F32),) * 6
    for k in range(NZ):
        sums = body(k, sums)
    lane = lanes_of(1, 128)
    out = jnp.zeros((1, 128), F32)
    for i, item in enumerate(sums):
        value = jnp.sum(jnp.sum(item, axis=0, keepdims=True), axis=1, keepdims=True)
        out = jnp.where(lane == i, value, out)
    products[...] = out


def move_kernel(products, first, second, out):
    one, two = weights_of(products)
    out[...] = one[None] * first[...] + two[None] * second[...]


def end_kernel(head, moved, products, first, second, out):
    one, two = weights_of(products)
    change = moved[...] + one[None] * first[...] + two[None] * second[...]
    out[...] = head[...] + moved_lanes(change, sorted_lanes(True))


VMEM = pl.BlockSpec(memory_space=pltpu.VMEM)
HBM = pl.BlockSpec(memory_space=pltpu.HBM)


def shape(*dims):
    return jax.ShapeDtypeStruct(dims, F32)


def buffer(*dims):
    return pltpu.VMEM(dims, F32)


ANY = pl.BlockSpec(memory_space=pl.ANY)


def call(kernel, args, outs, scratch, limit, in_hbm=(), out_hbm=(), unread=(), cost=None):
    place = [ANY if i in unread else HBM if i in in_hbm else VMEM for i in range(len(args))]
    args = [pltpu.with_memory_space_constraint(a, pltpu.HBM) if i in in_hbm else a for i, a in enumerate(args)]
    many = isinstance(outs, list)
    if many:
        outs = [pltpu.HBM(a.shape, a.dtype) if i in out_hbm else a for i, a in enumerate(outs)]
    spec = [HBM if i in out_hbm else VMEM for i in range(len(outs))] if many else VMEM
    return pl.pallas_call(
        kernel,
        out_shape=outs,
        in_specs=place,
        out_specs=spec,
        scratch_shapes=scratch,
        compiler_params=pltpu.CompilerParams(vmem_limit_bytes=limit),
        cost_estimate=cost,
    )(*args)


FINE = (NZ, 8, SA, LANES)


def soil_fields(inputs):
    cost = pl.CostEstimate(flops=10**7, bytes_accessed=2 * 10**7, transcendentals=0)
    scratch = [buffer(NZ, 2, 4 * SA, 128), buffer(*FINE)]
    return call(soil_kernel, inputs, [shape(*FINE)] * 5, scratch, 6 << 20, unread=(4,), cost=cost)


def fetched(stored, after):
    cost = pl.CostEstimate(flops=10**6, bytes_accessed=15 * 10**6, transcendentals=0)
    sem = [pltpu.SemaphoreType.DMA((7,))]
    return call(fetch_kernel, [*stored, after], [shape(*FINE)] * 7, sem, 1 << 20, range(7), unread=(7,), cost=cost)


def setup(inputs, second):
    fine = shape(*FINE)
    outs = (
        [fine] * 3 + [shape(NZ + 1, 8, SA, LANES)] + [fine] * 3
        + [shape(NZ, 2, SA, LANES)] * 3 + [shape(NZ + 1, 2, SA, LANES)] + [shape(NZ, 2, SA, LANES)] * 3
        + [shape(NZ, SB, LANES)] * 2 + [shape(NZ + 1, SB, LANES)] + [shape(NZ, SB, LANES)] * 2
        + [shape(SB, 128)] + ([] if second else [fine] * 7)
    )
    scratch = (
        [buffer(NZ if second else 2 * NZ, 2, 4 * SA, 128)] + [buffer(*FINE)] * 3
        + [buffer(NZ, 2, SA, LANES), buffer(NZ, SB, LANES), buffer(NZ, SA, LANES)]
        + ([] if second else [buffer(*FINE)] * 2 + [pltpu.SemaphoreType.DMA((7,))])
    )
    kernel = functools.partial(setup_kernel, second)
    return call(kernel, inputs, outs, scratch, (8 if second else 11) << 20, (), () if second else range(20, 27))


def work():
    return [buffer(NZ, 8, SB, LANES)] * 2 + [buffer(NZ, 2, SB, LANES)] * 2 + [buffer(NZ, SB, LANES)]


def shifted(field, axis, by):
    count = lax.axis_size(axis)
    return lax.ppermute(field, axis, [(i, (i + by) % count) for i in range(count)])


def wider(near):
    return shifted(near, "gx", 3), near, shifted(near, "gx", -3)


def pack_kernel(west, near, east, *refs):
    rows, to_north, to_south = refs[-3:]
    half = rows.shape[0] // 2
    lane = lanes_of(rows.shape[1], 128)

    def quarters(*parts):
        return jnp.where(lane < 64, jnp.where(lane < 32, *parts[:2]), jnp.where(lane < 96, *parts[2:]))

    def pack(f):
        low, high = [
            jnp.concatenate([part[i] for part in (west, near, east)], axis=0) for i in (f, f + half)
        ]
        rows[f] = low
        rows[f + half] = high
        to_north[f] = quarters(lane_roll(low, -32), lane_roll(low, -64), lane_roll(high, 32), high)
        to_south[f] = quarters(lane_roll(high, -64), lane_roll(high, 32), low, lane_roll(low, 96))

    each_layer(pack, 5, half)


def packed(parts, after=()):
    fields, rows = parts[0].shape[0], 3 * parts[0].shape[1]
    outs = [shape(fields, rows, BY)] + [shape(fields // 2, rows, BY)] * 2
    return call(pack_kernel, [*parts, *after], outs, [], 4 << 20, unread=range(3, 3 + len(after)))


def sideways(packs):
    rows, to_north, to_south = packs
    return rows, shifted(to_north, "gy", 1), shifted(to_south, "gy", -1)


def around(field):
    full = jnp.concatenate(sideways(packed((shifted(field, "gx", 1), field, shifted(field, "gx", -1)))), axis=0)
    return shifted(full, "gx", 3), full, shifted(full, "gx", -3)


def summed(field):
    count = lax.axis_size("gy")
    for flip in (1, 2, 6):
        if flip < count:
            field = field + lax.ppermute(field, "gy", [(i, i ^ flip) for i in range(count)])
    return field


def summed_over_all(row):
    axes = ("gx", "gy")
    count = lax.axis_size(axes)
    parts = lax.all_to_all(jnp.broadcast_to(row[None], (count, 1, 128)), axes, 0, 0, tiled=True)
    return jnp.sum(parts, axis=0)


def on_device(
    pressure, saturation_old, soil_type, recharge, ksat_table, alpha_table, porosity_table, residual_table
):
    tables = jnp.stack([ksat_table, alpha_table, porosity_table, residual_table])
    tables = jnp.pad(tables, ((0, 0), (0, 128 - tables.shape[1])))
    tables = jnp.broadcast_to(tables[:, None, :], (4, 8, 128))
    block = (NZ, BX, BY)
    start = call(
        start_kernel,
        [pressure, saturation_old, soil_type, recharge, tables],
        shape(3 * NZ, BX, BY),
        [buffer(*block), buffer(*block), pltpu.VMEM(block, jnp.int32), buffer(BX, BY), pltpu.SemaphoreType.DMA((4,))],
        4 << 20,
        range(4),
    )
    near = jnp.concatenate([shifted(start, "gx", 1), start, shifted(start, "gx", -1)], axis=1)
    soil_cells = sideways(packed(wider(near[:NZ])))
    packs = packed(wider(near[NZ:]), soil_cells[1:])
    cells = sideways(packs)
    given = soil_fields([tables, *soil_cells, packs[1]])
    moved = None
    for newton in range(2):
        if newton:
            parts = around(moved)
            got = setup([*parts, *fetched(stored, parts[1])], True)
        else:
            got = setup([*cells, *given], False)
            stored = got[20:]
        (c0, w0, s0, l0, g0, b0, x0, c1, w1, s1, l1, g1, b1, x1, m2, s2, l2, g2, b2, sums) = got[:20]
        weight = summed(sums)
        r0, y0, r1, y1, r2, sums, first = call(
            cycle_kernel,
            [weight, weight, *got[:19]],
            [shape(NZ, 8, SB, LANES)] * 2 + [shape(NZ, 2, SB, LANES)] * 2
            + [shape(NZ, SB, LANES), shape(SB, 128), shape(NZ, BX, BY)],
            work(),
            6 << 20,
        )
        total = summed(sums)
        products, second = call(
            last_kernel,
            [total, weight, c0, w0, s0, l0, g0, b0, c1, w1, s1, l1, g1, m2, s2, l2, g2, r0, y0, r1, y1, r2],
            [shape(1, 128), shape(NZ, BX, BY)],
            work(),
            6 << 20,
        )
        ends = [summed_over_all(products), first, second]
        if newton:
            return call(end_kernel, [pressure, moved, *ends], shape(NZ, BX, BY), [], 4 << 20)
        moved = call(move_kernel, ends, shape(NZ, BX, BY), [], 4 << 20)


def solution(mesh):
    placed = (P(None, "gx", "gy"),) * 3 + (P("gx", "gy"),) + (P(),) * 4
    return jax.shard_map(
        on_device, mesh=mesh, in_specs=placed, out_specs=P(None, "gx", "gy"), check_vma=False
    )
```

```python
import functools

import jax
import jax.numpy as jnp
from jax import lax
from jax.experimental import pallas as pl
from jax.experimental.pallas import tpu as pltpu
from jax.sharding import PartitionSpec as P


NZ = 10
BX = 8
BY = 128
REACH = 4
ROWS = (2 * REACH + 1) * BX
SA = 24
SB = 16
LANES = 128
OWN_S = REACH * BX // 4
OMEGA = 0.8
STORAGE = 0.05
EPSILON = 1e-06
F32 = jnp.float32


def lane_roll(v, shift):
    return pltpu.roll(v, shift % v.shape[1], 1)


def row_roll(v, shift):
    return pltpu.roll(v, shift % v.shape[0], 0)


def lanes_of(rows, width=LANES):
    return lax.broadcasted_iota(jnp.int32, (rows, width), 1)


def rows_of(rows, width=LANES):
    return lax.broadcasted_iota(jnp.int32, (rows, width), 0)


def pair_sum(u, step):
    low = (lanes_of(u.shape[0]) & step) == 0
    return u + jnp.where(low, lane_roll(u, -step), lane_roll(u, step))


def from_south(u, step):
    low = (lanes_of(u.shape[0]) & step) == 0
    return jnp.where(low, u, lane_roll(u, step))


def each_layer(body, together, count=NZ):
    if together == count:
        for k in range(count):
            body(k)
        return

    def step(i, carry):
        for j in range(together):
            body(together * i + j)
        return carry

    lax.fori_loop(0, count // together, step, 0)


def below(k):
    return max(k - 1, 0) if isinstance(k, int) else jnp.maximum(k - 1, 0)


def above(k):
    return min(k + 1, NZ - 1) if isinstance(k, int) else jnp.minimum(k + 1, NZ - 1)


def one_if(condition):
    return jnp.where(condition, 1.0, 0.0).astype(F32)


class Level:
    def __init__(self, storage, west, south, lower, gain, across, along, rows):
        self.storage, self.west, self.south, self.lower, self.gain = storage, west, south, lower, gain
        self.across, self.along, self.rows = across, along, rows
        self.parts = across * along

    def load(self, src, k):
        return [src[k, j, 0 : self.rows, :] for j in range(self.parts)]

    def from_west(self, v):
        n = self.along
        return [v[j - n] if j >= n else row_roll(v[self.parts - n + j], 1) for j in range(self.parts)]

    def from_east(self, v):
        n, m = self.along, self.parts
        return [v[j + n] if j + n < m else row_roll(v[j + n - m], -1) for j in range(m)]

    def from_south(self, v):
        n = self.along
        return [v[j - 1] if j % n else lane_roll(v[j + n - 1], 1) for j in range(self.parts)]

    def from_north(self, v):
        n = self.along
        return [v[j + 1] if (j + 1) % n else lane_roll(v[j + 1 - n], -1) for j in range(self.parts)]

    def diagonals(self, k):
        west, south = self.load(self.west, k), self.load(self.south, k)
        east, north = self.from_east(west), self.from_north(south)
        out = []
        for j in range(self.parts):
            s = slice(0, self.rows)
            total = self.storage[k, j, s, :] + west[j] + east[j] + south[j] + north[j]
            out.append(total + self.lower[k, j, s, :] + self.lower[k + 1, j, s, :])
        return out

    def sweep(self, src, dst, rhs, add, together):
        s = slice(0, self.rows)

        def body(k):
            def at(layer, j):
                return src[layer, j, s, :] if add is None else src[layer, j, s, :] + add(layer, j)

            now = [at(k, j) for j in range(self.parts)]
            west, south = self.load(self.west, k), self.load(self.south, k)
            w, b = self.from_west(now), self.from_south(now)
            e = self.from_east([p * q for p, q in zip(west, now)])
            f = self.from_north([p * q for p, q in zip(south, now)])
            for j in range(self.parts):
                total = rhs[k, j, s, :] + west[j] * w[j] + e[j] + south[j] * b[j] + f[j]
                total = total + self.lower[k, j, s, :] * at(below(k), j) + self.lower[k + 1, j, s, :] * at(above(k), j)
                dst[k, j, s, :] = (1.0 - OMEGA) * now[j] + self.gain[k, j, s, :] * total

        each_layer(body, together)

    def images(self, k, src, gravity=0.0, storage=True):
        s = slice(0, self.rows)
        now = self.load(src, k)
        west, south = self.load(self.west, k), self.load(self.south, k)
        w = [p * (v - n) for p, v, n in zip(west, now, self.from_west(now))]
        b = [p * (v - n) for p, v, n in zip(south, now, self.from_south(now))]
        e, f = self.from_east(w), self.from_north(b)
        out = []
        for j in range(self.parts):
            total = (w[j] - e[j]) + (b[j] - f[j])
            total = total + self.lower[k, j, s, :] * (now[j] - src[below(k), j, s, :] + gravity)
            total = total + self.lower[k + 1, j, s, :] * (now[j] - src[above(k), j, s, :] - gravity)
            if storage:
                total = total + self.storage[k, j, s, :] * now[j]
            out.append(total)
        return out


def restrict_to(fine, src, rhs, coarse, rhs_coarse, first, together):
    def body(k):
        images = fine.images(k, src)
        for j in range(coarse.parts):
            parts = [rhs[k, i, : fine.rows, :] - images[i] for i in range(4 * j, 4 * j + 4)]
            value = (parts[0] + parts[1]) + (parts[2] + parts[3])
            rhs_coarse[k, j, : fine.rows, :] = value
            first[k, j, : fine.rows, :] = coarse.gain[k, j, : fine.rows, :] * value

    each_layer(body, together)


def own_lanes(rows):
    lane = lanes_of(rows)
    return jnp.logical_and(lane >= BY // 4, lane < BY // 4 + BY // 2)


def strip_sums(fields):
    lane = lanes_of(SB, 128)
    out = jnp.zeros((SB, 128), F32)
    for i, field in enumerate(fields):
        for k in range(NZ):
            value = jnp.where(own_lanes(SB), field[k, :SB, :], 0.0)
            out = jnp.where(lane == 16 * i + k, 0.5 * jnp.sum(value, axis=1, keepdims=True), out)
    return out


def restrict_last(middle, src, rhs, rhs_last, together):
    def body(k):
        parts = [rhs[k, i, : middle.rows, :] - image for i, image in enumerate(middle.images(k, src))]
        rhs_last[k] = pair_sum(parts[0] + parts[1], 1)[:SB]

    each_layer(body, together)


def strip_pair(u):
    odd = (rows_of(u.shape[0], u.shape[1]) & 1) == 1
    return jnp.where(odd, row_roll(u, 1), row_roll(u, -1))


def coarsest(rhs, middle, south, lower, gain, sums, weight, out):
    num = sums + strip_pair(sums)
    den = weight + strip_pair(weight)
    mean = num / lane_roll(den, -16)

    lane = lanes_of(SB, 128)
    now = []
    for k in range(NZ):
        value = jnp.sum(jnp.where(lane == k, mean, 0.0), axis=1, keepdims=True)
        now.append(jnp.broadcast_to(value, (SB, LANES)))
    for _ in range(4):
        new = []
        for k in range(NZ):
            v, s = now[k], south[k]
            total = rhs[k] + s * lane_roll(v, 2) + lane_roll(s * v, -2) + middle[k] * strip_pair(v)
            total = total + lower[k] * now[below(k)] + lower[k + 1] * now[above(k)]
            new.append((1.0 - OMEGA) * v + gain[k] * total)
        now = new
    for k in range(NZ):
        out[k] = now[k]


def weights_of(sums):
    a, b, c, d, e, f = [sums[0:1, i : i + 1] for i in range(6)]
    beta2 = a + EPSILON
    beta = jnp.sqrt(beta2)
    kappa = (b + EPSILON) / beta2
    shift = EPSILON * (a - b) / beta2
    norm = kappa * shift - kappa * b + c
    h00 = (a - b) / beta2
    h10 = jnp.sqrt(jnp.maximum(norm, 0.0) / beta2 + EPSILON)
    scale = beta * h10
    scale2 = scale * scale
    h01 = (shift - kappa * b + d) / (beta * scale)
    h11 = (norm + kappa * (d + c - kappa * b) - e) / scale2
    p = kappa * (1.0 - h11) - h01 * h10
    q = h11 - 1.0 - kappa
    last = p * p * a + q * q * c + f + 2.0 * (p * q * b + p * d + q * e)
    h21_2 = jnp.maximum(last, 0.0) / scale2 + EPSILON
    g00 = h00 * h00 + h10 * h10
    g01 = h00 * h01 + h10 * h11
    g11 = h01 * h01 + h11 * h11 + h21_2
    r0 = beta * h00
    r1 = beta * h01
    factor = g01 / g00
    y1 = (r1 - factor * r0) / (g11 - factor * g01)
    y0 = (r0 - g01 * y1) / g00
    return y0 / beta + y1 * kappa / scale, -y1 / scale


def spread(field, left, right, first):
    lane = lanes_of(ROWS, 128)
    begin, end = lane < 32, lane >= 96
    tiles = []
    for odd in (0, 1):
        turn = 32 * odd + (0 if first else 64)
        low, high = (lane_roll(left, -turn), lane_roll(right, turn)) if turn else (left, right)
        tiles.append(jnp.where(begin, low, jnp.where(end, high, lane_roll(field, -32 if odd else 32))))
    return tiles


def put(ext, f, tiles):
    for half in (0, 1):
        ext[f, half, 0:ROWS, :] = tiles[half]
        ext[f, half, ROWS:, :] = tiles[half][0 : 4 * SA - ROWS]


def fetch(ext, f, j):
    return [ext[f, half, pl.ds(j, SA, stride=4), :] for half in (0, 1)]


def unpack_all(ext, cells, left, right, half, together):
    def unpack(f):
        put(ext, f, spread(cells(f), left(f), right(f), True))
        put(ext, f + half, spread(cells(f + half), left(f), right(f), False))

    each_layer(unpack, together, half)


def sorted_lanes(inverse=False):
    a, b = lanes_of(128), rows_of(128)
    if inverse:
        a, b = b, a
    return jnp.where(a == (b & 1) * 64 + (b >> 1), 1.0, 0.0).astype(F32)


def moved_lanes(field, matrix):
    rows = field.reshape(-1, 128)
    out = jnp.dot(rows, matrix, precision=lax.Precision.HIGHEST, preferred_element_type=F32)
    return out.reshape(field.shape)


def start_kernel(head_in, old_in, soil_in, recharge_in, tables, out, head, old, soil, recharge, sem):
    pairs = [(soil_in, soil), (old_in, old), (recharge_in, recharge), (head_in, head)]
    copies = [pltpu.make_async_copy(a, b, sem.at[i]) for i, (a, b) in enumerate(pairs)]
    for copy in copies:
        copy.start()
    matrix = sorted_lanes()
    copies[0].wait()
    out[0:NZ] = moved_lanes(soil[...].astype(F32), matrix)
    for copy in copies[1:]:
        copy.wait()
    base = []
    for k in range(NZ):
        porosity, resid = [jnp.take_along_axis(tables[i], soil[k], axis=1) for i in (2, 3)]
        value = porosity * (resid - old[k])
        base.append(value - recharge[...] if k == NZ - 1 else value)
    out[NZ : 2 * NZ] = moved_lanes(head[...], matrix)
    out[2 * NZ :] = moved_lanes(jnp.stack(base), matrix)


def soil_kernel(tables, cells, left, right, unread, *refs):
    (alpha, porous, hw, hs, hl), (ext, con) = refs[:5], refs[5:]
    unpack_all(ext, lambda f: cells[f], lambda f: left[f], lambda f: right[f], NZ // 2, 5)
    table = [jnp.concatenate([tables[i]] * (SA // 8), axis=0) for i in range(4)]

    def look_up(k):
        for j in range(4):
            for odd, tile in enumerate(fetch(ext, k, j)):
                kind = tile.astype(jnp.int32)
                con[k, 2 * j + odd], here, porosity, resid = [
                    jnp.take_along_axis(table[i], kind, axis=1) for i in range(4)
                ]
                alpha[k, 2 * j + odd] = here
                porous[k, 2 * j + odd] = porosity * (1.0 - resid)

    each_layer(look_up, 5)
    row = lax.axis_index("gx") * BX - REACH * BX + 4 * rows_of(SA)
    col = lax.axis_index("gy") * BY - BY // 2 + 2 * lanes_of(SA)
    edge_col = jnp.logical_or(col == 0, col == BY * lax.axis_size("gy"))
    edge_row = jnp.logical_or(row == 0, row == BX * lax.axis_size("gx"))

    def harmonic(k):
        inside = one_if(k != 0)
        for j in range(8):
            here = con[k, j]

            def face(there):
                return here * there / (here + there)

            west = face(con[k, j - 2]) if j > 1 else jnp.where(edge_row, 0.0, face(row_roll(con[k, 6 + j], 1)))
            south = face(con[k, j - 1]) if j % 2 else jnp.where(edge_col, 0.0, face(lane_roll(con[k, j + 1], 1)))
            hw[k, j] = west
            hs[k, j] = south
            hl[k, j] = inside * face(con[below(k), j])

    each_layer(harmonic, 5)


def fetch_kernel(*refs):
    stored, outs, sem = refs[:7], refs[8:15], refs[15]
    copies = [pltpu.make_async_copy(stored[i], outs[i], sem.at[i]) for i in range(7)]
    for copy in copies:
        copy.start()
    for copy in copies:
        copy.wait()


def setup_kernel(second, *refs):
    refs = list(refs)
    one, two, three = refs[:3]
    if second:
        statics, refs = refs[3:10], refs[10:]
    else:
        given, stored, refs = refs[3:8], refs[28:35], refs[8:28] + refs[35:]
        statics, sem = refs[27:29] + given, refs[29]
        copies = [pltpu.make_async_copy(statics[i], stored[i], sem.at[i]) for i in range(7)]
        for copy in copies[2:]:
            copy.start()
    head, base, alpha, porous, hw, hs, hl = statics
    (c0, w0, s0, l0, g0, b0, x0, c1, w1, s1, l1, g1, b1, x1, m2, s2, l2, g2, b2, sums) = refs[:20]
    ext, state, rel, x0a, x1a, c2, w2 = refs[20:27]
    if second:

        def rows(f):
            return jnp.concatenate([part[f] for part in (one, two, three)], axis=0)

        unpack_all(ext, rows, lambda f: rows(NZ + f), lambda f: rows(NZ + NZ // 2 + f), NZ // 2, 5)
    else:
        unpack_all(ext, lambda f: one[f], lambda f: two[f], lambda f: three[f], NZ, 5)

    def cells_of(k):
        for j in range(8):
            if j % 2 == 0:
                tiles = fetch(ext, k, j // 2)
                others = None if second else fetch(ext, NZ + k, j // 2)
            if second:
                moved = tiles[j % 2]
                here = head[k, j] + moved
                local = base[k, j] + STORAGE * moved
            else:
                here, local = tiles[j % 2], others[j % 2]
                head[k, j] = here
                base[k, j] = local
            effective = 1.0 / (1.0 + jnp.exp(-(alpha[k, j] * here)))
            state[k, j] = here
            rel[k, j] = effective * effective
            part = porous[k, j] * effective
            c0[k, j] = STORAGE + part * (alpha[k, j] * (1.0 - effective))
            b0[k, j] = local + part

    each_layer(cells_of, 10)
    if not second:
        for copy in copies[:2]:
            copy.start()

    fine = Level(c0, w0, s0, l0, g0, 4, 2, SA)
    mid = Level(c1, w1, s1, l1, g1, 2, 1, SA)

    def faces(k):
        wet = fine.load(rel, k)
        w, b = fine.from_west(wet), fine.from_south(wet)
        for j in range(8):
            w0[k, j] = hw[k, j] * (wet[j] + w[j])
            s0[k, j] = hs[k, j] * (wet[j] + b[j])
            l0[k, j] = hl[k, j] * (wet[j] + rel[below(k), j])

    each_layer(faces, 10)
    l0[NZ] = jnp.zeros((8, SA, LANES), F32)
    l1[NZ] = jnp.zeros((2, SA, LANES), F32)
    l2[NZ] = jnp.zeros((SB, LANES), F32)

    def residual(k):
        diagonals, images = fine.diagonals(k), fine.images(k, state, 1.0, False)
        for j in range(8):
            gain = OMEGA / diagonals[j]
            value = -(b0[k, j] + images[j])
            g0[k, j] = gain
            b0[k, j] = value
            x0a[k, j] = gain * value

    each_layer(residual, 5)

    def coarsen(k):
        for j in range(2):
            i = 4 * j
            c1[k, j] = (c0[k, i] + c0[k, i + 1]) + (c0[k, i + 2] + c0[k, i + 3])
            l1[k, j] = (l0[k, i] + l0[k, i + 1]) + (l0[k, i + 2] + l0[k, i + 3])
            w1[k, j] = w0[k, i] + w0[k, i + 1]
            s1[k, j] = s0[k, i] + s0[k, i + 2]

    each_layer(coarsen, 10)

    def coarse(k):
        for j, diagonal in enumerate(mid.diagonals(k)):
            g1[k, j] = OMEGA / diagonal
        c2[k] = pair_sum(c1[k, 0, :SB] + c1[k, 1, :SB], 1)
        l2[k] = pair_sum(l1[k, 0, :SB] + l1[k, 1, :SB], 1)
        w2[k] = pair_sum(w1[k, 0], 1)
        s2[k] = from_south(s1[k, 0, :SB] + s1[k, 1, :SB], 1)

    each_layer(coarse, 10)

    def coarse_gain(k):
        west = w2[k]
        east = row_roll(west, -1)[:SB]
        west = west[:SB]
        south = s2[k]
        diag = c2[k] + west + east + south + lane_roll(south, -2) + l2[k] + l2[k + 1]
        g2[k] = OMEGA / diag
        odd = (rows_of(SB) & 1) == 1
        m2[k] = jnp.where(odd, west, east)

    each_layer(coarse_gain, 10)
    fine.sweep(x0a, x0, b0, None, 10)
    restrict_to(fine, x0, b0, mid, b1, x1a, 5)
    mid.sweep(x1a, x1, b1, None, 10)
    restrict_last(mid, x1, b1, b2, 10)
    sums[...] = strip_sums([b2, c2])
    if not second:
        for copy in copies:
            copy.wait()


def finish(fine, mid, last, b0, x0, b1, x1, b2, sums, weight, work0, work1, e2):
    m2, s2, l2, g2 = last
    coarsest(b2, m2, s2, l2, g2, sums, weight, e2)
    mid.sweep(x1, work1[0], b1, lambda k, j: e2[k], 10)
    mid.sweep(work1[0], work1[1], b1, None, 10)
    corrected = work1[1]
    fine.sweep(x0, work0[0], b0, lambda k, j: corrected[k, j // 4, : fine.rows, :], 10)
    fine.sweep(work0[0], work0[1], b0, None, 10)
    return work0[1]


def write_own(dst, k, j, even, odd):
    lane = lanes_of(8, 128)
    s = slice(OWN_S, OWN_S + 8)
    own = jnp.where(lane < 64, lane_roll(even[s], -32), lane_roll(odd[s], 32))
    for half in (0, 1):
        dst[k, 4 * half + j : 4 * half + j + 1, :] = own[half : half + 1]


def cycle_kernel(
    total, weight, c0, w0, s0, l0, g0, b0, x0, c1, w1, s1, l1, g1, b1, x1, m2, s2, l2, g2, b2,
    r0, y0, r1, y1, r2, sums, move,
    f0, f1, h0, h1, e2,
):
    fine = Level(c0, w0, s0, l0, g0, 4, 2, SB)
    mid = Level(c1, w1, s1, l1, g1, 2, 1, SB)
    z = finish(
        fine, mid, (m2, s2, l2, g2), b0, x0, b1, x1, b2, total[...], weight[...], (f0, f1), (h0, h1), e2
    )

    def residual(k):
        images = fine.images(k, z)
        for j in range(8):
            value = b0[k, j, :SB, :] - images[j]
            r0[k, j] = value
            f0[k, j] = g0[k, j, :SB, :] * value
        for j in range(4):
            write_own(move, k, j, z[k, 2 * j], z[k, 2 * j + 1])

    each_layer(residual, 5)
    fine.sweep(f0, y0, r0, None, 10)
    restrict_to(fine, y0, r0, mid, r1, h0, 5)
    mid.sweep(h0, y1, r1, None, 10)
    restrict_last(mid, y1, r1, r2, 10)
    sums[...] = strip_sums([r2])


def last_kernel(
    total, weight, c0, w0, s0, l0, g0, start, c1, w1, s1, l1, g1, m2, s2, l2, g2, b0, x0, b1, x1, b2,
    products, move,
    f0, f1, h0, h1, e2,
):
    fine = Level(c0, w0, s0, l0, g0, 4, 2, SB)
    mid = Level(c1, w1, s1, l1, g1, 2, 1, SB)
    z = finish(
        fine, mid, (m2, s2, l2, g2), b0, x0, b1, x1, b2, total[...], weight[...], (f0, f1), (h0, h1), e2
    )
    row = rows_of(8)
    own = jnp.logical_and(own_lanes(8), row < 2)

    def body(k, sums):
        sums = list(sums)
        images = fine.images(k, z)
        for j in range(4):
            write_own(move, k, j, z[k, 2 * j], z[k, 2 * j + 1])
        for j in range(8):
            image = images[j][OWN_S : OWN_S + 8]
            u = jnp.where(own, start[k, j, OWN_S : OWN_S + 8, :], 0.0)
            t = jnp.where(own, b0[k, j, OWN_S : OWN_S + 8, :], 0.0)
            r = jnp.where(own, t - image, 0.0)
            for i, item in enumerate((u * u, u * t, t * t, u * r, t * r, r * r)):
                sums[i] = sums[i] + item
        return tuple(sums)

    sums = (jnp.zeros((8, LANES), F32),) * 6
    for k in range(NZ):
        sums = body(k, sums)
    lane = lanes_of(1, 128)
    out = jnp.zeros((1, 128), F32)
    for i, item in enumerate(sums):
        value = jnp.sum(jnp.sum(item, axis=0, keepdims=True), axis=1, keepdims=True)
        out = jnp.where(lane == i, value, out)
    products[...] = out


def move_kernel(products, first, second, out):
    one, two = weights_of(products)
    out[...] = one[None] * first[...] + two[None] * second[...]


def end_kernel(head, moved, products, first, second, out):
    one, two = weights_of(products)
    change = moved[...] + one[None] * first[...] + two[None] * second[...]
    out[...] = head[...] + moved_lanes(change, sorted_lanes(True))


VMEM = pl.BlockSpec(memory_space=pltpu.VMEM)
HBM = pl.BlockSpec(memory_space=pltpu.HBM)


def shape(*dims):
    return jax.ShapeDtypeStruct(dims, F32)


def buffer(*dims):
    return pltpu.VMEM(dims, F32)


ANY = pl.BlockSpec(memory_space=pl.ANY)


def call(kernel, args, outs, scratch, limit, in_hbm=(), out_hbm=(), unread=(), cost=None):
    place = [ANY if i in unread else HBM if i in in_hbm else VMEM for i in range(len(args))]
    args = [pltpu.with_memory_space_constraint(a, pltpu.HBM) if i in in_hbm else a for i, a in enumerate(args)]
    many = isinstance(outs, list)
    if many:
        outs = [pltpu.HBM(a.shape, a.dtype) if i in out_hbm else a for i, a in enumerate(outs)]
    spec = [HBM if i in out_hbm else VMEM for i in range(len(outs))] if many else VMEM
    return pl.pallas_call(
        kernel,
        out_shape=outs,
        in_specs=place,
        out_specs=spec,
        scratch_shapes=scratch,
        compiler_params=pltpu.CompilerParams(vmem_limit_bytes=limit),
        cost_estimate=cost,
    )(*args)


FINE = (NZ, 8, SA, LANES)


def soil_fields(inputs):
    cost = pl.CostEstimate(flops=10**7, bytes_accessed=2 * 10**7, transcendentals=0)
    scratch = [buffer(NZ, 2, 4 * SA, 128), buffer(*FINE)]
    return call(soil_kernel, inputs, [shape(*FINE)] * 5, scratch, 6 << 20, unread=(4,), cost=cost)


def fetched(stored, after):
    cost = pl.CostEstimate(flops=10**6, bytes_accessed=15 * 10**6, transcendentals=0)
    sem = [pltpu.SemaphoreType.DMA((7,))]
    return call(fetch_kernel, [*stored, after], [shape(*FINE)] * 7, sem, 1 << 20, range(7), unread=(7,), cost=cost)


def setup(inputs, second):
    fine = shape(*FINE)
    outs = (
        [fine] * 3 + [shape(NZ + 1, 8, SA, LANES)] + [fine] * 3
        + [shape(NZ, 2, SA, LANES)] * 3 + [shape(NZ + 1, 2, SA, LANES)] + [shape(NZ, 2, SA, LANES)] * 3
        + [shape(NZ, SB, LANES)] * 2 + [shape(NZ + 1, SB, LANES)] + [shape(NZ, SB, LANES)] * 2
        + [shape(SB, 128)] + ([] if second else [fine] * 7)
    )
    scratch = (
        [buffer(NZ if second else 2 * NZ, 2, 4 * SA, 128)] + [buffer(*FINE)] * 3
        + [buffer(NZ, 2, SA, LANES), buffer(NZ, SB, LANES), buffer(NZ, SA, LANES)]
        + ([] if second else [buffer(*FINE)] * 2 + [pltpu.SemaphoreType.DMA((7,))])
    )
    kernel = functools.partial(setup_kernel, second)
    return call(kernel, inputs, outs, scratch, (8 if second else 11) << 20, (), () if second else range(20, 27))


def work():
    return [buffer(NZ, 8, SB, LANES)] * 2 + [buffer(NZ, 2, SB, LANES)] * 2 + [buffer(NZ, SB, LANES)]


def shifted(field, axis, by):
    count = lax.axis_size(axis)
    return lax.ppermute(field, axis, [(i, (i + by) % count) for i in range(count)])


def wider(near):
    return shifted(near, "gx", 3), near, shifted(near, "gx", -3)


def pack_kernel(west, near, east, *refs):
    rows, to_north, to_south = refs[-3:]
    half = rows.shape[0] // 2
    lane = lanes_of(rows.shape[1], 128)

    def quarters(*parts):
        return jnp.where(lane < 64, jnp.where(lane < 32, *parts[:2]), jnp.where(lane < 96, *parts[2:]))

    def pack(f):
        low, high = [
            jnp.concatenate([part[i] for part in (west, near, east)], axis=0) for i in (f, f + half)
        ]
        rows[f] = low
        rows[f + half] = high
        to_north[f] = quarters(lane_roll(low, -32), lane_roll(low, -64), lane_roll(high, 32), high)
        to_south[f] = quarters(lane_roll(high, -64), lane_roll(high, 32), low, lane_roll(low, 96))

    each_layer(pack, 5, half)


def packed(parts, after=()):
    fields, rows = parts[0].shape[0], 3 * parts[0].shape[1]
    outs = [shape(fields, rows, BY)] + [shape(fields // 2, rows, BY)] * 2
    return call(pack_kernel, [*parts, *after], outs, [], 4 << 20, unread=range(3, 3 + len(after)))


def sideways(packs):
    rows, to_north, to_south = packs
    return rows, shifted(to_north, "gy", 1), shifted(to_south, "gy", -1)


def around(field):
    full = jnp.concatenate(sideways(packed((shifted(field, "gx", 1), field, shifted(field, "gx", -1)))), axis=0)
    return shifted(full, "gx", 3), full, shifted(full, "gx", -3)


def summed(field):
    count = lax.axis_size("gy")
    for flip in (1, 2, 6):
        if flip < count:
            field = field + lax.ppermute(field, "gy", [(i, i ^ flip) for i in range(count)])
    return field


def summed_over_all(row):
    axes = ("gx", "gy")
    count = lax.axis_size(axes)
    parts = lax.all_to_all(jnp.broadcast_to(row[None], (count, 1, 128)), axes, 0, 0, tiled=True)
    return jnp.sum(parts, axis=0)


def on_device(
    pressure, saturation_old, soil_type, recharge, ksat_table, alpha_table, porosity_table, residual_table
):
    tables = jnp.stack([ksat_table, alpha_table, porosity_table, residual_table])
    tables = jnp.pad(tables, ((0, 0), (0, 128 - tables.shape[1])))
    tables = jnp.broadcast_to(tables[:, None, :], (4, 8, 128))
    block = (NZ, BX, BY)
    start = call(
        start_kernel,
        [pressure, saturation_old, soil_type, recharge, tables],
        shape(3 * NZ, BX, BY),
        [buffer(*block), buffer(*block), pltpu.VMEM(block, jnp.int32), buffer(BX, BY), pltpu.SemaphoreType.DMA((4,))],
        4 << 20,
        range(4),
    )
    near = jnp.concatenate([shifted(start, "gx", 1), start, shifted(start, "gx", -1)], axis=1)
    parts = wider(near)
    soil_packs = packed([part[:NZ] for part in parts])
    soil_cells = sideways(soil_packs)
    packs = packed([part[NZ:] for part in parts], soil_packs[1:])
    cells = sideways(packs)
    given = soil_fields([tables, *soil_cells, packs[1]])
    moved = None
    for newton in range(2):
        if newton:
            parts = around(moved)
            got = setup([*parts, *fetched(stored, parts[1])], True)
        else:
            got = setup([*cells, *given], False)
            stored = got[20:]
        (c0, w0, s0, l0, g0, b0, x0, c1, w1, s1, l1, g1, b1, x1, m2, s2, l2, g2, b2, sums) = got[:20]
        weight = summed(sums)
        r0, y0, r1, y1, r2, sums, first = call(
            cycle_kernel,
            [weight, weight, *got[:19]],
            [shape(NZ, 8, SB, LANES)] * 2 + [shape(NZ, 2, SB, LANES)] * 2
            + [shape(NZ, SB, LANES), shape(SB, 128), shape(NZ, BX, BY)],
            work(),
            6 << 20,
        )
        total = summed(sums)
        products, second = call(
            last_kernel,
            [total, weight, c0, w0, s0, l0, g0, b0, c1, w1, s1, l1, g1, m2, s2, l2, g2, r0, y0, r1, y1, r2],
            [shape(1, 128), shape(NZ, BX, BY)],
            work(),
            6 << 20,
        )
        ends = [summed_over_all(products), first, second]
        if newton:
            return call(end_kernel, [pressure, moved, *ends], shape(NZ, BX, BY), [], 4 << 20)
        moved = call(move_kernel, ends, shape(NZ, BX, BY), [], 4 << 20)


def solution(mesh):
    placed = (P(None, "gx", "gy"),) * 3 + (P("gx", "gy"),) + (P(),) * 4
    return jax.shard_map(
        on_device, mesh=mesh, in_specs=placed, out_specs=P(None, "gx", "gy"), check_vma=False
    )
```
